32 devices in a mesh: section: 2 (over x), dp: 4 (over z), tensor: 4 (over y, core).
Axes of the slice: x: 2, y: 2, z: 4, core: 2. Of those that a mesh axis runs over, the one named last changes fastest.
Arguments:
- codes: bfloat16 [8, 256, 3, 1024], P('dp', 'tensor'), may hold values from -6 to 6
- cotangent: bfloat16 [8, 256, 3, 1024], P('dp', 'tensor'), may hold values from -6 to 6
- doc_lengths: int32 [8, 4], P('dp'), may hold values from 1 to 240, 256 in all within a row
- w_qkv: bfloat16 [2, 3, 1024, 1024], P('section', None, 'dp', 'tensor'), may hold values from -0.1875 to 0.1875
- w_out: bfloat16 [2, 1024, 1024], P('section', 'tensor', 'dp'), may hold values from -0.5 to 0.5
- w_up: bfloat16 [2, 1024, 4096], P('section', 'dp', 'tensor'), may hold values from -0.1875 to 0.1875
- w_down: bfloat16 [2, 4096, 1024], P('section', 'tensor', 'dp'), may hold values from -0.09375 to 0.09375
- gains: float32 [2, 2, 1024], P('section'), may hold values from 0.1 to 1.9
Outputs:
- results: bfloat16 [2, 8, 256, 3, 1024], P('section', 'dp', 'tensor')
- grad_qkv: float32 [2, 3, 1024, 1024], P('section', None, 'dp', 'tensor')
- grad_out: float32 [2, 1024, 1024], P('section', 'tensor', 'dp')
- grad_up: float32 [2, 1024, 4096], P('section', 'dp', 'tensor')
- grad_down: float32 [2, 4096, 1024], P('section', 'tensor', 'dp')
- grad_gains: float32 [2, 2, 1024], P('section')
The draws below stay inside these ranges and needn't reach their ends.
Inputs may be any that keep to these rules, and one draw needn't show every extreme that they name: `doc_lengths`: each packed row of 256 frames is cut into 4 documents whose lengths sum to 256; the longest of each row has exactly 240 frames.
All inputs are finite; a program needn't handle non-finite values.
Results may differ from the reference program's by a relative error of at most 0.017.
Values may be sent and summed in bfloat16 or wider, within the bound.
No kernel may reach another device: no remote copies, remote signals or barrier semaphores. Data moves between devices by JAX's collectives and lax.ppermute only.
A program may use at most 128 MiB of HBM per device.

```python
import math
import jax
import jax.numpy as jnp
import numpy as np
from jax import lax

D = 1024
HEAD_DIM = 64
FF = 4096
CODES = 3
FRAMES_MB = 256
DOCS = 4
LONGEST = 240
ROWS = 8


def steps_of(stream_key, extent, cuts, smallest, high):
    level = 1.0
    for dim, parts in cuts:
        steps = jax.random.uniform(jax.random.fold_in(jax.random.fold_in(stream_key, 6), dim), (parts,), jnp.float32, smallest / len(cuts), high / len(cuts))
        level = level * jnp.repeat(jnp.exp(steps), extent[dim] // parts).reshape((-1,) + (1,) * (len(extent) - 1 - dim))
    return level


def length_profile(number_of, total, reach, slope):
    weights = [(1 << 20) // math.isqrt(rank ** slope) + 1 for rank in range(2, number_of + 1)]
    rest, counts = total - reach - (number_of - 1), [1] * (number_of - 1)
    while rest > 0:
        free = [i for i in range(number_of - 1) if counts[i] < reach]
        pool, left = sum([weights[i] for i in free]), rest
        for i in free:
            more = min(reach - counts[i], max(1, left * weights[i] // pool), rest)
            counts[i] = counts[i] + more
            rest = rest - more
    return np.array([reach] + counts)


def uneven(rng, amount, total, reach, slope):
    if amount == 2:
        one = jax.random.randint(rng, (), max(1, total - reach), min(reach, total - 1) + 1)
        return jnp.stack([one, total - one])
    tallies = jnp.asarray(length_profile(amount, total, reach, slope), jnp.int32)
    couples = (amount - 1) // 2
    donor, taker = tallies[1:1 + 2 * couples:2], tallies[2:2 + 2 * couples:2]
    margin = jnp.minimum(donor - 1, reach - taker)
    shifted = jax.random.randint(jax.random.fold_in(rng, 1), (couples,), 0, 1 << 20) % (margin + 1)
    tallies = tallies.at[1:1 + 2 * couples:2].set(donor - shifted).at[2:2 + 2 * couples:2].set(taker + shifted)
    return tallies[jax.random.permutation(jax.random.fold_in(rng, 2), amount)]


def scatter_about(stream_key, dims, width, limit, pieces=(), dtype=jnp.bfloat16):
    values = width * jax.random.normal(stream_key, dims, jnp.float32)
    if pieces:
        values = values * steps_of(stream_key, dims, pieces, -0.22, 0.18)
    return jnp.clip(values, -limit, limit).astype(dtype)


def setup_inputs(seed: int = 0) -> dict:
    keys = jax.random.split(jax.random.key(seed), 9)
    return {
        "codes": scatter_about(keys[0], (ROWS, FRAMES_MB, CODES, D), 1.0, 6.0, ((0, 4), (1, 4))),
        "cotangent": scatter_about(keys[1], (ROWS, FRAMES_MB, CODES, D), 1.0, 6.0, ((0, 4), (1, 4))),
        "doc_lengths": jax.vmap(lambda own: uneven(own, DOCS, FRAMES_MB, LONGEST, 2))(jax.random.split(keys[2], ROWS)).reshape((ROWS, DOCS)).astype(jnp.int32),
        "w_qkv": scatter_about(keys[3], (2, 3, D, D), D ** -0.5, 0.1875, ((0, 2), (2, 4), (3, 4))),
        "w_out": scatter_about(keys[4], (2, D, D), (D // 8) ** -0.5, 0.5, ((0, 2), (1, 4), (2, 4))),
        "w_up": scatter_about(keys[5], (2, D, FF), D ** -0.5, 0.1875, ((0, 2), (1, 4), (2, 4))),
        "w_down": scatter_about(keys[6], (2, FF, D), FF ** -0.5, 0.09375, ((0, 2), (1, 4), (2, 4))),
        "gains": jnp.clip(1.0 + 0.18 * jax.random.normal(keys[7], (2, 2, D), jnp.float32), 0.1, 1.9),
    }


@jax.custom_vjp
def low(v):
    return lax.optimization_barrier(v.astype(jnp.bfloat16)).astype(jnp.float32)

@jax.custom_vjp
def low_back(v):
    return v

def low_keep(v):
    return (low(v), None)

def low_pass(kept, grad):
    return (grad,)

def back_keep(v):
    return (v, None)

def back_low(kept, grad):
    return (low(grad),)
low.defvjp(low_keep, low_pass)
low_back.defvjp(back_keep, back_low)
EPS = 1e-05
NEG = -1e+30
SCALE = 0.125
HIGH = lax.Precision.HIGHEST

def rms_gain(values, gain):
    return values * lax.rsqrt(lax.optimization_barrier(jnp.mean(values * values, axis=-1, keepdims=True)) + EPS) * gain

def layout_specs(layout):
    if layout == 'frames':
        return ('qhd,khd->hqk', 'hqk,khd->qhd')
    return ('fqhd,fkhd->fhqk', 'fhqk,fkhd->fqhd')

def attend(projected, layout, allowed):
    row_count = projected.shape[0]
    model_width = projected.shape[1] // 3
    head_count = model_width // HEAD_DIM
    lead = (row_count,) if layout == 'frames' else (row_count // 3, 3)
    split_heads = projected.reshape(lead + (3, head_count, HEAD_DIM))
    queries = split_heads[..., 0, :, :]
    key_rows = split_heads[..., 1, :, :]
    value_rows = split_heads[..., 2, :, :]
    specs = layout_specs(layout)
    scores = low_back(jnp.einsum(specs[0], queries, key_rows, precision=HIGH)) * SCALE
    scores = jnp.where(allowed, scores, NEG)
    attn_weights = low(jax.nn.softmax(scores, axis=-1))
    mixed = jnp.einsum(specs[1], attn_weights, value_rows, precision=HIGH)
    return mixed.reshape(row_count, model_width)

def block(stream, layer, params, layout, allowed):
    w_qkv, w_out, w_up, w_down, gains = params
    model_width = stream.shape[1]
    normed_in = low(rms_gain(stream, gains[layer, 0]))
    joined = w_qkv[layer].transpose(1, 0, 2).reshape(model_width, 3 * model_width)
    projected = low_back(low(jnp.dot(normed_in, joined, precision=HIGH)))
    mixed_heads = low_back(low(attend(projected, layout, allowed)))
    hidden = stream + low_back(jnp.dot(mixed_heads, w_out[layer], precision=HIGH))
    normed_mid = low(rms_gain(hidden, gains[layer, 1]))
    pre_act = low_back(jnp.dot(normed_mid, w_up[layer], precision=HIGH))
    activated = low(jax.nn.gelu(pre_act))
    return hidden + jnp.dot(activated, w_down[layer], precision=HIGH)

def row_pass(codes_row, segment, params):
    frame_count = codes_row.shape[0]
    position = lax.iota(jnp.int32, frame_count)
    allowed = ((position[:, None] >= position[None, :]) & (segment[:, None] == segment[None, :]))[None]
    token_pos = lax.iota(jnp.int32, codes_row.shape[1])
    token_mask = (token_pos[:, None] >= token_pos[None, :])[None, None]
    frame_in = lax.optimization_barrier(jnp.sum(codes_row, axis=1))
    frame_out = block(frame_in, 0, params, 'frames', allowed)
    sent = low_back(low(frame_out))
    local_in = low_back(codes_row + sent[:, None, :])
    local_out = block(local_in.reshape(-1, codes_row.shape[2]), 1, params, 'codes', token_mask)
    return local_out.reshape(codes_row.shape)

def reference(codes, cotangent, doc_lengths, w_qkv, w_out, w_up, w_down, gains):
    ends = jnp.cumsum(doc_lengths, axis=1).astype(jnp.int32)
    position = lax.iota(jnp.int32, codes.shape[1])
    segments = lax.optimization_barrier(jnp.sum((position[None, :, None] >= ends[:, None, :]).astype(jnp.int32), axis=2)).astype(jnp.int32)

    def forward(code_values, qkv_w, out_w, up_w, down_w, gain_w):
        params = (qkv_w, out_w, up_w, down_w, gain_w)
        return lax.map(lambda item: jax.checkpoint(row_pass)(item[0], item[1], params), (code_values, segments))
    local_out, pullback = jax.vjp(forward, codes.astype(jnp.float32), w_qkv.astype(jnp.float32), w_out.astype(jnp.float32), w_up.astype(jnp.float32), w_down.astype(jnp.float32), gains.astype(jnp.float32))
    grads = pullback(cotangent.astype(jnp.float32))
    results = jnp.stack([grads[0].astype(jnp.bfloat16), local_out.astype(jnp.bfloat16)])
    return (results, grads[1], grads[2], grads[3], grads[4], grads[5])
```

```python
import functools

import jax
import jax.numpy as jnp
from jax import lax
from jax.experimental import pallas as pl
from jax.experimental.pallas import tpu as pltpu
from jax.sharding import PartitionSpec as P

HEAD_DIM = 64
BLK = 256
HEADS = BLK // HEAD_DIM
EPS = 1e-05
NEG = -1e30
SCALE = 0.125
F32 = jnp.float32
BF16 = jnp.bfloat16
VMEM = 48 * 1024 * 1024


def mm(left, right):
    return jnp.dot(left, right, preferred_element_type=F32)


def mm_t(left, right):
    return lax.dot_general(left, right, (((1,), (1,)), ((), ())), preferred_element_type=F32)


def inner(left, right):
    return lax.dot_general(left, right, (((0,), (0,)), ((), ())), preferred_element_type=F32)


def unit_of(values):
    inv_root = lax.rsqrt(jnp.mean(values * values, axis=-1, keepdims=True) + EPS)
    return values * inv_root, inv_root


def normed(values, gain):
    return (unit_of(values)[0] * gain).astype(BF16)


def norm_back(values, gain, grad):
    unit_rows, inv_root = unit_of(values)
    scaled = grad * gain
    back = inv_root * (scaled - unit_rows * jnp.mean(unit_rows * scaled, axis=-1, keepdims=True))
    return back, jnp.sum(grad * unit_rows, axis=0, keepdims=True)


def gelu_pair(pre):
    square = pre * pre
    th = jnp.tanh(0.7978845608028654 * pre * (1.0 + 0.044715 * square))
    half = 0.5 + 0.5 * th
    act = pre * half
    slope = half + act * (1.0 - th) * (0.7978845608028654 + 3 * 0.044715 * 0.7978845608028654 * square)
    return act, slope


def cols(value, index):
    return value[:, index * BLK : (index + 1) * BLK]


def head_masks(shape):
    lane = lax.broadcasted_iota(jnp.int32, shape, 1) // HEAD_DIM
    return [lane == h for h in range(HEADS)]


def spread(value, masks):
    zero = jnp.zeros_like(value)
    return jnp.concatenate([jnp.where(m, value, zero) for m in masks], axis=0)


def gathered(value, masks):
    n = value.shape[0] // HEADS
    out = jnp.where(masks[0], value[:n], 0.0)
    for h in range(1, HEADS):
        out = jnp.where(masks[h], value[h * n : (h + 1) * n], out)
    return out


def head_weights(q4, k, bias):
    s = mm_t(q4, k) * SCALE + jnp.concatenate([bias] * HEADS, axis=0)
    e = jnp.exp(s - jnp.max(s, axis=-1, keepdims=True))
    return e / jnp.sum(e, axis=-1, keepdims=True)


def frames_in_body(order, s_ref, wq_ref, wo_ref, gain_ref, bias_ref, nin_ref, proj_ref, mixed_ref, hid_ref, nmid_ref, held):
    g = pl.program_id(0)
    R, N = bias_ref.shape[:2]

    @pl.when(g == 0)
    def _():
        s = s_ref[...]
        nin_ref[...] = normed(s, gain_ref[0:1])
        hid_ref[...] = s

    for which in range(3):
        acc = mm(nin_ref[:, :BLK], wq_ref[0, 0, which])
        for z in range(1, wq_ref.shape[0]):
            acc += mm(nin_ref[:, z * BLK : (z + 1) * BLK], wq_ref[z, 0, which])
        proj_ref[0, which] = acc.astype(BF16)
    masks = head_masks((N, BLK))
    for r in range(R):
        rows = pl.ds(r * N, N)
        p = head_weights(spread(proj_ref[0, 0, rows], masks), proj_ref[0, 1, rows], bias_ref[r])
        held[rows] = gathered(mm(p.astype(BF16), proj_ref[0, 2, rows]), masks).astype(BF16)
    for z in range(wo_ref.shape[0]):
        hid_ref[:, z * BLK : (z + 1) * BLK] += mm(held[...], wo_ref[z, 0, 0])

    @pl.when(g == 0)
    def _():
        mixed_ref[...] = held[...]

    @pl.when(g == pl.num_programs(0) - 1)
    def _():
        nmid_ref[...] = normed(hid_ref[...], gain_ref[1:2])


def whole(shape):
    return pl.BlockSpec(shape, lambda g, order: (0,) * len(shape))


def call(body, order, inputs, in_specs, outs, out_specs, grid, scratch=(), flops=0, moved=0):
    return pl.pallas_call(
        body,
        out_shape=outs,
        grid_spec=pltpu.PrefetchScalarGridSpec(
            num_scalar_prefetch=1,
            grid=(grid,),
            in_specs=in_specs,
            out_specs=out_specs,
            scratch_shapes=scratch,
        ),
        compiler_params=pltpu.CompilerParams(
            dimension_semantics=("arbitrary",), vmem_limit_bytes=VMEM
        ),
        cost_estimate=pl.CostEstimate(flops=flops, bytes_accessed=moved, transcendentals=0),
    )(order, *inputs)


def struct(shape, dtype):
    return jax.ShapeDtypeStruct(shape, dtype)


def qkv_spec(nz):
    return pl.BlockSpec((nz, 1, 3, BLK, BLK), lambda g, order: (0, order[g], 0, 0, 0))


def out_spec(nz):
    return pl.BlockSpec((nz, 1, 1, BLK, BLK), lambda g, order: (0, order[g], 3, 0, 0))


def mlp_spec(nz, first, per):
    return pl.BlockSpec(
        (nz, 1, 1, BLK, BLK), lambda g, order: (0, order[g // per], first + g % per, 0, 0)
    )


def frames_in(order, s, W, gain, bias):
    rows, D = s.shape
    nz, T = W.shape[:2]
    return call(
        frames_in_body,
        order,
        (s, W, W, gain, bias),
        [whole(s.shape), qkv_spec(nz), out_spec(nz), whole(gain.shape), whole(bias.shape)],
        (
            struct((rows, D), BF16),
            struct((T, 3, rows, BLK), BF16),
            struct((rows, BLK), BF16),
            struct((rows, D), F32),
            struct((rows, D), BF16),
        ),
        (
            whole((rows, D)),
            pl.BlockSpec((1, 3, rows, BLK), lambda g, order: (g, 0, 0, 0)),
            whole((rows, BLK)),
            whole((rows, D)),
            whole((rows, D)),
        ),
        T,
        (pltpu.VMEM((rows, BLK), BF16),),
        flops=2 * rows * D * 4 * D,
        moved=8 * D * D + rows * D * 16,
    )


def own_rows(ref, R, own):
    n = ref.shape[0] // R
    return jnp.concatenate([ref[r * n : r * n + own] for r in range(R)], axis=0)


def frames_mlp_body(R, own, order, nmid_ref, hid_ref, wu_ref, wd_ref, act_ref, slope_ref, out_ref, acc):
    g = pl.program_id(0)
    nz = wu_ref.shape[0]

    @pl.when(g == 0)
    def _():
        acc[...] = own_rows(hid_ref, R, own)

    pre = mm(nmid_ref[:, :BLK], wu_ref[0, 0, 0])
    for z in range(1, nz):
        pre += mm(nmid_ref[:, z * BLK : (z + 1) * BLK], wu_ref[z, 0, 0])
    act, slope = gelu_pair(pre)
    slope_ref[0] = slope.astype(BF16)
    act = act.astype(BF16)

    @pl.when(g < 4)
    def _():
        act_ref[0] = act

    n = act.shape[0] // R
    mine = jnp.concatenate([act[r * n : r * n + own] for r in range(R)], axis=0)
    for z in range(nz):
        acc[:, z * BLK : (z + 1) * BLK] += mm(mine, wd_ref[z, 0, 0])

    @pl.when(g == pl.num_programs(0) - 1)
    def _():
        out_ref[...] = acc[...].astype(BF16)


def frames_mlp(order, nmid, hid, W, R, own):
    rows, D = hid.shape
    nz, T = W.shape[:2]
    per = 4
    return call(
        functools.partial(frames_mlp_body, R, own),
        order,
        (nmid, hid, W, W),
        [whole(nmid.shape), whole(hid.shape), mlp_spec(nz, 4, per), mlp_spec(nz, 8, per)],
        (
            struct((per, rows, BLK), BF16),
            struct((T * per, rows, BLK), BF16),
            struct((R * own, D), BF16),
        ),
        (
            pl.BlockSpec((1, rows, BLK), lambda g, order: (jnp.minimum(g, per - 1), 0, 0)),
            pl.BlockSpec((1, rows, BLK), lambda g, order: (g, 0, 0)),
            whole((R * own, D)),
        ),
        T * per,
        (pltpu.VMEM((R * own, D), F32),),
        flops=2 * (rows + R * own) * D * 4 * D,
        moved=16 * D * D + rows * D * 14,
    )


def frames_mlp_back_body(R, own, order, gy_ref, hid_ref, slope_ref, wu_ref, wd_ref, gain_ref, gpre_ref, ghid_ref, branch_ref, gg_ref, acc):
    g = pl.program_id(0)
    nz = wu_ref.shape[0]
    gact = mm_t(gy_ref[:, :BLK], wd_ref[0, 0, 0])
    for z in range(1, nz):
        gact += mm_t(gy_ref[:, z * BLK : (z + 1) * BLK], wd_ref[z, 0, 0])
    gpre = (gact * slope_ref[0].astype(F32)).astype(BF16)

    @pl.when(g < 4)
    def _():
        gpre_ref[0] = gpre

    for z in range(nz):
        part = mm_t(gpre, wu_ref[z, 0, 0])
        at = slice(z * BLK, (z + 1) * BLK)

        @pl.when(g == 0)
        def _():
            acc[:, at] = part

        @pl.when(g > 0)
        def _():
            acc[:, at] += part

    @pl.when(g == pl.num_programs(0) - 1)
    def _():
        back, _ = norm_back(hid_ref[...], gain_ref[1:2], acc[...])
        ghid = gy_ref[...].astype(F32) + back
        branch_ref[...] = ghid.astype(BF16)
        acc_own = own_rows(acc, R, own)
        hid_own = own_rows(hid_ref, R, own)
        back_own, gg = norm_back(hid_own, gain_ref[1:2], acc_own)
        gg_ref[...] = gg
        ghid_ref[...] = own_rows(gy_ref, R, own).astype(F32) + back_own


def frames_mlp_back(order, gy, hid, slope, W, gain, R, own):
    rows, D = hid.shape
    nz, T = W.shape[:2]
    per = 4
    return call(
        functools.partial(frames_mlp_back_body, R, own),
        order,
        (gy, hid, slope, W, W, gain),
        [
            whole(gy.shape),
            whole(hid.shape),
            pl.BlockSpec((1, rows, BLK), lambda g, order: (g, 0, 0)),
            mlp_spec(nz, 4, per),
            mlp_spec(nz, 8, per),
            whole(gain.shape),
        ],
        (
            struct((per, rows, BLK), BF16),
            struct((R * own, D), F32),
            struct((rows, D), BF16),
            struct((1, D), F32),
        ),
        (
            pl.BlockSpec((1, rows, BLK), lambda g, order: (jnp.minimum(g, per - 1), 0, 0)),
            whole((R * own, D)),
            whole((rows, D)),
            whole((1, D)),
        ),
        T * per,
        (pltpu.VMEM((rows, D), F32),),
        flops=4 * rows * D * 4 * D,
        moved=16 * D * D + rows * D * 14,
    )


def frames_back_body(own, order, branch_ref, proj_ref, wq_ref, wo_ref, bias_ref, s_ref, ghid_ref, glocal_ref, gain_ref, gproj_ref, grad_ref, gg_ref, held, acc):
    g = pl.program_id(0)
    R, N = bias_ref.shape[:2]
    nz = wq_ref.shape[0]
    gmix = mm_t(branch_ref[:, :BLK], wo_ref[0, 0, 0])
    for z in range(1, nz):
        gmix += mm_t(branch_ref[:, z * BLK : (z + 1) * BLK], wo_ref[z, 0, 0])
    gmix = gmix.astype(BF16)
    masks = head_masks((N, BLK))
    for r in range(R):
        rows = pl.ds(r * N, N)
        q, k, v = (proj_ref[0, i, rows] for i in range(3))
        q4 = spread(q, masks)
        p = head_weights(q4, k, bias_ref[r])
        gm4 = spread(gmix[r * N : (r + 1) * N], masks)
        ga = mm_t(gm4, v)
        gs = (SCALE * p * (ga - jnp.sum(p * ga, axis=-1, keepdims=True))).astype(BF16)
        held[0, rows] = gathered(mm(gs, k), masks).astype(BF16)
        held[1, rows] = inner(gs, q4).astype(BF16)
        held[2, rows] = inner(p.astype(BF16), gm4).astype(BF16)

    @pl.when(g == 0)
    def _():
        gproj_ref[...] = held[...]
        acc[...] = jnp.zeros_like(acc)

    for which in range(3):
        mine = jnp.concatenate([held[which, r * N : r * N + own] for r in range(R)], axis=0)
        for z in range(nz):
            acc[:, z * BLK : (z + 1) * BLK] += mm_t(mine, wq_ref[z, 0, which])

    @pl.when(g == pl.num_programs(0) - 1)
    def _():
        back, gg = norm_back(own_rows(s_ref, R, own), gain_ref[0:1], acc[...])
        gg_ref[...] = gg
        frame = ghid_ref[...] + back
        for c in range(glocal_ref.shape[0]):
            grad_ref[c] = (glocal_ref[c].astype(F32) + frame).astype(BF16)


def frames_back(order, branch, proj, W, bias, s, ghid, glocal, gain, own):
    rows, D = branch.shape
    nz, T = W.shape[:2]
    R = bias.shape[0]
    return call(
        functools.partial(frames_back_body, own),
        order,
        (branch, proj, W, W, bias, s, ghid, glocal, gain),
        [
            whole(branch.shape),
            pl.BlockSpec((1, 3, rows, BLK), lambda g, order: (g, 0, 0, 0)),
            qkv_spec(nz),
            out_spec(nz),
            whole(bias.shape),
            whole(s.shape),
            whole(ghid.shape),
            whole(glocal.shape),
            whole(gain.shape),
        ],
        (struct((3, rows, BLK), BF16), struct(glocal.shape, BF16), struct((1, D), F32)),
        (whole((3, rows, BLK)), whole(glocal.shape), whole((1, D))),
        T,
        (pltpu.VMEM((3, rows, BLK), BF16), pltpu.VMEM((R * own, D), F32)),
        flops=2 * rows * D * 4 * D,
        moved=8 * D * D + rows * D * 16,
    )


def head_sum(prods):
    row = lax.broadcasted_iota(jnp.int32, (BLK, BLK), 0) // HEAD_DIM
    col = lax.broadcasted_iota(jnp.int32, (BLK, BLK), 1) // HEAD_DIM
    ones = jnp.where(row == col, 1.0, 0.0).astype(BF16)
    high = prods.astype(BF16)
    low = (prods - high.astype(F32)).astype(BF16)
    return mm(high, ones) + mm(low, ones)


def token_pairs(count):
    return [(a, b) for a in range(count) for b in range(a + 1)]


def token_weights(q, k, count):
    pairs = token_pairs(count)
    m = q[0].shape[0]
    s = head_sum(jnp.concatenate([q[a] * k[b] for a, b in pairs], axis=0)) * SCALE
    s = {pair: s[i * m : (i + 1) * m] for i, pair in enumerate(pairs)}
    out = {}
    for a in range(count):
        top = s[a, 0]
        for b in range(1, a + 1):
            top = jnp.maximum(top, s[a, b])
        e = [jnp.exp(s[a, b] - top) for b in range(a + 1)]
        total = e[0]
        for b in range(1, a + 1):
            total = total + e[b]
        for b in range(a + 1):
            out[a, b] = e[b] / total
    return out


def split_tokens(value, count):
    m = value.shape[0] // count
    return [value[i * m : (i + 1) * m].astype(F32) for i in range(count)]


def codes_in_body(order, codes_ref, sent_ref, wq_ref, wo_ref, gain_ref, nin_ref, proj_ref, keep_ref, send_ref, hid_ref, nmid_ref):
    g = pl.program_id(0)
    C, m, _ = codes_ref.shape
    nz = wq_ref.shape[0]

    @pl.when(g == 0)
    def _():
        for c in range(C):
            s = codes_ref[c].astype(F32) + sent_ref[...].astype(F32)
            rows = pl.ds(c * m, m)
            nin_ref[rows] = normed(s, gain_ref[0:1])
            hid_ref[rows] = s

    part = []
    for which in range(3):
        acc = mm(nin_ref[:, :BLK], wq_ref[0, 0, which])
        for z in range(1, nz):
            acc += mm(nin_ref[:, z * BLK : (z + 1) * BLK], wq_ref[z, 0, which])
        acc = acc.astype(BF16)
        proj_ref[0, which] = acc
        part.append(split_tokens(acc, C))
    q, k, v = part
    p = token_weights(q, k, C)
    mixed = []
    for a in range(C):
        total = p[a, 0].astype(BF16).astype(F32) * v[0]
        for b in range(1, a + 1):
            total += p[a, b].astype(BF16).astype(F32) * v[b]
        mixed.append(total)
    mixed = jnp.concatenate(mixed, axis=0).astype(BF16)

    @pl.when(g < 2)
    def _():
        keep_ref[0] = mixed

    @pl.when(g >= 2)
    def _():
        send_ref[0] = mixed

    for z in range(nz):
        hid_ref[:, z * BLK : (z + 1) * BLK] += mm(mixed, wo_ref[z, 0, 0])

    @pl.when(g == pl.num_programs(0) - 1)
    def _():
        nmid_ref[...] = normed(hid_ref[...], gain_ref[1:2])


def kept(shape, half):
    return pl.BlockSpec(
        (1,) + shape, lambda g, order: (jnp.minimum(g, half - 1),) + (0,) * len(shape)
    )


def given(shape, half):
    return pl.BlockSpec(
        (1,) + shape, lambda g, order: (jnp.maximum(g - half, 0),) + (0,) * len(shape)
    )


def codes_in(order, codes, sent, W, gain):
    C, m, D = codes.shape
    rows = C * m
    nz, T = W.shape[:2]
    return call(
        codes_in_body,
        order,
        (codes, sent, W, W, gain),
        [whole(codes.shape), whole(sent.shape), qkv_spec(nz), out_spec(nz), whole(gain.shape)],
        (
            struct((rows, D), BF16),
            struct((T, 3, rows, BLK), BF16),
            struct((T // 2, rows, BLK), BF16),
            struct((T // 2, rows, BLK), BF16),
            struct((rows, D), F32),
            struct((rows, D), BF16),
        ),
        (
            whole((rows, D)),
            pl.BlockSpec((1, 3, rows, BLK), lambda g, order: (g, 0, 0, 0)),
            kept((rows, BLK), 2),
            given((rows, BLK), 2),
            whole((rows, D)),
            whole((rows, D)),
        ),
        T,
        flops=2 * rows * D * 4 * D,
        moved=8 * D * D + rows * D * 16,
    )


def codes_gact_body(order, cot_ref, wd_ref, gact_ref):
    gact = mm_t(cot_ref[:, :BLK], wd_ref[0, 0, 0])
    for z in range(1, wd_ref.shape[0]):
        gact += mm_t(cot_ref[:, z * BLK : (z + 1) * BLK], wd_ref[z, 0, 0])
    gact_ref[0] = gact.astype(BF16)


def codes_gact(order, cot, W):
    rows, D = cot.shape
    nz, T = W.shape[:2]
    per = 4
    return call(
        codes_gact_body,
        order,
        (cot, W),
        [whole(cot.shape), mlp_spec(nz, 8, per)],
        struct((T * per, rows, BLK), BF16),
        pl.BlockSpec((1, rows, BLK), lambda g, order: (g, 0, 0)),
        T * per,
        flops=2 * rows * D * 4 * D,
        moved=8 * D * D + rows * D * 10,
    )


def codes_mlp_body(order, nmid_ref, hid_ref, cot_ref, gact_ref, wu_ref, gain_ref, akeep_ref, asend_ref, gkeep_ref, gsend_ref, ghid_ref, branch_ref, gg_ref, acc):
    g = pl.program_id(0)
    half = pl.num_programs(0) // 2
    nz = wu_ref.shape[0]
    pre = mm(nmid_ref[:, :BLK], wu_ref[0, 0, 0])
    for z in range(1, nz):
        pre += mm(nmid_ref[:, z * BLK : (z + 1) * BLK], wu_ref[z, 0, 0])
    act, slope = gelu_pair(pre)
    act = act.astype(BF16)
    gpre = (gact_ref[0].astype(F32) * slope).astype(BF16)

    @pl.when(g < half)
    def _():
        akeep_ref[0] = act
        gkeep_ref[0] = gpre

    @pl.when(g >= half)
    def _():
        asend_ref[0] = act
        gsend_ref[0] = gpre

    for z in range(nz):
        part = mm_t(gpre, wu_ref[z, 0, 0])
        at = slice(z * BLK, (z + 1) * BLK)

        @pl.when(g == 0)
        def _():
            acc[:, at] = part

        @pl.when(g > 0)
        def _():
            acc[:, at] += part

    @pl.when(g == pl.num_programs(0) - 1)
    def _():
        back, gg = norm_back(hid_ref[...], gain_ref[1:2], acc[...])
        gg_ref[...] = gg
        ghid = cot_ref[...].astype(F32) + back
        ghid_ref[...] = ghid
        branch_ref[...] = ghid.astype(BF16)


def codes_mlp(order, nmid, hid, cot, gact, W, gain):
    rows, D = hid.shape
    nz, T = W.shape[:2]
    per = 4
    half = T * per // 2
    blocks = struct((half, rows, BLK), BF16)
    return call(
        codes_mlp_body,
        order,
        (nmid, hid, cot, gact, W, gain),
        [
            whole(nmid.shape),
            whole(hid.shape),
            whole(cot.shape),
            pl.BlockSpec((1, rows, BLK), lambda g, order: (g, 0, 0)),
            mlp_spec(nz, 4, per),
            whole(gain.shape),
        ],
        (
            blocks,
            blocks,
            blocks,
            blocks,
            struct((rows, D), F32),
            struct((rows, D), BF16),
            struct((1, D), F32),
        ),
        (
            kept((rows, BLK), half),
            given((rows, BLK), half),
            kept((rows, BLK), half),
            given((rows, BLK), half),
            whole((rows, D)),
            whole((rows, D)),
            whole((1, D)),
        ),
        T * per,
        (pltpu.VMEM((rows, D), F32),),
        flops=4 * rows * D * 4 * D,
        moved=8 * D * D + rows * D * 30,
    )


def codes_back_body(order, branch_ref, proj_ref, wq_ref, wo_ref, codes_ref, sent_ref, ghid_ref, gain_ref, keep_ref, send_ref, glocal_ref, gsent_ref, gg_ref, acc):
    g = pl.program_id(0)
    C, m, _ = codes_ref.shape
    nz = wq_ref.shape[0]
    gmix = mm_t(branch_ref[:, :BLK], wo_ref[0, 0, 0])
    for z in range(1, nz):
        gmix += mm_t(branch_ref[:, z * BLK : (z + 1) * BLK], wo_ref[z, 0, 0])
    gm = split_tokens(gmix.astype(BF16), C)
    q, k, v = (split_tokens(proj_ref[0, i], C) for i in range(3))
    p = token_weights(q, k, C)
    pairs = token_pairs(C)
    ga = head_sum(jnp.concatenate([gm[a] * v[b] for a, b in pairs], axis=0))
    ga = {pair: ga[i * m : (i + 1) * m] for i, pair in enumerate(pairs)}
    gq, gk, gv = [], [None] * C, [None] * C

    def add(left, right):
        return right if left is None else left + right

    for a in range(C):
        centre = p[a, 0] * ga[a, 0]
        for b in range(1, a + 1):
            centre += p[a, b] * ga[a, b]
        total = None
        for b in range(a + 1):
            gs = (SCALE * p[a, b] * (ga[a, b] - centre)).astype(BF16).astype(F32)
            total = add(total, gs * k[b])
            gk[b] = add(gk[b], gs * q[a])
            gv[b] = add(gv[b], p[a, b].astype(BF16).astype(F32) * gm[a])
        gq.append(total)
    joined = [jnp.concatenate(part, axis=0).astype(BF16) for part in (gq, gk, gv)]

    @pl.when(g < 2)
    def _():
        for which in range(3):
            keep_ref[0, which] = joined[which]

    @pl.when(g >= 2)
    def _():
        for which in range(3):
            send_ref[0, which] = joined[which]

    for z in range(nz):
        part = mm_t(joined[0], wq_ref[z, 0, 0])
        for which in range(1, 3):
            part += mm_t(joined[which], wq_ref[z, 0, which])
        at = slice(z * BLK, (z + 1) * BLK)

        @pl.when(g == 0)
        def _():
            acc[:, at] = part

        @pl.when(g > 0)
        def _():
            acc[:, at] += part

    @pl.when(g == pl.num_programs(0) - 1)
    def _():
        total = None
        gains = None
        for c in range(C):
            rows = slice(c * m, (c + 1) * m)
            s = codes_ref[c].astype(F32) + sent_ref[...].astype(F32)
            back, gg = norm_back(s, gain_ref[0:1], acc[rows])
            gains = add(gains, gg)
            local = (ghid_ref[rows] + back).astype(BF16)
            glocal_ref[c] = local
            total = add(total, local.astype(F32))
        gsent_ref[...] = total.astype(BF16)
        gg_ref[...] = gains


def codes_back(order, branch, proj, W, codes, sent, ghid, gain):
    rows, D = branch.shape
    C, m, _ = codes.shape
    nz, T = W.shape[:2]
    blocks = struct((T // 2, 3, rows, BLK), BF16)
    return call(
        codes_back_body,
        order,
        (branch, proj, W, W, codes, sent, ghid, gain),
        [
            whole(branch.shape),
            pl.BlockSpec((1, 3, rows, BLK), lambda g, order: (g, 0, 0, 0)),
            qkv_spec(nz),
            out_spec(nz),
            whole(codes.shape),
            whole(sent.shape),
            whole(ghid.shape),
            whole(gain.shape),
        ],
        (blocks, blocks, struct(codes.shape, BF16), struct((m, D), BF16), struct((1, D), F32)),
        (
            kept((3, rows, BLK), 2),
            given((3, rows, BLK), 2),
            whole(codes.shape),
            whole((m, D)),
            whole((1, D)),
        ),
        T,
        (pltpu.VMEM((rows, D), F32),),
        flops=2 * rows * D * 4 * D,
        moved=8 * D * D + rows * D * 20,
    )


def codes_out_body(order, hid_ref, keep_ref, send_ref, wd_ref, out_ref, acc):
    g = pl.program_id(0)
    half = pl.num_programs(0) // 2
    C, m, _ = out_ref.shape

    @pl.when(g == 0)
    def _():
        acc[...] = hid_ref[...]

    act = jnp.where(g < half, keep_ref[0], send_ref[0])
    for z in range(wd_ref.shape[0]):
        acc[:, z * BLK : (z + 1) * BLK] += mm(act, wd_ref[z, 0, 0])

    @pl.when(g == pl.num_programs(0) - 1)
    def _():
        for c in range(C):
            out_ref[c] = acc[c * m : (c + 1) * m].astype(BF16)


def codes_out(order, hid, keep, send, W, C):
    rows, D = hid.shape
    nz, T = W.shape[:2]
    per = 4
    half = T * per // 2
    m = rows // C
    return call(
        codes_out_body,
        order,
        (hid, keep, send, W),
        [whole(hid.shape), kept((rows, BLK), half), given((rows, BLK), half), mlp_spec(nz, 8, per)],
        struct((C, m, D), BF16),
        whole((C, m, D)),
        T * per,
        (pltpu.VMEM((rows, D), F32),),
        flops=2 * rows * D * 4 * D,
        moved=8 * D * D + rows * D * 14,
    )


def pair_rows(wide, narrow):
    return inner(wide, narrow)


def put(ref, value, by_rows):
    for z in range(ref.shape[0]):
        at = slice(z * BLK, (z + 1) * BLK)
        ref[z, 0] = (value[at] if by_rows else value[:, at]).astype(BF16)


def got(ref, by_rows):
    parts = [ref[z, 0].astype(F32) for z in range(ref.shape[0])]
    return jnp.concatenate(parts, axis=0 if by_rows else 1)


def far_body(split, flag, wide_a, wide_b, row_a, col_a, swide_a, swide_b, row_b, col_b, out_ref):
    g = pl.program_id(0)

    @pl.when((flag[0] == 0) & (g < split))
    def _():
        put(out_ref, inner(wide_a[...], row_a[0]) + inner(swide_a[...], row_b[0]), True)

    @pl.when((flag[0] == 0) & (g >= split))
    def _():
        put(out_ref, inner(col_a[0], wide_b[...]) + inner(col_b[0], swide_b[...]), False)


def last_body(split, flag, w0a, w0b, row_0, col_0, wide_a, wide_b, row_a, col_a, swide_a, swide_b, row_b, col_b, got_ref, out_ref):
    g = pl.program_id(0)

    @pl.when((flag[0] == 1) & (g < split))
    def _():
        put(out_ref, inner(w0a[...], row_0[0]), True)

    @pl.when((flag[0] == 1) & (g >= split))
    def _():
        put(out_ref, inner(col_0[0], w0b[...]), False)

    @pl.when((flag[0] == 0) & (g < split))
    def _():
        total = inner(wide_a[...], row_a[0]) + inner(swide_a[...], row_b[0])
        put(out_ref, total + got(got_ref, True), True)

    @pl.when((flag[0] == 0) & (g >= split))
    def _():
        total = inner(col_a[0], wide_b[...]) + inner(col_b[0], swide_b[...])
        put(out_ref, total + got(got_ref, False), False)


def part_specs(split, count, base, rows):
    row = pl.BlockSpec((1, rows, BLK), lambda g, f: (base * split + jnp.minimum(g, split - 1), 0, 0))
    ncol = count - split
    col = pl.BlockSpec((1, rows, BLK), lambda g, f: (base * ncol + jnp.maximum(g - split, 0), 0, 0))
    return [row, col]


def grads_far(flag, own, sib, split, count, nz):
    rows, D = own[0].shape
    specs = [whole(own[0].shape), whole(own[1].shape)] + part_specs(split, count, 1, rows)
    return call(
        functools.partial(far_body, split),
        flag,
        own + sib,
        specs + specs,
        struct((nz, count, BLK, BLK), BF16),
        pl.BlockSpec((nz, 1, BLK, BLK), lambda g, f: (0, g, 0, 0)),
        count,
        flops=4 * rows * D * BLK * count,
        moved=rows * D * 16,
    )


def grads_last(flag, first, own, sib, received, split, count, nz):
    rows0 = first[0].shape[0]
    rows, D = own[0].shape
    first_specs = [whole(first[0].shape), whole(first[1].shape)] + part_specs(split, count, 0, rows0)
    specs = [whole(own[0].shape), whole(own[1].shape)] + part_specs(split, count, 0, rows)
    block = pl.BlockSpec((nz, 1, BLK, BLK), lambda g, f: (0, g, 0, 0))
    return call(
        functools.partial(last_body, split),
        flag,
        first + own + sib + (received,),
        first_specs + specs + specs + [block],
        struct((nz, count, BLK, BLK), BF16),
        block,
        count,
        flops=4 * rows * D * BLK * count,
        moved=rows * D * 24,
    )


def swap(value, axis, bit):
    count = lax.axis_size(axis)
    return lax.ppermute(value, axis, [(i, i ^ bit) for i in range(count)])


def swap_in(value, section, bit):
    count = lax.axis_size("tensor")
    pairs = [(section * count + i, section * count + (i ^ bit)) for i in range(count)]
    return lax.ppermute(value, ("section", "tensor"), pairs)


def gather_weights(w_qkv, w_out, w_up, w_down):
    depth = w_qkv.shape[1]
    shards = lax.axis_size("dp")
    slices = lax.axis_size("tensor")
    both = ("dp", "tensor")
    if depth == BLK:
        up_blocks = w_up.reshape(BLK, -1, BLK).transpose(1, 0, 2)
        flat = jnp.concatenate(
            [w_qkv, w_out[None], up_blocks, w_down.reshape(-1, BLK, BLK)], axis=0
        )
        out = lax.all_gather(flat, both)
        return out.reshape(shards, slices, *flat.shape)
    per = BLK // depth
    nz = shards // per

    def by_rows(value):
        out = lax.all_gather(value, both).reshape(nz, per, slices, value.shape[0], depth, BLK)
        return out.transpose(0, 2, 3, 1, 4, 5).reshape(nz, slices, -1, BLK, BLK)

    def by_cols(value):
        out = lax.all_gather(value, both)
        out = out.reshape(nz, per, slices, value.shape[0] // BLK, BLK, depth)
        return out.transpose(0, 2, 3, 4, 1, 5).reshape(nz, slices, -1, BLK, BLK)

    up_blocks = w_up.reshape(depth, -1, BLK).transpose(1, 0, 2)
    return jnp.concatenate(
        [by_rows(w_qkv), by_cols(w_out), by_rows(up_blocks), by_cols(w_down)], axis=2
    )


def scatter_blocks(parts, split):
    shards = lax.axis_size("dp")
    nz, count = parts.shape[:2]
    per = shards // nz
    if per == 1:
        out = lax.psum_scatter(parts, "dp", scatter_dimension=0, tiled=False)
        return out[:split], out[split:]
    depth = BLK // per
    rows = parts[:, :split].reshape(nz, split, per, depth, BLK)
    rows = rows.transpose(0, 2, 1, 3, 4).reshape(shards, -1, BLK)
    columns = parts[:, split:].reshape(nz, count - split, BLK, per, depth)
    columns = columns.transpose(0, 3, 1, 2, 4).reshape(shards, -1, BLK)
    out = lax.psum_scatter(
        jnp.concatenate([rows, columns], axis=1), "dp", scatter_dimension=0, tiled=False
    )
    cut = split * depth
    return out[:cut].reshape(split, depth, BLK), out[cut:].reshape(-1, BLK, depth)


def on_device(codes, cotangent, doc_lengths, w_qkv, w_out, w_up, w_down, gains):
    is_first = lax.axis_index("section") == 0
    flag = is_first.astype(jnp.int32).reshape(1)
    t = lax.axis_index("tensor")
    T = lax.axis_size("tensor")
    R, F, C, D = codes.shape
    M = R * F
    N = T * F
    gain = gains[0]
    W = gather_weights(w_qkv[0], w_out[0], w_up[0], w_down[0])
    nz = W.shape[0]
    order = t ^ jnp.array([0, 2, 1, 3], jnp.int32)
    codes_t = codes.transpose(2, 0, 1, 3).reshape(C, M, D)
    cot = cotangent.transpose(2, 0, 1, 3).reshape(C * M, D)

    frame_own = jnp.sum(codes_t.astype(F32), axis=0).reshape(R, F, D)
    far = swap(frame_own, "tensor", 2)
    near = swap(jnp.stack([frame_own, far]), "tensor", 1)
    s0 = jnp.stack([frame_own, near[0], far, near[1]], axis=1).reshape(R * N, D)
    place = t ^ lax.iota(jnp.int32, T)
    pos = (place[:, None] * F + lax.iota(jnp.int32, F)[None]).reshape(N)
    ends = jnp.cumsum(doc_lengths, axis=1)
    seg = jnp.sum((pos[None, :, None] >= ends[:, None, :]).astype(jnp.int32), axis=2)
    allowed = (pos[:, None] >= pos[None, :])[None] & (seg[:, :, None] == seg[:, None, :])
    bias = jnp.where(allowed, 0.0, NEG).astype(F32)

    n_in0, proj0, mixed0, hid0, n_mid0 = frames_in(order, s0, W, gain, bias)
    act0, slope0, out0 = frames_mlp(order, n_mid0, hid0, W, R, F)
    sent = lax.ppermute(out0, "section", [(0, 1)])

    gact1 = codes_gact(order, cot, W)
    n_in1, proj1, mixed1, mixed1_s, hid1, n_mid1 = codes_in(order, codes_t, sent, W, gain)
    act1, act1_s, gpre1, gpre1_s, ghid1, branch1, gg_mid1 = codes_mlp(
        order, n_mid1, hid1, cot, gact1, W, gain
    )
    gproj1, gproj1_s, glocal, gsent, gg_in1 = codes_back(
        order, branch1, proj1, W, codes_t, sent, ghid1, gain
    )

    gsent = lax.ppermute(gsent, "section", [(1, 0)])
    glocal = lax.ppermute(glocal, "section", [(1, 0)])
    gfar = swap_in(gsent, 0, 2)
    gnear = swap_in(jnp.stack([gsent, gfar]), 0, 1)
    gy0 = (
        jnp.stack([gsent, gnear[0], gfar, gnear[1]], axis=0)
        .reshape(T, R, F, D)
        .transpose(1, 0, 2, 3)
        .reshape(R * N, D)
    )

    def exchange(value):
        return swap_in(value, 1, 1)

    out1 = codes_out(order, hid1, act1, act1_s, W, C)
    per = act1.shape[0] // 2
    mlp_own = (n_mid1, cot, gpre1, act1)
    mlp_sib = (exchange(n_mid1), exchange(cot), exchange(gpre1_s), exchange(act1_s))
    mlp_got = swap_in(grads_far(flag, mlp_own, mlp_sib, per, 2 * per, nz), 1, 2)
    att_own = (n_in1, branch1, gproj1.reshape(-1, C * M, BLK), mixed1)
    att_sib = (
        exchange(n_in1),
        exchange(branch1),
        exchange(gproj1_s).reshape(-1, C * M, BLK),
        exchange(mixed1_s),
    )
    att_got = swap_in(grads_far(flag, att_own, att_sib, 3, 4, nz), 1, 2)

    gpre0, ghid0, branch0, gg_mid0 = frames_mlp_back(order, gy0, hid0, slope0, W, gain, R, F)
    mlp_total = grads_last(
        flag, (n_mid0, gy0, gpre0, act0), mlp_own, mlp_sib, mlp_got, per, 2 * per, nz
    )
    up_part, down_part = scatter_blocks(mlp_total, per)
    gproj0, code_grad, gg_in0 = frames_back(
        order, branch0, proj0, W, bias, s0, ghid0, glocal, gain, F
    )
    att_total = grads_last(
        flag, (n_in0, branch0, gproj0, mixed0[None]), att_own, att_sib, att_got, 3, 4, nz
    )
    qkv_part, out_part = scatter_blocks(att_total, 3)

    gain_part = jnp.where(
        is_first,
        jnp.concatenate([gg_in0, gg_mid0], axis=0),
        jnp.concatenate([gg_in1, gg_mid1], axis=0),
    )
    grad_gains = lax.psum(gain_part, ("dp", "tensor"))
    result = jnp.where(is_first, code_grad, out1).reshape(C, R, F, D).transpose(1, 2, 0, 3)
    depth = w_up.shape[1]
    return (
        result[None],
        qkv_part.astype(F32)[None],
        out_part.reshape(-1, depth).astype(F32)[None],
        up_part.transpose(1, 0, 2).reshape(depth, -1).astype(F32)[None],
        down_part.reshape(-1, depth).astype(F32)[None],
        grad_gains[None],
    )


def solution(mesh):
    placed = (
        P("dp", "tensor", None, None),
        P("dp", "tensor", None, None),
        P("dp", None),
        P("section", None, "dp", "tensor"),
        P("section", "tensor", "dp"),
        P("section", "dp", "tensor"),
        P("section", "tensor", "dp"),
        P("section", None, None),
    )
    return jax.shard_map(
        on_device,
        mesh=mesh,
        in_specs=placed,
        out_specs=(
            P("section", "dp", "tensor", None, None),
            P("section", None, "dp", "tensor"),
            P("section", "tensor", "dp"),
            P("section", "dp", "tensor"),
            P("section", "tensor", "dp"),
            P("section", None, None),
        ),
        check_vma=False,
    )
```

```python
import functools

import jax
import jax.numpy as jnp
from jax import lax
from jax.experimental import pallas as pl
from jax.experimental.pallas import tpu as pltpu
from jax.sharding import PartitionSpec as P

HEAD_DIM = 64
BLK = 256
HEADS = BLK // HEAD_DIM
EPS = 1e-05
NEG = -1e30
SCALE = 0.125
F32 = jnp.float32
BF16 = jnp.bfloat16
VMEM = 60 * 1024 * 1024
ACTIVE = 4
COST = 8


def mm(left, right):
    return jnp.dot(left, right, preferred_element_type=F32)


def mm_t(left, right):
    return lax.dot_general(left, right, (((1,), (1,)), ((), ())), preferred_element_type=F32)


def inner(left, right):
    return lax.dot_general(left, right, (((0,), (0,)), ((), ())), preferred_element_type=F32)


def unit_of(values):
    inv_root = lax.rsqrt(jnp.mean(values * values, axis=-1, keepdims=True) + EPS)
    return values * inv_root, inv_root


def normed(values, gain):
    return (unit_of(values)[0] * gain).astype(BF16)


def norm_back(values, gain, grad):
    unit_rows, inv_root = unit_of(values)
    scaled = grad * gain
    back = inv_root * (scaled - unit_rows * jnp.mean(unit_rows * scaled, axis=-1, keepdims=True))
    return back, jnp.sum(grad * unit_rows, axis=0, keepdims=True)


def gelu_pair(pre):
    square = pre * pre
    th = jnp.tanh(0.7978845608028654 * pre * (1.0 + 0.044715 * square))
    half = 0.5 + 0.5 * th
    act = pre * half
    slope = half + act * (1.0 - th) * (0.7978845608028654 + 3 * 0.044715 * 0.7978845608028654 * square)
    return act, slope


def head_masks(shape):
    lane = lax.broadcasted_iota(jnp.int32, shape, 1) // HEAD_DIM
    return [lane == h for h in range(HEADS)]


def spread(value, masks):
    zero = jnp.zeros_like(value)
    return jnp.concatenate([jnp.where(m, value, zero) for m in masks], axis=0)


def gathered(value, masks):
    n = value.shape[0] // HEADS
    out = jnp.where(masks[0], value[:n], 0.0)
    for h in range(1, HEADS):
        out = jnp.where(masks[h], value[h * n : (h + 1) * n], out)
    return out


def head_weights(q4, k, bias):
    s = mm_t(q4, k) * SCALE + jnp.concatenate([bias] * HEADS, axis=0)
    e = jnp.exp(s - jnp.max(s, axis=-1, keepdims=True))
    return e / jnp.sum(e, axis=-1, keepdims=True)


def whole(shape):
    return pl.BlockSpec(shape, lambda g, order: (0,) * len(shape))


def struct(shape, dtype):
    return jax.ShapeDtypeStruct(shape, dtype)


def call(body, order, inputs, in_specs, outs, out_specs, grid, scratch=(), flops=0, moved=0):
    def run(flags, *refs):
        if flags.shape[0] <= ACTIVE:
            return body(flags, *refs)

        @pl.when(flags[ACTIVE] == 1)
        def _():
            body(flags, *refs)

    return pl.pallas_call(
        run,
        out_shape=outs,
        grid_spec=pltpu.PrefetchScalarGridSpec(
            num_scalar_prefetch=1,
            grid=(grid,),
            in_specs=in_specs,
            out_specs=out_specs,
            scratch_shapes=scratch,
        ),
        compiler_params=pltpu.CompilerParams(
            dimension_semantics=("arbitrary",), vmem_limit_bytes=VMEM
        ),
        cost_estimate=pl.CostEstimate(
            flops=flops // COST, bytes_accessed=moved // COST, transcendentals=0
        ),
    )(order, *inputs)


def weight_spec(W, third):
    nz = W.shape[0]

    def at(g, order):
        step, which = third(g)
        return (0, order[step] * order[ACTIVE], which * order[ACTIVE], 0, 0)

    return pl.BlockSpec((nz, 1, 4, BLK, BLK), at)


def clip(g, low, high):
    return jnp.minimum(jnp.maximum(g, low), high)


def deep(ref, index):
    return ref[:, 0, index].reshape(-1, BLK)


def store_out(g, first, held, sems, outs):
    for i, out in enumerate(outs):

        @pl.when(g == first + i)
        def _():
            pltpu.make_async_copy(held.at[i], out, sems.at[i]).start()


def stored(held, sems, outs):
    for i, out in enumerate(outs):
        pltpu.make_async_copy(held.at[i], out, sems.at[i]).wait()


HBM_REF = pl.BlockSpec(memory_space=pl.ANY)


def pick(ref, r, R, F):
    return jnp.concatenate(
        [ref[pl.ds(at, F)] for at in range(r * F, ref.shape[0], R * F)], axis=0
    )


def place(ref, r, R, F, value):
    for i, at in enumerate(range(r * F, ref.shape[0], R * F)):
        ref[pl.ds(at, F)] = value[i * F : (i + 1) * F]


def frames_fwd_body(own, order, s_ref, wa_ref, wb_ref, gain_ref, bias_ref, nin_ref, proj_ref, mixed_ref, hid_ref, nmid_ref, act_ref, slope_ref, out_ref, held, acc, acts, sems):
    g = pl.program_id(0)
    T = pl.num_programs(0) // 2
    R, N = bias_ref.shape[:2]
    nz = wa_ref.shape[0]

    @pl.when(g == 0)
    def _():
        s = s_ref[...]
        nin_ref[...] = normed(s, gain_ref[0:1])
        hid_ref[...] = s

    @pl.when(g < T)
    def _():
        for which in range(3):
            proj_ref[0, which] = mm(nin_ref[...], deep(wa_ref, which)).astype(BF16)
        masks = head_masks((N, BLK))
        for r in range(R):
            q, k, v = (pick(proj_ref.at[0, i], r, R, own) for i in range(3))
            p = head_weights(spread(q, masks), k, bias_ref[r])
            place(held, r, R, own, gathered(mm(p.astype(BF16), v), masks).astype(BF16))
        for z in range(nz):
            hid_ref[:, z * BLK : (z + 1) * BLK] += mm(held[...], wa_ref[z, 0, 3])

    @pl.when(g == 0)
    def _():
        mixed_ref[...] = held[...]

    @pl.when(g == T)
    def _():
        nmid_ref[...] = normed(hid_ref[...], gain_ref[1:2])
        acc[...] = hid_ref[: R * own]

    @pl.when(g >= T)
    def _():
        mine = []
        for j in range(4):
            act, slope = gelu_pair(mm(nmid_ref[...], deep(wa_ref, j)))
            slope_ref[0, j] = slope.astype(BF16)
            act = act.astype(BF16)
            acts[jnp.minimum(g - T, 1), j] = act
            mine.append(act[: R * own])
        mine = jnp.concatenate(mine, axis=1)
        for z in range(nz):
            acc[:, z * BLK : (z + 1) * BLK] += mm(mine, wb_ref[z, 0].reshape(-1, BLK))

    store_out(g, T, acts, sems, [act_ref])

    @pl.when(g == 2 * T - 1)
    def _():
        out_ref[...] = acc[...].astype(BF16)
        stored(acts, sems, [act_ref])


def frames_fwd(order, s, W, gain, bias, own):
    rows, D = s.shape
    T = W.shape[1]
    R = bias.shape[0]
    return call(
        functools.partial(frames_fwd_body, own),
        order,
        (s, W, W, gain, bias),
        [
            whole(s.shape),
            weight_spec(W, lambda g: (g % T, g // T)),
            weight_spec(W, lambda g: (jnp.maximum(g - T, 0), 2)),
            whole(gain.shape),
            whole(bias.shape),
        ],
        (
            struct((rows, D), BF16),
            struct((T, 3, rows, BLK), BF16),
            struct((rows, BLK), BF16),
            struct((rows, D), F32),
            struct((rows, D), BF16),
            struct((4, rows, BLK), BF16),
            struct((T, 4, rows, BLK), BF16),
            struct((R * own, D), BF16),
        ),
        (
            whole((rows, D)),
            pl.BlockSpec((1, 3, rows, BLK), lambda g, order: (jnp.minimum(g, T - 1) * order[ACTIVE], 0, 0, 0)),
            whole((rows, BLK)),
            whole((rows, D)),
            whole((rows, D)),
            HBM_REF,
            pl.BlockSpec((1, 4, rows, BLK), lambda g, order: (jnp.maximum(g - T, 0) * order[ACTIVE], 0, 0, 0)),
            whole((R * own, D)),
        ),
        2 * T,
        (
            pltpu.VMEM((rows, BLK), BF16),
            pltpu.VMEM((R * own, D), F32),
            pltpu.VMEM((2, 4, rows, BLK), BF16),
            pltpu.SemaphoreType.DMA((1,)),
        ),
        flops=2 * rows * D * 10 * D,
        moved=24 * D * D + rows * D * 30,
    )


def frames_bwd_body(own, order, gy_ref, hid_ref, slope_ref, wa_ref, wb_ref, gain_ref, proj_ref, bias_ref, s_ref, gpre_ref, branch_ref, gproj_ref, frame_ref, gg_ref, held, acc, acc_in, ghid, pres, gmix, sems):
    g = pl.program_id(0)
    T = pl.num_programs(0) // 2
    R, N = bias_ref.shape[:2]
    nz = wa_ref.shape[0]

    @pl.when(g < T)
    def _():
        part = None
        for j in range(4):
            lanes = jnp.concatenate([wb_ref[z, 0, j] for z in range(nz)], axis=1)
            gpre = (mm_t(gy_ref[...], lanes) * slope_ref[0, j].astype(F32)).astype(BF16)

            pres[jnp.minimum(g, 1), j] = gpre
            piece = mm_t(gpre, deep(wa_ref, j))
            part = piece if part is None else part + piece
        acc[...] = part + jnp.where(g == 0, 0.0, acc[...])

    store_out(g, 0, pres, sems, [gpre_ref])

    @pl.when(g == T - 1)
    def _():
        back, _ = norm_back(hid_ref[...], gain_ref[1:2], acc[...])
        branch_ref[...] = (gy_ref[...].astype(F32) + back).astype(BF16)
        back_own, gg = norm_back(hid_ref[: R * own], gain_ref[1:2], acc[: R * own])
        gg_ref[1:2] = gg
        ghid[...] = gy_ref[: R * own].astype(F32) + back_own

    @pl.when(g >= T)
    def _():
        lanes = jnp.concatenate([wa_ref[z, 0, 3] for z in range(nz)], axis=1)
        gmix[...] = mm_t(branch_ref[...], lanes).astype(BF16)
        masks = head_masks((N, BLK))
        for r in range(R):
            q, k, v = (pick(proj_ref.at[0, i], r, R, own) for i in range(3))
            q4 = spread(q, masks)
            p = head_weights(q4, k, bias_ref[r])
            gm4 = spread(pick(gmix, r, R, own), masks)
            ga = mm_t(gm4, v)
            gs = (SCALE * p * (ga - jnp.sum(p * ga, axis=-1, keepdims=True))).astype(BF16)
            place(held.at[0], r, R, own, gathered(mm(gs, k), masks).astype(BF16))
            place(held.at[1], r, R, own, inner(gs, q4).astype(BF16))
            place(held.at[2], r, R, own, inner(p.astype(BF16), gm4).astype(BF16))

        @pl.when(g == T)
        def _():
            gproj_ref[...] = held[...]

        part = None
        for which in range(3):
            piece = mm_t(held[which, : R * own], deep(wa_ref, which))
            part = piece if part is None else part + piece
        acc_in[...] = part + jnp.where(g == T, 0.0, acc_in[...])

    @pl.when(g == 2 * T - 1)
    def _():
        back, gg = norm_back(s_ref[: R * own], gain_ref[0:1], acc_in[...])
        gg_ref[0:1] = gg
        frame_ref[...] = ghid[...] + back
        stored(pres, sems, [gpre_ref])


def frames_bwd(order, gy, hid, slope, W, gain, proj, bias, s, own):
    rows, D = hid.shape
    T = W.shape[1]
    R = bias.shape[0]
    return call(
        functools.partial(frames_bwd_body, own),
        order,
        (gy, hid, slope, W, W, gain, proj, bias, s),
        [
            whole(gy.shape),
            whole(hid.shape),
            pl.BlockSpec((1, 4, rows, BLK), lambda g, order: (jnp.minimum(g, T - 1) * order[ACTIVE], 0, 0, 0)),
            weight_spec(W, lambda g: (g % T, 1 - g // T)),
            weight_spec(W, lambda g: (jnp.minimum(g, T - 1), 2)),
            whole(gain.shape),
            pl.BlockSpec((1, 3, rows, BLK), lambda g, order: (jnp.maximum(g - T, 0) * order[ACTIVE], 0, 0, 0)),
            whole(bias.shape),
            whole(s.shape),
        ],
        (
            struct((4, rows, BLK), BF16),
            struct((rows, D), BF16),
            struct((3, rows, BLK), BF16),
            struct((R * own, D), F32),
            struct((2, D), F32),
        ),
        (
            HBM_REF,
            whole((rows, D)),
            whole((3, rows, BLK)),
            whole((R * own, D)),
            whole((2, D)),
        ),
        2 * T,
        (
            pltpu.VMEM((3, rows, BLK), BF16),
            pltpu.VMEM((rows, D), F32),
            pltpu.VMEM((R * own, D), F32),
            pltpu.VMEM((R * own, D), F32),
            pltpu.VMEM((2, 4, rows, BLK), BF16),
            pltpu.VMEM((rows, BLK), BF16),
            pltpu.SemaphoreType.DMA((1,)),
        ),
        flops=2 * rows * D * 14 * D,
        moved=24 * D * D + rows * D * 30,
    )


def head_sum(prods):
    row = lax.broadcasted_iota(jnp.int32, (BLK, BLK), 0) // HEAD_DIM
    col = lax.broadcasted_iota(jnp.int32, (BLK, BLK), 1) // HEAD_DIM
    ones = jnp.where(row == col, 1.0, 0.0).astype(BF16)
    high = prods.astype(BF16)
    low = (prods - high.astype(F32)).astype(BF16)
    return mm(high, ones) + mm(low, ones)


def token_pairs(count):
    return [(a, b) for a in range(1, count) for b in range(a + 1)]


def pair_sums(left, right, count):
    pairs = token_pairs(count)
    m = left[0].shape[0]
    sums = head_sum(jnp.concatenate([left[a] * right[b] for a, b in pairs], axis=0))
    return {pair: sums[i * m : (i + 1) * m] for i, pair in enumerate(pairs)}


def token_weights(q, k, count):
    s = pair_sums(q, k, count)
    out = {}
    for a in range(1, count):
        top = s[a, 0]
        for b in range(1, a + 1):
            top = jnp.maximum(top, s[a, b])
        e = [jnp.exp((s[a, b] - top) * SCALE) for b in range(a + 1)]
        total = e[0]
        for b in range(1, a + 1):
            total = total + e[b]
        share = 1.0 / total
        for b in range(a + 1):
            out[a, b] = e[b] * share
    return out


def rounded(value):
    return value.astype(BF16).astype(F32)


def split_tokens(value, count):
    m = value.shape[0] // count
    return [value[i * m : (i + 1) * m].astype(F32) for i in range(count)]


def codes_fwd_body(order, codes_ref, sent_ref, cot_ref, gact_ref, w_ref, gain_ref, proj_ref, hid_ref, ghid_ref, gg_ref, own_ref, far_ref, other_ref, bundle_ref, nin, nmid, branch, acc, acts, pres, mixes, sems):
    g = pl.program_id(0)
    T = pl.num_programs(0) // 2
    C, m, _ = codes_ref.shape
    nz = w_ref.shape[0]
    four = lambda ref, at: ref.at[pl.ds(at, 4)]
    to_a = [four(own_ref, 0), far_ref, four(bundle_ref, 0), other_ref]
    to_p = [four(own_ref, 4), four(own_ref, 8), four(bundle_ref, 4), four(bundle_ref, 8)]
    to_m = [own_ref.at[12], own_ref.at[13], bundle_ref.at[24], bundle_ref.at[25]]
    wides = [(nin, 12), (nmid, 16), (branch, 20)]

    def move(i):
        wide, at = wides[i]
        return pltpu.make_async_copy(wide, four(bundle_ref, at), sems.at[3, i])

    @pl.when(g == 0)
    def _():
        for c in range(C):
            s = codes_ref[c].astype(F32) + sent_ref[...].astype(F32)
            rows = pl.ds(c * m, m)
            hid_ref[rows] = s
            s = normed(s, gain_ref[0:1])
            for z in range(nz):
                nin[z, rows] = s[:, z * BLK : (z + 1) * BLK]
        move(0).start()

    @pl.when(g < T)
    def _():
        part = []
        wide = jnp.concatenate([nin[z] for z in range(nz)], axis=1)
        for which in range(3):
            block = mm(wide, deep(w_ref, which)).astype(BF16)
            proj_ref[0, which] = block
            part.append(split_tokens(block, C))
        q, k, v = part
        p = token_weights(q, k, C)
        mixed = [v[0]]
        for a in range(1, C):
            total = rounded(p[a, 0]) * v[0]
            for b in range(1, a + 1):
                total += rounded(p[a, b]) * v[b]
            mixed.append(total)
        mixed = jnp.concatenate(mixed, axis=0).astype(BF16)
        mixes[g] = mixed
        for z in range(nz):
            hid_ref[:, z * BLK : (z + 1) * BLK] += mm(mixed, w_ref[z, 0, 3])

    @pl.when(g == T)
    def _():
        s = normed(hid_ref[...], gain_ref[1:2])
        for z in range(nz):
            nmid[z] = s[:, z * BLK : (z + 1) * BLK]
        move(1).start()

    @pl.when(g >= T)
    def _():
        part = None
        wide = jnp.concatenate([nmid[z] for z in range(nz)], axis=1)
        for j in range(4):
            act, slope = gelu_pair(mm(wide, deep(w_ref, j)))
            gpre = (gact_ref[0, j].astype(F32) * slope).astype(BF16)
            acts[g - T, j] = act.astype(BF16)
            pres[g - T, j] = gpre
            piece = mm_t(gpre, deep(w_ref, j))
            part = piece if part is None else part + piece
        acc[...] = part + jnp.where(g == T, 0.0, acc[...])

    store_out(g, 0, mixes, sems.at[0], to_m)
    store_out(g, T, acts, sems.at[1], to_a)
    store_out(g, T, pres, sems.at[2], to_p)

    @pl.when(g == 2 * T - 1)
    def _():
        back, gg = norm_back(hid_ref[...], gain_ref[1:2], acc[...])
        gg_ref[...] = gg
        ghid = cot_ref[...].astype(F32) + back
        ghid_ref[...] = ghid
        for z in range(nz):
            branch[z] = ghid[:, z * BLK : (z + 1) * BLK].astype(BF16)
        move(2).start()
        stored(mixes, sems.at[0], to_m)
        stored(acts, sems.at[1], to_a)
        stored(pres, sems.at[2], to_p)
        for i in range(3):
            move(i).wait()


OWN_BLOCKS, BUNDLE = 14, 26


def kept(shape, first, half):
    return pl.BlockSpec(
        (1,) + shape, lambda g, order: (clip(g - first, 0, half - 1) * order[ACTIVE],) + (0,) * len(shape)
    )


def codes_fwd(order, codes, sent, cot, gact, W, gain):
    C, m, D = codes.shape
    rows = C * m
    nz, T = W.shape[:2]
    act = struct((4, rows, BLK), BF16)
    wide = pltpu.VMEM((nz, rows, BLK), BF16)
    return call(
        codes_fwd_body,
        order,
        (codes, sent, cot, gact, W, gain),
        [
            whole(codes.shape),
            whole(sent.shape),
            whole(cot.shape),
            kept((4, rows, BLK), T, T),
            weight_spec(W, lambda g: (g % T, g // T)),
            whole(gain.shape),
        ],
        (
            struct((T, 3, rows, BLK), BF16),
            struct((rows, D), F32),
            struct((rows, D), F32),
            struct((1, D), F32),
            struct((OWN_BLOCKS, rows, BLK), BF16),
            act,
            act,
            struct((BUNDLE, rows, BLK), BF16),
        ),
        (
            kept((3, rows, BLK), 0, T),
            whole((rows, D)),
            whole((rows, D)),
            whole((1, D)),
            *[HBM_REF] * 4,
        ),
        2 * T,
        (
            wide,
            wide,
            wide,
            pltpu.VMEM((rows, D), F32),
            pltpu.VMEM((T, 4, rows, BLK), BF16),
            pltpu.VMEM((T, 4, rows, BLK), BF16),
            pltpu.VMEM((T, rows, BLK), BF16),
            pltpu.SemaphoreType.DMA((4, T)),
        ),
        flops=2 * rows * D * 12 * D,
        moved=16 * D * D + rows * D * 40,
    )


def codes_gact_body(order, cot_ref, wd_ref, gact_ref):
    for j in range(4):
        lanes = jnp.concatenate([wd_ref[z, 0, j] for z in range(wd_ref.shape[0])], axis=1)
        gact_ref[0, j] = mm_t(cot_ref[...], lanes).astype(BF16)


def codes_gact(order, cot, W):
    rows, D = cot.shape
    T = W.shape[1]
    return call(
        codes_gact_body,
        order,
        (cot, W),
        [whole(cot.shape), weight_spec(W, lambda g: (g, 2))],
        struct((T, 4, rows, BLK), BF16),
        pl.BlockSpec((1, 4, rows, BLK), lambda g, order: (g * order[ACTIVE], 0, 0, 0)),
        T,
        flops=2 * rows * D * 4 * D,
        moved=8 * D * D + rows * D * 10,
    )


def codes_back_body(order, proj_ref, w_ref, codes_ref, sent_ref, ghid_ref, gain_ref, keep_ref, send_ref, glocal_ref, gsent_ref, gg_ref, acc, held, branch, sems):
    g = pl.program_id(0)
    C, m, _ = codes_ref.shape
    T = pl.num_programs(0)

    @pl.when(g == 0)
    def _():
        branch[...] = ghid_ref[...].astype(BF16)

    nz = w_ref.shape[0]
    lanes = jnp.concatenate([w_ref[z, 0, 3] for z in range(nz)], axis=1)
    gmix = mm_t(branch[...], lanes)
    gm = split_tokens(gmix.astype(BF16), C)
    q, k, v = (split_tokens(proj_ref[0, i], C) for i in range(3))
    p = token_weights(q, k, C)
    ga = pair_sums(gm, v, C)

    def add(left, right):
        return right if left is None else left + right

    gq, gk, gv = [jnp.zeros_like(q[0])], [None] * C, [gm[0]] + [None] * (C - 1)
    for a in range(1, C):
        centre = p[a, 0] * ga[a, 0]
        for b in range(1, a + 1):
            centre += p[a, b] * ga[a, b]
        total = None
        for b in range(a + 1):
            gs = rounded(SCALE * p[a, b] * (ga[a, b] - centre))
            total = add(total, gs * k[b])
            gk[b] = add(gk[b], gs * q[a])
            gv[b] = add(gv[b], rounded(p[a, b]) * gm[a])
        gq.append(total)
    joined = [jnp.concatenate(part, axis=0).astype(BF16) for part in (gq, gk, gv)]

    for which in range(3):
        held[g, which] = joined[which]
    part = None
    for which in range(3):
        part = add(part, mm_t(joined[which], deep(w_ref, which)))
    acc[...] = part + jnp.where(g == 0, 0.0, acc[...])
    outs = [keep_ref.at[0], keep_ref.at[1], send_ref.at[0], send_ref.at[1]]
    store_out(g, 0, held, sems, outs)

    @pl.when(g == T - 1)
    def _():
        total = None
        gains = None
        for c in range(C):
            rows = slice(c * m, (c + 1) * m)
            s = codes_ref[c].astype(F32) + sent_ref[...].astype(F32)
            back, gg = norm_back(s, gain_ref[0:1], acc[rows])
            gains = add(gains, gg)
            local = (ghid_ref[rows] + back).astype(BF16)
            glocal_ref[c] = local
            total = add(total, local.astype(F32))
        gsent_ref[...] = total.astype(BF16)
        gg_ref[...] = gains
        stored(held, sems, outs)


def codes_back(order, proj, W, codes, sent, ghid, gain):
    rows, D = ghid.shape
    C, m, _ = codes.shape
    T = W.shape[1]
    half = T // 2
    blocks = struct((half, 3, rows, BLK), BF16)
    return call(
        codes_back_body,
        order,
        (proj, W, codes, sent, ghid, gain),
        [
            pl.BlockSpec((1, 3, rows, BLK), lambda g, order: (g * order[ACTIVE], 0, 0, 0)),
            weight_spec(W, lambda g: (g, 0)),
            whole(codes.shape),
            whole(sent.shape),
            whole(ghid.shape),
            whole(gain.shape),
        ],
        (blocks, blocks, struct(codes.shape, BF16), struct((m, D), BF16), struct((1, D), F32)),
        (
            HBM_REF,
            HBM_REF,
            whole(codes.shape),
            whole((m, D)),
            whole((1, D)),
        ),
        T,
        (
            pltpu.VMEM((rows, D), F32),
            pltpu.VMEM((T, 3, rows, BLK), BF16),
            pltpu.VMEM((rows, D), BF16),
            pltpu.SemaphoreType.DMA((T,)),
        ),
        flops=2 * rows * D * 4 * D,
        moved=8 * D * D + rows * D * 20,
    )


def codes_out_body(order, hid_ref, a0_ref, a1_ref, a2_ref, a3_ref, wd_ref, out_ref, acc):
    g = pl.program_id(0)
    T = pl.num_programs(0)
    C, m, _ = out_ref.shape

    @pl.when(g == 0)
    def _():
        acc[...] = hid_ref[...]

    for i, act_ref in enumerate((a0_ref, a1_ref, a2_ref, a3_ref)):

        @pl.when(g == i)
        def _():
            act = jnp.concatenate([act_ref[j] for j in range(4)], axis=1)
            for z in range(wd_ref.shape[0]):
                acc[:, z * BLK : (z + 1) * BLK] += mm(act, wd_ref[z, 0].reshape(-1, BLK))

    @pl.when(g == T - 1)
    def _():
        for c in range(C):
            out_ref[c] = acc[c * m : (c + 1) * m].astype(BF16)


def codes_out(order, hid, acts, W, C):
    rows, D = hid.shape
    T = W.shape[1]
    m = rows // C
    return call(
        codes_out_body,
        order,
        (hid, *acts, W),
        [
            whole(hid.shape),
            *[pl.BlockSpec((4, rows, BLK), lambda g, order: (0, 0, 0))] * 4,
            weight_spec(W, lambda g: (g, 2)),
        ],
        struct((C, m, D), BF16),
        whole((C, m, D)),
        T,
        (pltpu.VMEM((rows, D), F32),),
        flops=2 * rows * D * 4 * D,
        moved=8 * D * D + rows * D * 14,
    )


def put(ref, value, by_rows):
    for z in range(ref.shape[0]):
        at = slice(z * BLK, (z + 1) * BLK)
        ref[z, 0] = (value[at] if by_rows else value[:, at]).astype(BF16)


def got(ref, by_rows):
    parts = [ref[z, 0].astype(F32) for z in range(ref.shape[0])]
    return jnp.concatenate(parts, axis=0 if by_rows else 1)


def grads_body(parts, has_got, flag, *refs):
    g = pl.program_id(0)
    slots = sum(part[0] and max(part[3], part[4]) for part in parts)
    out_ref = refs[len(refs) - 1 - slots]
    turned = refs[len(refs) - slots :]
    got_ref = refs[len(refs) - 2 - slots]
    at = 0
    for by_rows, begin, end, ones, zeros in parts:
        for value, count in ((1, ones), (0, zeros)):
            pairs = [(refs[at + 2 * i], refs[at + 2 * i + 1]) for i in range(count)]
            at += 2 * count
            if not count:
                continue

            def full(wide):
                if len(wide.shape) == 3:
                    return jnp.concatenate([wide[z] for z in range(wide.shape[0])], axis=1)
                return wide[...]

            if by_rows:

                @pl.when((flag[0] == value) & (g == begin))
                def _():
                    for (wide, _), turn in zip(pairs, turned):
                        turn[:, : wide.shape[-2]] = full(wide).T

            @pl.when((flag[0] == value) & (g >= begin) & (g < end))
            def _():
                total = None
                for i, (wide, narrow) in enumerate(pairs):
                    if by_rows:
                        piece = mm(turned[i][:, : wide.shape[-2]], narrow[0])
                    else:
                        piece = inner(narrow[0], full(wide))
                    total = piece if total is None else total + piece
                if has_got and value == 0:
                    total = total + got(got_ref, by_rows)
                put(out_ref, total, by_rows)


def grads(flag, nz, parts, received=None):
    inputs, specs, plan = [], [], []
    begin = flops = moved = 0
    for by_rows, count, ones, zeros in parts:
        for wide, narrow, base, *more in ones + zeros:
            if isinstance(wide, tuple):
                wide, at = wide
                rows = wide.shape[1]
                specs.append(
                    pl.BlockSpec((nz, rows, BLK), lambda g, f, a=at // nz: (a, 0, 0))
                )
            else:
                rows = wide.shape[0]
                specs.append(whole(wide.shape))
            specs.append(
                pl.BlockSpec(
                    (1, rows, BLK),
                    lambda g, f, s=begin, b=base, c=count, m=sum(more): (
                        b + clip(g - s, 0, c - 1),
                        m,
                        0,
                    ),
                )
            )
            inputs += [wide, narrow]
            flops += rows * nz * BLK * BLK * count
            moved += 4 * rows * nz * BLK
        plan.append((by_rows, begin, begin + count, len(ones), len(zeros)))
        begin += count
    turns = []
    for by_rows, _, ones, zeros in parts:
        if by_rows:
            rows = [[p[1].shape[1] for p in side] for side in (ones, zeros)]
            for i in range(max(len(side) for side in rows)):
                longest = max(side[i] for side in rows if len(side) > i)
                turns.append(pltpu.VMEM((nz * BLK, longest), BF16))
    block = pl.BlockSpec((nz, 1, BLK, BLK), lambda g, f: (0, g, 0, 0))
    if received is not None:
        inputs.append(received)
        specs.append(block)
    return call(
        functools.partial(grads_body, plan, received is not None),
        flag,
        inputs,
        specs,
        struct((nz, begin, BLK, BLK), BF16),
        block,
        begin,
        turns,
        flops=2 * flops,
        moved=moved + nz * begin * BLK * BLK * 4,
    )


def swap(value, axis, bit):
    count = lax.axis_size(axis)
    return lax.ppermute(value, axis, [(i, i ^ bit) for i in range(count)])


def swap_in(value, section, bit):
    count = lax.axis_size("tensor")
    pairs = [(section * count + i, section * count + (i ^ bit)) for i in range(count)]
    return lax.ppermute(value, ("section", "tensor"), pairs)


def together(*values):
    return lax.optimization_barrier(values)


def after(value, *others):
    return together(value, *others)[0]


def gather_weights(w_qkv, w_out, w_up, w_down):
    depth = w_qkv.shape[1]
    shards = lax.axis_size("dp")
    slices = lax.axis_size("tensor")
    both = ("dp", "tensor")
    if depth == BLK:
        up_blocks = [w_up[None, :, i : i + BLK] for i in range(0, w_up.shape[1], BLK)]
        flat = jnp.concatenate(
            [w_qkv, w_out[None], *up_blocks, w_down.reshape(-1, BLK, BLK)], axis=0
        )
        out = lax.all_gather(flat, both)
        return out.reshape(shards, slices, *flat.shape)
    per = BLK // depth
    nz = shards // per

    def by_rows(value):
        out = lax.all_gather(value, both).reshape(nz, per, slices, value.shape[0], depth, BLK)
        return out.transpose(0, 2, 3, 1, 4, 5).reshape(nz, slices, -1, BLK, BLK)

    def by_cols(value):
        out = lax.all_gather(value, both)
        out = out.reshape(nz, per, slices, value.shape[0] // BLK, BLK, depth)
        return out.transpose(0, 2, 3, 4, 1, 5).reshape(nz, slices, -1, BLK, BLK)

    up_blocks = w_up.reshape(depth, -1, BLK).transpose(1, 0, 2)
    return jnp.concatenate(
        [by_rows(w_qkv), by_cols(w_out), by_rows(up_blocks), by_cols(w_down)], axis=2
    )


def scatter_blocks(parts, split):
    shards = lax.axis_size("dp")
    nz, count = parts.shape[:2]
    per = shards // nz
    if per == 1:
        out = lax.psum_scatter(parts, "dp", scatter_dimension=0, tiled=False)
        return out[:split], out[split:]
    depth = BLK // per
    rows = parts[:, :split].reshape(nz, split, per, depth, BLK)
    rows = rows.transpose(0, 2, 1, 3, 4).reshape(shards, -1, BLK)
    columns = parts[:, split:].reshape(nz, count - split, BLK, per, depth)
    columns = columns.transpose(0, 3, 1, 2, 4).reshape(shards, -1, BLK)
    out = lax.psum_scatter(
        jnp.concatenate([rows, columns], axis=1), "dp", scatter_dimension=0, tiled=False
    )
    cut = split * depth
    return out[:cut].reshape(split, depth, BLK), out[cut:].reshape(-1, BLK, depth)


def on_device(codes, cotangent, doc_lengths, w_qkv, w_out, w_up, w_down, gains):
    is_first = lax.axis_index("section") == 0
    flag = is_first.astype(jnp.int32).reshape(1)
    t = lax.axis_index("tensor")
    T = lax.axis_size("tensor")
    R, F, C, D = codes.shape
    M = R * F
    N = T * F
    gain = gains[0]
    W = gather_weights(w_qkv[0], w_out[0], w_up[0], w_down[0])
    nz = W.shape[0]
    slices = t ^ jnp.array([0, 2, 1, 3], jnp.int32)
    order0 = jnp.concatenate([slices, flag])
    order1 = jnp.concatenate([slices, 1 - flag])
    codes_t = codes.transpose(2, 0, 1, 3).reshape(C, M, D)
    cot = cotangent.transpose(2, 0, 1, 3).reshape(C * M, D)

    frame_own = jnp.sum(codes_t.astype(F32), axis=0)
    far = swap(frame_own, "tensor", 2)
    s0 = jnp.concatenate(
        [frame_own, swap(frame_own, "tensor", 1), far, swap(far, "tensor", 1)], axis=0
    )
    spot = t ^ lax.iota(jnp.int32, T)
    pos = (spot[:, None] * F + lax.iota(jnp.int32, F)[None]).reshape(N)
    ends = jnp.cumsum(doc_lengths, axis=1)
    seg = jnp.sum((pos[None, :, None] >= ends[:, None, :]).astype(jnp.int32), axis=2)
    allowed = (pos[:, None] >= pos[None, :])[None] & (seg[:, :, None] == seg[:, None, :])
    bias = jnp.where(allowed, 0.0, NEG).astype(F32)

    n_in0, proj0, mixed0, hid0, n_mid0, act0, slope0, out0 = frames_fwd(order0, s0, W, gain, bias, F)
    sent = lax.ppermute(out0, "section", [(0, 1)])

    def swap1(value, bit):
        return swap_in(value, 1, bit)

    gact1 = codes_gact(order1, cot, W)
    late = after(cot, s0)
    cot_y = swap1(late, 2)
    cot_s, cot_d = swap1(late, 1), swap1(cot_y, 1)
    sent = after(sent, cot_s, cot_d)
    proj1, hid1, ghid1, gg_mid1, own1, act_far, act_other, bundle = codes_fwd(
        order1, codes_t, sent, cot, gact1, W, gain
    )
    act_y = swap1(act_far, 2)
    act_o = swap1(act_other, 1)
    bundle_s = swap1(bundle, 1)
    gproj1, gproj1_s, glocal, gsent, gg_in1 = codes_back(
        order1, proj1, W, codes_t, sent, ghid1, gain
    )

    gproj1, gproj1_s, glocal, gsent, gg_in1, act_y, act_o, bundle_s = together(
        gproj1, gproj1_s, glocal, gsent, gg_in1, act_y, act_o, bundle_s
    )

    gsent = lax.ppermute(gsent, "section", [(1, 0)])
    act_d = swap1(act_o, 2)
    out1 = codes_out(order1, hid1, [own1, act_far, bundle, act_other], W, C)
    gsent, out1 = together(gsent, out1)
    gfar = swap_in(gsent, 0, 2)

    M1 = C * M
    gproj1 = gproj1.reshape(-1, M1, BLK)
    bundle_s = after(bundle_s, gsent)
    gproj1_s = swap1(after(gproj1_s, gsent), 1).reshape(-1, M1, BLK)
    up_far = grads(
        flag, nz, [(True, 4, [], [((bundle, 16), own1, 8), ((bundle_s, 16), bundle_s, 8)])]
    )
    up_got = swap1(up_far, 2)
    att_far = grads(
        flag,
        nz,
        [
            (True, 3, [], [((bundle, 12), gproj1, 3), ((bundle_s, 12), gproj1_s, 3)]),
            (False, 1, [], [((bundle, 20), own1, 13), ((bundle_s, 20), bundle_s, 25)]),
        ],
    )
    gfar, up_far, att_far = together(gfar, up_far, att_far)
    att_got = swap1(att_far, 2)
    glocal = lax.ppermute(after(glocal, gfar), "section", [(1, 0)])
    gy0 = jnp.concatenate(
        [gsent, swap_in(gsent, 0, 1), gfar, swap_in(gfar, 0, 1)], axis=0
    )

    down_total = grads(
        flag,
        nz,
        [
            (
                False,
                4,
                [(gy0, act0, 0)],
                [(cot, own1, 0), (cot_s, bundle_s, 0), (cot_y, act_y, 0), (cot_d, act_d, 0)],
            )
        ],
    )
    down_part = scatter_blocks(down_total, 0)[1]

    gpre0, branch0, gproj0, frame, gg0 = frames_bwd(
        order0, gy0, hid0, slope0, W, gain, proj0, bias, s0, F
    )
    up_total = grads(
        flag,
        nz,
        [
            (
                True,
                4,
                [(n_mid0, gpre0, 0)],
                [((bundle, 16), own1, 4), ((bundle_s, 16), bundle_s, 4)],
            )
        ],
        up_got,
    )
    up_part = scatter_blocks(up_total, 4)[0]
    gproj0 = after(gproj0, up_total, glocal)
    att_total = grads(
        flag,
        nz,
        [
            (
                True,
                3,
                [(n_in0, gproj0, 0)],
                [((bundle, 12), gproj1, 0), ((bundle_s, 12), gproj1_s, 0)],
            ),
            (
                False,
                1,
                [(branch0, mixed0[None], 0)],
                [((bundle, 20), own1, 12), ((bundle_s, 20), bundle_s, 24)],
            ),
        ],
        att_got,
    )
    qkv_part, out_part = scatter_blocks(att_total, 3)
    gain_part = jnp.where(is_first, gg0, jnp.concatenate([gg_in1, gg_mid1], axis=0))
    grad_gains = lax.psum(after(gain_part, att_total), ("dp", "tensor"))

    code_grad = (glocal.astype(F32) + frame[None]).astype(BF16)
    result = jnp.where(is_first, code_grad, out1).reshape(C, R, F, D).transpose(1, 2, 0, 3)
    depth = w_up.shape[1]
    return (
        result[None],
        qkv_part.astype(F32)[None],
        out_part.reshape(-1, depth).astype(F32)[None],
        up_part.transpose(1, 0, 2).reshape(depth, -1).astype(F32)[None],
        down_part.reshape(-1, depth).astype(F32)[None],
        grad_gains[None],
    )


def solution(mesh):
    placed = (
        P("dp", "tensor", None, None),
        P("dp", "tensor", None, None),
        P("dp", None),
        P("section", None, "dp", "tensor"),
        P("section", "tensor", "dp"),
        P("section", "dp", "tensor"),
        P("section", "tensor", "dp"),
        P("section", None, None),
    )
    return jax.shard_map(
        on_device,
        mesh=mesh,
        in_specs=placed,
        out_specs=(
            P("section", "dp", "tensor", None, None),
            P("section", None, "dp", "tensor"),
            P("section", "tensor", "dp"),
            P("section", "dp", "tensor"),
            P("section", "tensor", "dp"),
            P("section", None, None),
        ),
        check_vma=False,
    )
```

```python
import functools

import jax
import jax.numpy as jnp
from jax import lax
from jax.experimental import pallas as pl
from jax.experimental.pallas import tpu as pltpu
from jax.sharding import PartitionSpec as P

HEAD_DIM = 64
BLK = 256
HEADS = BLK // HEAD_DIM
EPS = 1e-05
NEG = -1e30
SCALE = 0.125
F32 = jnp.float32
BF16 = jnp.bfloat16
VMEM = 60 * 1024 * 1024
ACTIVE = 4
COST = 8
LONG = 10**11


def mm(left, right):
    return jnp.dot(left, right, preferred_element_type=F32)


def mm_t(left, right):
    return lax.dot_general(left, right, (((1,), (1,)), ((), ())), preferred_element_type=F32)


def inner(left, right):
    return lax.dot_general(left, right, (((0,), (0,)), ((), ())), preferred_element_type=F32)


def unit_of(values):
    inv_root = lax.rsqrt(jnp.mean(values * values, axis=-1, keepdims=True) + EPS)
    return values * inv_root, inv_root


def normed(values, gain):
    return (unit_of(values)[0] * gain).astype(BF16)


def norm_back(values, gain, grad):
    unit_rows, inv_root = unit_of(values)
    scaled = grad * gain
    back = inv_root * (scaled - unit_rows * jnp.mean(unit_rows * scaled, axis=-1, keepdims=True))
    return back, jnp.sum(grad * unit_rows, axis=0, keepdims=True)


def gelu_pair(pre):
    square = pre * pre
    th = jnp.tanh(0.7978845608028654 * pre * (1.0 + 0.044715 * square))
    half = 0.5 + 0.5 * th
    act = pre * half
    slope = half + act * (1.0 - th) * (0.7978845608028654 + 3 * 0.044715 * 0.7978845608028654 * square)
    return act, slope


def head_masks(shape):
    lane = lax.broadcasted_iota(jnp.int32, shape, 1) // HEAD_DIM
    return [lane == h for h in range(HEADS)]


def spread(value, masks):
    zero = jnp.zeros_like(value)
    return jnp.concatenate([jnp.where(m, value, zero) for m in masks], axis=0)


def gathered(value, masks):
    n = value.shape[0] // HEADS
    out = jnp.where(masks[0], value[:n], 0.0)
    for h in range(1, HEADS):
        out = jnp.where(masks[h], value[h * n : (h + 1) * n], out)
    return out


def head_weights(q4, k, bias):
    s = mm_t(q4, k) * SCALE + jnp.concatenate([bias] * HEADS, axis=0)
    e = jnp.exp(s - jnp.max(s, axis=-1, keepdims=True))
    return e / jnp.sum(e, axis=-1, keepdims=True)


def whole(shape):
    return pl.BlockSpec(shape, lambda g, order: (0,) * len(shape))


def struct(shape, dtype):
    return jax.ShapeDtypeStruct(shape, dtype)


def call(body, order, inputs, in_specs, outs, out_specs, grid, scratch=(), flops=0, moved=0):
    def run(flags, *refs):
        if flags.shape[0] <= ACTIVE:
            return body(flags, *refs)

        @pl.when(flags[ACTIVE] == 1)
        def _():
            body(flags, *refs)

    return pl.pallas_call(
        run,
        out_shape=outs,
        grid_spec=pltpu.PrefetchScalarGridSpec(
            num_scalar_prefetch=1,
            grid=(grid,),
            in_specs=in_specs,
            out_specs=out_specs,
            scratch_shapes=scratch,
        ),
        compiler_params=pltpu.CompilerParams(
            dimension_semantics=("arbitrary",), vmem_limit_bytes=VMEM
        ),
        cost_estimate=pl.CostEstimate(
            flops=flops // COST, bytes_accessed=moved // COST, transcendentals=0
        ),
    )(order, *inputs)


def weight_spec(W, third):
    nz = W.shape[0]

    def at(g, order):
        step, which = third(g)
        return (0, order[step] * order[ACTIVE], which * order[ACTIVE], 0, 0)

    return pl.BlockSpec((nz, 1, 4, BLK, BLK), at)


def clip(g, low, high):
    return jnp.minimum(jnp.maximum(g, low), high)


def deep(ref, index):
    return ref[:, 0, index].reshape(-1, BLK)


def store_out(g, first, held, sems, outs):
    for i, out in enumerate(outs):

        @pl.when(g == first + i)
        def _():
            pltpu.make_async_copy(held.at[i], out, sems.at[i]).start()


def stored(held, sems, outs):
    for i, out in enumerate(outs):
        pltpu.make_async_copy(held.at[i], out, sems.at[i]).wait()


HBM_REF = pl.BlockSpec(memory_space=pl.ANY)


def pick(ref, r, R, F):
    return jnp.concatenate(
        [ref[pl.ds(at, F)] for at in range(r * F, ref.shape[0], R * F)], axis=0
    )


def place(ref, r, R, F, value):
    for i, at in enumerate(range(r * F, ref.shape[0], R * F)):
        ref[pl.ds(at, F)] = value[i * F : (i + 1) * F]


def frames_fwd_body(own, order, s_ref, wa_ref, gain_ref, bias_ref, nin_ref, proj_ref, mixed_ref, hid_ref, nmid_ref, act_ref, slope_ref, held, acts, sems):
    g = pl.program_id(0)
    T = pl.num_programs(0) // 2
    R, N = bias_ref.shape[:2]
    nz = wa_ref.shape[0]

    @pl.when(g == 0)
    def _():
        s = s_ref[...]
        nin_ref[...] = normed(s, gain_ref[0:1])
        hid_ref[...] = s

    @pl.when(g < T)
    def _():
        for which in range(3):
            proj_ref[0, which] = mm(nin_ref[...], deep(wa_ref, which)).astype(BF16)
        masks = head_masks((N, BLK))
        for r in range(R):
            q, k, v = (pick(proj_ref.at[0, i], r, R, own) for i in range(3))
            p = head_weights(spread(q, masks), k, bias_ref[r])
            place(held, r, R, own, gathered(mm(p.astype(BF16), v), masks).astype(BF16))
        for z in range(nz):
            hid_ref[:, z * BLK : (z + 1) * BLK] += mm(held[...], wa_ref[z, 0, 3])

    @pl.when(g == 0)
    def _():
        mixed_ref[...] = held[...]

    @pl.when(g == T)
    def _():
        nmid_ref[...] = normed(hid_ref[...], gain_ref[1:2])

    @pl.when(g >= T)
    def _():
        for j in range(4):
            act, slope = gelu_pair(mm(nmid_ref[...], deep(wa_ref, j)))
            slope_ref[0, j] = slope.astype(BF16)
            acts[jnp.minimum(g - T, 1), j] = act.astype(BF16)

    store_out(g, T, acts, sems, [act_ref])

    @pl.when(g == 2 * T - 1)
    def _():
        stored(acts, sems, [act_ref])


def frames_fwd(order, s, W, gain, bias, own):
    rows, D = s.shape
    T = W.shape[1]
    return call(
        functools.partial(frames_fwd_body, own),
        order,
        (s, W, gain, bias),
        [
            whole(s.shape),
            weight_spec(W, lambda g: (g % T, g // T)),
            whole(gain.shape),
            whole(bias.shape),
        ],
        (
            struct((rows, D), BF16),
            struct((T, 3, rows, BLK), BF16),
            struct((rows, BLK), BF16),
            struct((rows, D), F32),
            struct((rows, D), BF16),
            struct((4, rows, BLK), BF16),
            struct((T, 4, rows, BLK), BF16),
        ),
        (
            whole((rows, D)),
            pl.BlockSpec((1, 3, rows, BLK), lambda g, order: (jnp.minimum(g, T - 1) * order[ACTIVE], 0, 0, 0)),
            whole((rows, BLK)),
            whole((rows, D)),
            whole((rows, D)),
            HBM_REF,
            pl.BlockSpec((1, 4, rows, BLK), lambda g, order: (jnp.maximum(g - T, 0) * order[ACTIVE], 0, 0, 0)),
        ),
        2 * T,
        (
            pltpu.VMEM((rows, BLK), BF16),
            pltpu.VMEM((2, 4, rows, BLK), BF16),
            pltpu.SemaphoreType.DMA((1,)),
        ),
        flops=2 * rows * D * 10 * D,
        moved=24 * D * D + rows * D * 30,
    )


def frames_own_body(own, order, s_ref, wa_ref, wb_ref, gain_ref, bias_ref, out_ref, nin, keys, values, held, hid, nmid):
    g = pl.program_id(0)
    T = pl.num_programs(0) // 2
    R, N = bias_ref.shape[:2]
    nz = wa_ref.shape[0]
    mine = R * own

    @pl.when(g == 0)
    def _():
        nin[...] = normed(s_ref[...], gain_ref[0:1])
        hid[...] = s_ref[:mine]

    @pl.when(g < T)
    def _():
        queries = mm(nin[:mine], deep(wa_ref, 0)).astype(BF16)
        keys[...] = mm(nin[...], deep(wa_ref, 1)).astype(BF16)
        values[...] = mm(nin[...], deep(wa_ref, 2)).astype(BF16)
        masks = head_masks((own, BLK))
        for r in range(R):
            q4 = spread(queries[r * own : (r + 1) * own], masks)
            p = head_weights(q4, pick(keys, r, R, own), bias_ref[r, :own])
            mixed = gathered(mm(p.astype(BF16), pick(values, r, R, own)), masks)
            held[r * own : (r + 1) * own] = mixed.astype(BF16)
        for z in range(nz):
            hid[:, z * BLK : (z + 1) * BLK] += mm(held[...], wa_ref[z, 0, 3])

    @pl.when(g == T)
    def _():
        nmid[...] = normed(hid[...], gain_ref[1:2])

    @pl.when(g >= T)
    def _():
        act = [gelu_pair(mm(nmid[...], deep(wa_ref, j)))[0].astype(BF16) for j in range(4)]
        act = jnp.concatenate(act, axis=1)
        for z in range(nz):
            hid[:, z * BLK : (z + 1) * BLK] += mm(act, wb_ref[z, 0].reshape(-1, BLK))

    @pl.when(g == 2 * T - 1)
    def _():
        out_ref[...] = hid[...].astype(BF16)


def frames_own(order, s, W, gain, bias, own):
    rows, D = s.shape
    T = W.shape[1]
    mine = bias.shape[0] * own
    return call(
        functools.partial(frames_own_body, own),
        order,
        (s, W, W, gain, bias),
        [
            whole(s.shape),
            weight_spec(W, lambda g: (g % T, g // T)),
            weight_spec(W, lambda g: (jnp.maximum(g - T, 0), 2)),
            whole(gain.shape),
            whole(bias.shape),
        ],
        struct((mine, D), BF16),
        whole((mine, D)),
        2 * T,
        (
            pltpu.VMEM((rows, D), BF16),
            pltpu.VMEM((rows, BLK), BF16),
            pltpu.VMEM((rows, BLK), BF16),
            pltpu.VMEM((mine, BLK), BF16),
            pltpu.VMEM((mine, D), F32),
            pltpu.VMEM((mine, D), BF16),
        ),
        flops=2 * mine * D * 12 * D,
        moved=24 * D * D,
    )


def frames_bwd_body(own, order, gy_ref, hid_ref, slope_ref, wa_ref, wb_ref, gain_ref, proj_ref, bias_ref, s_ref, gpre_ref, branch_ref, gproj_ref, frame_ref, gg_ref, held, acc, acc_in, ghid, pres, gmix, sems, hid_at, s_at, bias_at):
    g = pl.program_id(0)
    late = [
        pltpu.make_async_copy(a, b, sems.at[1 + i])
        for i, (a, b) in enumerate([(hid_ref, hid_at), (s_ref, s_at), (bias_ref, bias_at)])
    ]
    T = pl.num_programs(0) // 2
    R, N = bias_ref.shape[:2]
    nz = wa_ref.shape[0]

    @pl.when(g == 0)
    def _():
        for copy in late:
            copy.start()

    @pl.when(g < T)
    def _():
        part = None
        for j in range(4):
            lanes = jnp.concatenate([wb_ref[z, 0, j] for z in range(nz)], axis=1)
            gpre = (mm_t(gy_ref[...], lanes) * slope_ref[0, j].astype(F32)).astype(BF16)

            pres[jnp.minimum(g, 1), j] = gpre
            piece = mm_t(gpre, deep(wa_ref, j))
            part = piece if part is None else part + piece
        acc[...] = part + jnp.where(g == 0, 0.0, acc[...])

    store_out(g, 0, pres, sems, [gpre_ref])

    @pl.when(g == T - 1)
    def _():
        for copy in late:
            copy.wait()
        back, _ = norm_back(hid_at[...], gain_ref[1:2], acc[...])
        branch_ref[...] = (gy_ref[...].astype(F32) + back).astype(BF16)
        back_own, gg = norm_back(hid_at[: R * own], gain_ref[1:2], acc[: R * own])
        gg_ref[1:2] = gg
        ghid[...] = gy_ref[: R * own].astype(F32) + back_own

    @pl.when(g >= T)
    def _():
        lanes = jnp.concatenate([wa_ref[z, 0, 3] for z in range(nz)], axis=1)
        gmix[...] = mm_t(branch_ref[...], lanes).astype(BF16)
        masks = head_masks((N, BLK))
        for r in range(R):
            q, k, v = (pick(proj_ref.at[0, i], r, R, own) for i in range(3))
            q4 = spread(q, masks)
            p = head_weights(q4, k, bias_at[r])
            gm4 = spread(pick(gmix, r, R, own), masks)
            ga = mm_t(gm4, v)
            gs = (SCALE * p * (ga - jnp.sum(p * ga, axis=-1, keepdims=True))).astype(BF16)
            place(held.at[0], r, R, own, gathered(mm(gs, k), masks).astype(BF16))
            place(held.at[1], r, R, own, inner(gs, q4).astype(BF16))
            place(held.at[2], r, R, own, inner(p.astype(BF16), gm4).astype(BF16))

        @pl.when(g == T)
        def _():
            gproj_ref[...] = held[...]

        part = None
        for which in range(3):
            piece = mm_t(held[which, : R * own], deep(wa_ref, which))
            part = piece if part is None else part + piece
        acc_in[...] = part + jnp.where(g == T, 0.0, acc_in[...])

    @pl.when(g == 2 * T - 1)
    def _():
        back, gg = norm_back(s_at[...], gain_ref[0:1], acc_in[...])
        gg_ref[0:1] = gg
        frame_ref[...] = ghid[...] + back
        stored(pres, sems, [gpre_ref])


def frames_bwd(order, gy, hid, slope, W, gain, proj, bias, s, own):
    rows, D = hid.shape
    T = W.shape[1]
    R = bias.shape[0]
    return call(
        functools.partial(frames_bwd_body, own),
        order,
        (gy, hid, slope, W, W, gain, proj, bias, s),
        [
            whole(gy.shape),
            HBM_REF,
            pl.BlockSpec((1, 4, rows, BLK), lambda g, order: (jnp.minimum(g, T - 1) * order[ACTIVE], 0, 0, 0)),
            weight_spec(W, lambda g: (g % T, 1 - g // T)),
            weight_spec(W, lambda g: (jnp.minimum(g, T - 1), 2)),
            whole(gain.shape),
            pl.BlockSpec((1, 3, rows, BLK), lambda g, order: (jnp.maximum(g - T, 0) * order[ACTIVE], 0, 0, 0)),
            HBM_REF,
            HBM_REF,
        ],
        (
            struct((4, rows, BLK), BF16),
            struct((rows, D), BF16),
            struct((3, rows, BLK), BF16),
            struct((R * own, D), F32),
            struct((2, D), F32),
        ),
        (
            HBM_REF,
            whole((rows, D)),
            whole((3, rows, BLK)),
            whole((R * own, D)),
            whole((2, D)),
        ),
        2 * T,
        (
            pltpu.VMEM((3, rows, BLK), BF16),
            pltpu.VMEM((rows, D), F32),
            pltpu.VMEM((R * own, D), F32),
            pltpu.VMEM((R * own, D), F32),
            pltpu.VMEM((2, 4, rows, BLK), BF16),
            pltpu.VMEM((rows, BLK), BF16),
            pltpu.SemaphoreType.DMA((4,)),
            pltpu.VMEM((rows, D), F32),
            pltpu.VMEM((R * own, D), F32),
            pltpu.VMEM(bias.shape, F32),
        ),
        flops=2 * rows * D * 14 * D,
        moved=24 * D * D + rows * D * 30,
    )


def head_sum(prods):
    row = lax.broadcasted_iota(jnp.int32, (BLK, BLK), 0) // HEAD_DIM
    col = lax.broadcasted_iota(jnp.int32, (BLK, BLK), 1) // HEAD_DIM
    ones = jnp.where(row == col, 1.0, 0.0).astype(BF16)
    high = prods.astype(BF16)
    low = (prods - high.astype(F32)).astype(BF16)
    return mm(high, ones) + mm(low, ones)


def token_pairs(count):
    return [(a, b) for a in range(1, count) for b in range(a + 1)]


def pair_sums(left, right, count):
    pairs = token_pairs(count)
    m = left[0].shape[0]
    sums = head_sum(jnp.concatenate([left[a] * right[b] for a, b in pairs], axis=0))
    return {pair: sums[i * m : (i + 1) * m] for i, pair in enumerate(pairs)}


def token_weights(q, k, count):
    s = pair_sums(q, k, count)
    out = {}
    for a in range(1, count):
        top = s[a, 0]
        for b in range(1, a + 1):
            top = jnp.maximum(top, s[a, b])
        e = [jnp.exp((s[a, b] - top) * SCALE) for b in range(a + 1)]
        total = e[0]
        for b in range(1, a + 1):
            total = total + e[b]
        share = 1.0 / total
        for b in range(a + 1):
            out[a, b] = e[b] * share
    return out


def rounded(value):
    return value.astype(BF16).astype(F32)


def split_tokens(value, count):
    m = value.shape[0] // count
    return [value[i * m : (i + 1) * m].astype(F32) for i in range(count)]


def codes_fwd_body(order, codes_ref, sent_ref, cot_ref, gact_ref, w_ref, gain_ref, proj_ref, hid_ref, ghid_ref, gg_ref, own_ref, far_ref, other_ref, bundle_ref, nin, nmid, branch, acc, acts, pres, mixes, sems):
    g = pl.program_id(0)
    T = pl.num_programs(0) // 2
    C, m, _ = codes_ref.shape
    nz = w_ref.shape[0]
    four = lambda ref, at: ref.at[pl.ds(at, 4)]
    to_a = [four(own_ref, 0), far_ref, four(bundle_ref, 0), other_ref]
    to_p = [four(own_ref, 4), four(own_ref, 8), four(bundle_ref, 4), four(bundle_ref, 8)]
    to_m = [own_ref.at[12], own_ref.at[13], bundle_ref.at[24], bundle_ref.at[25]]
    wides = [(nin, 12), (nmid, 16), (branch, 20)]

    def move(i):
        wide, at = wides[i]
        return pltpu.make_async_copy(wide, four(bundle_ref, at), sems.at[3, i])

    @pl.when(g == 0)
    def _():
        for c in range(C):
            s = codes_ref[c].astype(F32) + sent_ref[...].astype(F32)
            rows = pl.ds(c * m, m)
            hid_ref[rows] = s
            s = normed(s, gain_ref[0:1])
            for z in range(nz):
                nin[z, rows] = s[:, z * BLK : (z + 1) * BLK]
        move(0).start()

    @pl.when(g < T)
    def _():
        part = []
        wide = jnp.concatenate([nin[z] for z in range(nz)], axis=1)
        for which in range(3):
            block = mm(wide, deep(w_ref, which)).astype(BF16)
            proj_ref[0, which] = block
            part.append(split_tokens(block, C))
        q, k, v = part
        p = token_weights(q, k, C)
        mixed = [v[0]]
        for a in range(1, C):
            total = rounded(p[a, 0]) * v[0]
            for b in range(1, a + 1):
                total += rounded(p[a, b]) * v[b]
            mixed.append(total)
        mixed = jnp.concatenate(mixed, axis=0).astype(BF16)
        mixes[g] = mixed
        for z in range(nz):
            hid_ref[:, z * BLK : (z + 1) * BLK] += mm(mixed, w_ref[z, 0, 3])

    @pl.when(g == T)
    def _():
        s = normed(hid_ref[...], gain_ref[1:2])
        for z in range(nz):
            nmid[z] = s[:, z * BLK : (z + 1) * BLK]
        move(1).start()

    @pl.when(g >= T)
    def _():
        part = None
        wide = jnp.concatenate([nmid[z] for z in range(nz)], axis=1)
        for j in range(4):
            act, slope = gelu_pair(mm(wide, deep(w_ref, j)))
            gpre = (gact_ref[0, j].astype(F32) * slope).astype(BF16)
            acts[g - T, j] = act.astype(BF16)
            pres[g - T, j] = gpre
            piece = mm_t(gpre, deep(w_ref, j))
            part = piece if part is None else part + piece
        acc[...] = part + jnp.where(g == T, 0.0, acc[...])

    store_out(g, 0, mixes, sems.at[0], to_m)
    store_out(g, T, acts, sems.at[1], to_a)
    store_out(g, T, pres, sems.at[2], to_p)

    @pl.when(g == 2 * T - 1)
    def _():
        back, gg = norm_back(hid_ref[...], gain_ref[1:2], acc[...])
        gg_ref[...] = gg
        ghid = cot_ref[...].astype(F32) + back
        ghid_ref[...] = ghid
        for z in range(nz):
            branch[z] = ghid[:, z * BLK : (z + 1) * BLK].astype(BF16)
        move(2).start()
        stored(mixes, sems.at[0], to_m)
        stored(acts, sems.at[1], to_a)
        stored(pres, sems.at[2], to_p)
        for i in range(3):
            move(i).wait()


OWN_BLOCKS, BUNDLE = 14, 26


def kept(shape, first, half):
    return pl.BlockSpec(
        (1,) + shape, lambda g, order: (clip(g - first, 0, half - 1) * order[ACTIVE],) + (0,) * len(shape)
    )


def codes_fwd(order, codes, sent, cot, gact, W, gain):
    C, m, D = codes.shape
    rows = C * m
    nz, T = W.shape[:2]
    act = struct((4, rows, BLK), BF16)
    wide = pltpu.VMEM((nz, rows, BLK), BF16)
    return call(
        codes_fwd_body,
        order,
        (codes, sent, cot, gact, W, gain),
        [
            whole(codes.shape),
            whole(sent.shape),
            whole(cot.shape),
            kept((4, rows, BLK), T, T),
            weight_spec(W, lambda g: (g % T, g // T)),
            whole(gain.shape),
        ],
        (
            struct((T, 3, rows, BLK), BF16),
            struct((rows, D), F32),
            struct((rows, D), F32),
            struct((1, D), F32),
            struct((OWN_BLOCKS, rows, BLK), BF16),
            act,
            act,
            struct((BUNDLE, rows, BLK), BF16),
        ),
        (
            kept((3, rows, BLK), 0, T),
            whole((rows, D)),
            whole((rows, D)),
            whole((1, D)),
            *[HBM_REF] * 4,
        ),
        2 * T,
        (
            wide,
            wide,
            wide,
            pltpu.VMEM((rows, D), F32),
            pltpu.VMEM((T, 4, rows, BLK), BF16),
            pltpu.VMEM((T, 4, rows, BLK), BF16),
            pltpu.VMEM((T, rows, BLK), BF16),
            pltpu.SemaphoreType.DMA((4, T)),
        ),
        flops=2 * rows * D * 12 * D,
        moved=16 * D * D + rows * D * 40,
    )


def codes_gact_body(order, cot_ref, wd_ref, gact_ref):
    for j in range(4):
        lanes = jnp.concatenate([wd_ref[z, 0, j] for z in range(wd_ref.shape[0])], axis=1)
        gact_ref[0, j] = mm_t(cot_ref[...], lanes).astype(BF16)


def codes_gact(order, cot, W):
    rows, D = cot.shape
    T = W.shape[1]
    return call(
        codes_gact_body,
        order,
        (cot, W),
        [whole(cot.shape), weight_spec(W, lambda g: (g, 2))],
        struct((T, 4, rows, BLK), BF16),
        pl.BlockSpec((1, 4, rows, BLK), lambda g, order: (g * order[ACTIVE], 0, 0, 0)),
        T,
        flops=2 * rows * D * 4 * D,
        moved=8 * D * D + rows * D * 10,
    )


def codes_back_body(order, proj_ref, w_ref, codes_ref, sent_ref, ghid_ref, gain_ref, keep_ref, send_ref, glocal_ref, gsent_ref, gg_ref, acc, held, branch, sems):
    g = pl.program_id(0)
    C, m, _ = codes_ref.shape
    T = pl.num_programs(0)

    @pl.when(g == 0)
    def _():
        branch[...] = ghid_ref[...].astype(BF16)

    nz = w_ref.shape[0]
    lanes = jnp.concatenate([w_ref[z, 0, 3] for z in range(nz)], axis=1)
    gmix = mm_t(branch[...], lanes)
    gm = split_tokens(gmix.astype(BF16), C)
    q, k, v = (split_tokens(proj_ref[0, i], C) for i in range(3))
    p = token_weights(q, k, C)
    ga = pair_sums(gm, v, C)

    def add(left, right):
        return right if left is None else left + right

    gq, gk, gv = [jnp.zeros_like(q[0])], [None] * C, [gm[0]] + [None] * (C - 1)
    for a in range(1, C):
        centre = p[a, 0] * ga[a, 0]
        for b in range(1, a + 1):
            centre += p[a, b] * ga[a, b]
        total = None
        for b in range(a + 1):
            gs = rounded(SCALE * p[a, b] * (ga[a, b] - centre))
            total = add(total, gs * k[b])
            gk[b] = add(gk[b], gs * q[a])
            gv[b] = add(gv[b], rounded(p[a, b]) * gm[a])
        gq.append(total)
    joined = [jnp.concatenate(part, axis=0).astype(BF16) for part in (gq, gk, gv)]

    for which in range(3):
        held[g, which] = joined[which]
    part = None
    for which in range(3):
        part = add(part, mm_t(joined[which], deep(w_ref, which)))
    acc[...] = part + jnp.where(g == 0, 0.0, acc[...])
    outs = [keep_ref.at[0], keep_ref.at[1], send_ref.at[0], send_ref.at[1]]
    store_out(g, 0, held, sems, outs)

    @pl.when(g == T - 1)
    def _():
        total = None
        gains = None
        for c in range(C):
            rows = slice(c * m, (c + 1) * m)
            s = codes_ref[c].astype(F32) + sent_ref[...].astype(F32)
            back, gg = norm_back(s, gain_ref[0:1], acc[rows])
            gains = add(gains, gg)
            local = (ghid_ref[rows] + back).astype(BF16)
            glocal_ref[c] = local
            total = add(total, local.astype(F32))
        gsent_ref[...] = total.astype(BF16)
        gg_ref[...] = gains
        stored(held, sems, outs)


def codes_back(order, proj, W, codes, sent, ghid, gain):
    rows, D = ghid.shape
    C, m, _ = codes.shape
    T = W.shape[1]
    half = T // 2
    blocks = struct((half, 3, rows, BLK), BF16)
    return call(
        codes_back_body,
        order,
        (proj, W, codes, sent, ghid, gain),
        [
            pl.BlockSpec((1, 3, rows, BLK), lambda g, order: (g * order[ACTIVE], 0, 0, 0)),
            weight_spec(W, lambda g: (g, 0)),
            whole(codes.shape),
            whole(sent.shape),
            whole(ghid.shape),
            whole(gain.shape),
        ],
        (blocks, blocks, struct(codes.shape, BF16), struct((m, D), BF16), struct((1, D), F32)),
        (
            HBM_REF,
            HBM_REF,
            whole(codes.shape),
            whole((m, D)),
            whole((1, D)),
        ),
        T,
        (
            pltpu.VMEM((rows, D), F32),
            pltpu.VMEM((T, 3, rows, BLK), BF16),
            pltpu.VMEM((rows, D), BF16),
            pltpu.SemaphoreType.DMA((T,)),
        ),
        flops=2 * rows * D * 4 * D,
        moved=8 * D * D + rows * D * 20,
    )


def codes_out_body(order, hid_ref, a0_ref, a1_ref, a2_ref, a3_ref, wd_ref, out_ref, acc):
    g = pl.program_id(0)
    T = pl.num_programs(0)
    C, m, _ = out_ref.shape

    @pl.when(g == 0)
    def _():
        acc[...] = hid_ref[...]

    for i, act_ref in enumerate((a0_ref, a1_ref, a2_ref, a3_ref)):

        @pl.when(g == i)
        def _():
            act = jnp.concatenate([act_ref[j] for j in range(4)], axis=1)
            for z in range(wd_ref.shape[0]):
                acc[:, z * BLK : (z + 1) * BLK] += mm(act, wd_ref[z, 0].reshape(-1, BLK))

    @pl.when(g == T - 1)
    def _():
        for c in range(C):
            out_ref[c] = acc[c * m : (c + 1) * m].astype(BF16)


def codes_out(order, hid, acts, W, C):
    rows, D = hid.shape
    T = W.shape[1]
    m = rows // C
    return call(
        codes_out_body,
        order,
        (hid, *acts, W),
        [
            whole(hid.shape),
            *[pl.BlockSpec((4, rows, BLK), lambda g, order: (0, 0, 0))] * 4,
            weight_spec(W, lambda g: (g, 2)),
        ],
        struct((C, m, D), BF16),
        whole((C, m, D)),
        T,
        (pltpu.VMEM((rows, D), F32),),
        flops=2 * rows * D * 4 * D,
        moved=8 * D * D + rows * D * 14,
    )


def put(ref, value, by_rows):
    for z in range(ref.shape[0]):
        at = slice(z * BLK, (z + 1) * BLK)
        ref[z, 0] = (value[at] if by_rows else value[:, at]).astype(BF16)


def got(ref, by_rows):
    parts = [ref[z, 0].astype(F32) for z in range(ref.shape[0])]
    return jnp.concatenate(parts, axis=0 if by_rows else 1)


def grads_body(parts, has_got, flag, *refs):
    g = pl.program_id(0)
    slots = sum(part[0] and max(part[3], part[4]) for part in parts)
    out_ref = refs[len(refs) - 1 - slots]
    turned = refs[len(refs) - slots :]
    got_ref = refs[len(refs) - 2 - slots]
    at = 0
    for by_rows, begin, end, ones, zeros in parts:
        for value, count in ((1, ones), (0, zeros)):
            pairs = [(refs[at + 2 * i], refs[at + 2 * i + 1]) for i in range(count)]
            at += 2 * count
            if not count:
                continue

            def full(wide):
                if len(wide.shape) == 3:
                    return jnp.concatenate([wide[z] for z in range(wide.shape[0])], axis=1)
                return wide[...]

            if by_rows:

                @pl.when((flag[0] == value) & (g == begin))
                def _():
                    for (wide, _), turn in zip(pairs, turned):
                        turn[:, : wide.shape[-2]] = full(wide).T

            @pl.when((flag[0] == value) & (g >= begin) & (g < end))
            def _():
                total = None
                for i, (wide, narrow) in enumerate(pairs):
                    if by_rows:
                        piece = mm(turned[i][:, : wide.shape[-2]], narrow[0])
                    else:
                        piece = inner(narrow[0], full(wide))
                    total = piece if total is None else total + piece
                if has_got and value == 0:
                    total = total + got(got_ref, by_rows)
                put(out_ref, total, by_rows)


def grads(flag, nz, parts, received=None):
    inputs, specs, plan = [], [], []
    begin = 0
    for by_rows, count, ones, zeros in parts:
        for wide, narrow, base, *more in ones + zeros:
            if isinstance(wide, tuple):
                wide, at = wide
                rows = wide.shape[1]
                specs.append(
                    pl.BlockSpec((nz, rows, BLK), lambda g, f, a=at // nz: (a, 0, 0))
                )
            else:
                rows = wide.shape[0]
                specs.append(whole(wide.shape))
            specs.append(
                pl.BlockSpec(
                    (1, rows, BLK),
                    lambda g, f, s=begin, b=base, c=count, m=sum(more): (
                        b + clip(g - s, 0, c - 1),
                        m,
                        0,
                    ),
                )
            )
            inputs += [wide, narrow]
        plan.append((by_rows, begin, begin + count, len(ones), len(zeros)))
        begin += count
    turns = []
    for by_rows, _, ones, zeros in parts:
        if by_rows:
            rows = [[p[1].shape[1] for p in side] for side in (ones, zeros)]
            for i in range(max(len(side) for side in rows)):
                longest = max(side[i] for side in rows if len(side) > i)
                turns.append(pltpu.VMEM((nz * BLK, longest), BF16))
    block = pl.BlockSpec((nz, 1, BLK, BLK), lambda g, f: (0, g, 0, 0))
    if received is not None:
        inputs.append(received)
        specs.append(block)
    return call(
        functools.partial(grads_body, plan, received is not None),
        flag,
        inputs,
        specs,
        struct((nz, begin, BLK, BLK), BF16),
        block,
        begin,
        turns,
        flops=COST * (LONG if received is not None else 10**9),
    )


def swap(value, axis, bit):
    count = lax.axis_size(axis)
    return lax.ppermute(value, axis, [(i, i ^ bit) for i in range(count)])


def swap_in(value, section, bit):
    count = lax.axis_size("tensor")
    pairs = [(section * count + i, section * count + (i ^ bit)) for i in range(count)]
    return lax.ppermute(value, ("section", "tensor"), pairs)


def together(*values):
    return lax.optimization_barrier(values)


def after(value, *others):
    return together(value, *others)[0]


def pack_body(qkv_ref, out_ref, up_ref, down_ref, flat_ref):
    flat_ref[0:3] = qkv_ref[...]
    flat_ref[3] = out_ref[...]
    for j in range(4):
        flat_ref[4 + j] = up_ref[:, j * BLK : (j + 1) * BLK]
    flat_ref[8:12] = down_ref[...]


def gather_weights(w_qkv, w_out, w_up, w_down):
    depth = w_qkv.shape[1]
    shards = lax.axis_size("dp")
    slices = lax.axis_size("tensor")
    both = ("dp", "tensor")
    if depth == BLK:
        flat = pl.pallas_call(
            pack_body,
            out_shape=struct((12, BLK, BLK), BF16),
        )(w_qkv, w_out, w_up, w_down.reshape(-1, BLK, BLK))
        out = lax.all_gather(flat, both)
        return out.reshape(shards, slices, *flat.shape)
    per = BLK // depth
    nz = shards // per

    def by_rows(value):
        out = lax.all_gather(value, both).reshape(nz, per, slices, value.shape[0], depth, BLK)
        return out.transpose(0, 2, 3, 1, 4, 5).reshape(nz, slices, -1, BLK, BLK)

    def by_cols(value):
        out = lax.all_gather(value, both)
        out = out.reshape(nz, per, slices, value.shape[0] // BLK, BLK, depth)
        return out.transpose(0, 2, 3, 4, 1, 5).reshape(nz, slices, -1, BLK, BLK)

    up_blocks = w_up.reshape(depth, -1, BLK).transpose(1, 0, 2)
    return jnp.concatenate(
        [by_rows(w_qkv), by_cols(w_out), by_rows(up_blocks), by_cols(w_down)], axis=2
    )


def scatter_blocks(parts, split):
    shards = lax.axis_size("dp")
    nz, count = parts.shape[:2]
    per = shards // nz
    if per == 1:
        out = lax.psum_scatter(parts, "dp", scatter_dimension=0, tiled=False)
        return out[:split], out[split:]
    depth = BLK // per
    rows = parts[:, :split].reshape(nz, split, per, depth, BLK)
    rows = rows.transpose(0, 2, 1, 3, 4).reshape(shards, -1, BLK)
    columns = parts[:, split:].reshape(nz, count - split, BLK, per, depth)
    columns = columns.transpose(0, 3, 1, 2, 4).reshape(shards, -1, BLK)
    out = lax.psum_scatter(
        jnp.concatenate([rows, columns], axis=1), "dp", scatter_dimension=0, tiled=False
    )
    cut = split * depth
    return out[:cut].reshape(split, depth, BLK), out[cut:].reshape(-1, BLK, depth)


def on_device(codes, cotangent, doc_lengths, w_qkv, w_out, w_up, w_down, gains):
    is_first = lax.axis_index("section") == 0
    flag = is_first.astype(jnp.int32).reshape(1)
    t = lax.axis_index("tensor")
    T = lax.axis_size("tensor")
    R, F, C, D = codes.shape
    M = R * F
    N = T * F
    gain = gains[0]
    W = gather_weights(w_qkv[0], w_out[0], w_up[0], w_down[0])
    nz = W.shape[0]
    slices = t ^ jnp.array([0, 2, 1, 3], jnp.int32)
    order0 = jnp.concatenate([slices, flag])
    order1 = jnp.concatenate([slices, 1 - flag])
    codes_t = codes.transpose(2, 0, 1, 3).reshape(C, M, D)
    cot = cotangent.transpose(2, 0, 1, 3).reshape(C * M, D)

    frame_own = jnp.sum(codes_t.astype(F32), axis=0)
    far = swap(frame_own, "tensor", 2)
    s0 = jnp.concatenate(
        [frame_own, swap(frame_own, "tensor", 1), far, swap(far, "tensor", 1)], axis=0
    )
    spot = t ^ lax.iota(jnp.int32, T)
    pos = (spot[:, None] * F + lax.iota(jnp.int32, F)[None]).reshape(N)
    ends = jnp.cumsum(doc_lengths, axis=1)
    seg = jnp.sum((pos[None, :, None] >= ends[:, None, :]).astype(jnp.int32), axis=2)
    allowed = (pos[:, None] >= pos[None, :])[None] & (seg[:, :, None] == seg[:, None, :])
    bias = jnp.where(allowed, 0.0, NEG).astype(F32)

    out0 = frames_own(order0, s0, W, gain, bias, F)
    sent = lax.ppermute(out0, "section", [(0, 1)])
    s0 = after(s0, out0)
    n_in0, proj0, mixed0, hid0, n_mid0, act0, slope0 = frames_fwd(order0, s0, W, gain, bias, F)

    def swap1(value, bit):
        return swap_in(value, 1, bit)

    gact1 = codes_gact(order1, cot, W)
    cot_y = swap1(after(cot, out0), 2)
    cot_s = swap1(after(cot, out0), 1)
    sent, gact1, cot_y, cot_s, proj0 = together(sent, gact1, cot_y, cot_s, proj0)
    proj1, hid1, ghid1, gg_mid1, own1, act_far, act_other, bundle = codes_fwd(
        order1, codes_t, sent, cot, gact1, W, gain
    )
    act_y = swap1(act_far, 2)
    act_o = swap1(act_other, 1)
    bundle_s = swap1(bundle, 1)
    gproj1, gproj1_s, glocal, gsent, gg_in1 = codes_back(
        order1, proj1, W, codes_t, sent, ghid1, gain
    )

    gproj1, gproj1_s, glocal, gsent, gg_in1, act_y, act_o, bundle_s = together(
        gproj1, gproj1_s, glocal, gsent, gg_in1, act_y, act_o, bundle_s
    )

    gsent = lax.ppermute(gsent, "section", [(1, 0)])
    act_d = swap1(act_o, 2)
    cot_d = swap1(after(cot_y, act_o), 1)

    M1 = C * M
    gproj1 = gproj1.reshape(-1, M1, BLK)
    up_far = grads(
        flag, nz, [(True, 4, [], [((bundle, 16), own1, 8), ((bundle_s, 16), bundle_s, 8)])]
    )
    up_got = swap1(up_far, 2)
    gsent, _, act_d, cot_d = together(gsent, up_far, act_d, cot_d)
    gfar = swap_in(gsent, 0, 2)
    gy0 = jnp.concatenate(
        [gsent, swap_in(gsent, 0, 1), gfar, swap_in(gfar, 0, 1)], axis=0
    )

    down_total = grads(
        flag,
        nz,
        [
            (
                False,
                4,
                [(gy0, act0, 0)],
                [(cot, own1, 0), (cot_s, bundle_s, 0), (cot_y, act_y, 0), (cot_d, act_d, 0)],
            )
        ],
    )
    down_part = scatter_blocks(down_total, 0)[1]
    hid0 = after(hid0, down_total)
    gpre0, branch0, gproj0, frame, gg0 = frames_bwd(
        order0, gy0, hid0, slope0, W, gain, proj0, bias, frame_own, F
    )
    gproj1, gproj1_s = together(gproj1, gproj1_s, down_total)[:2]
    gproj1_s = swap1(gproj1_s, 1).reshape(-1, M1, BLK)
    att_far = grads(
        flag,
        nz,
        [
            (True, 3, [], [((bundle, 12), gproj1, 3), ((bundle_s, 12), gproj1_s, 3)]),
            (False, 1, [], [((bundle, 20), own1, 13), ((bundle_s, 20), bundle_s, 25)]),
        ],
    )
    att_got = swap1(att_far, 2)
    hid1, glocal = together(hid1, glocal, att_far)[:2]
    glocal = lax.ppermute(glocal, "section", [(1, 0)])
    out1 = codes_out(order1, hid1, [own1, act_far, bundle, act_other], W, C)
    up_total = grads(
        flag,
        nz,
        [
            (
                True,
                4,
                [(n_mid0, gpre0, 0)],
                [((bundle, 16), own1, 4), ((bundle_s, 16), bundle_s, 4)],
            )
        ],
        up_got,
    )
    up_part = scatter_blocks(up_total, 4)[0]
    gproj0, out1 = together(gproj0, out1, up_total, glocal)[:2]
    att_total = grads(
        flag,
        nz,
        [
            (
                True,
                3,
                [(n_in0, gproj0, 0)],
                [((bundle, 12), gproj1, 0), ((bundle_s, 12), gproj1_s, 0)],
            ),
            (
                False,
                1,
                [(branch0, mixed0[None], 0)],
                [((bundle, 20), own1, 12), ((bundle_s, 20), bundle_s, 24)],
            ),
        ],
        att_got,
    )
    qkv_part, out_part = scatter_blocks(att_total, 3)
    gain_part = jnp.where(is_first, gg0, jnp.concatenate([gg_in1, gg_mid1], axis=0))
    grad_gains = lax.psum(after(gain_part, att_total), ("dp", "tensor"))

    code_grad = (glocal.astype(F32) + frame[None]).astype(BF16)
    result = jnp.where(is_first, code_grad, out1).reshape(C, R, F, D).transpose(1, 2, 0, 3)
    depth = w_up.shape[1]
    return (
        result[None],
        qkv_part.astype(F32)[None],
        out_part.reshape(-1, depth).astype(F32)[None],
        up_part.transpose(1, 0, 2).reshape(depth, -1).astype(F32)[None],
        down_part.reshape(-1, depth).astype(F32)[None],
        grad_gains[None],
    )


def solution(mesh):
    placed = (
        P("dp", "tensor", None, None),
        P("dp", "tensor", None, None),
        P("dp", None),
        P("section", None, "dp", "tensor"),
        P("section", "tensor", "dp"),
        P("section", "dp", "tensor"),
        P("section", "tensor", "dp"),
        P("section", None, None),
    )
    return jax.shard_map(
        on_device,
        mesh=mesh,
        in_specs=placed,
        out_specs=(
            P("section", "dp", "tensor", None, None),
            P("section", None, "dp", "tensor"),
            P("section", "tensor", "dp"),
            P("section", "dp", "tensor"),
            P("section", "tensor", "dp"),
            P("section", None, None),
        ),
        check_vma=False,
    )
```

```python
import functools

import jax
import jax.numpy as jnp
from jax import lax
from jax.experimental import pallas as pl
from jax.experimental.pallas import tpu as pltpu
from jax.sharding import PartitionSpec as P

HEAD_DIM = 64
BLK = 256
HEADS = BLK // HEAD_DIM
EPS = 1e-05
NEG = -1e30
SCALE = 0.125
F32 = jnp.float32
BF16 = jnp.bfloat16
VMEM = 60 * 1024 * 1024
ACTIVE = 4
COST = 8
LONG = 10**11


def mm(left, right):
    return jnp.dot(left, right, preferred_element_type=F32)


def mm_t(left, right):
    return lax.dot_general(left, right, (((1,), (1,)), ((), ())), preferred_element_type=F32)


def inner(left, right):
    return lax.dot_general(left, right, (((0,), (0,)), ((), ())), preferred_element_type=F32)


def unit_of(values):
    inv_root = lax.rsqrt(jnp.mean(values * values, axis=-1, keepdims=True) + EPS)
    return values * inv_root, inv_root


def normed(values, gain):
    return (unit_of(values)[0] * gain).astype(BF16)


def norm_back(values, gain, grad):
    unit_rows, inv_root = unit_of(values)
    scaled = grad * gain
    back = inv_root * (scaled - unit_rows * jnp.mean(unit_rows * scaled, axis=-1, keepdims=True))
    return back, jnp.sum(grad * unit_rows, axis=0, keepdims=True)


def gelu_pair(pre):
    square = pre * pre
    th = jnp.tanh(0.7978845608028654 * pre * (1.0 + 0.044715 * square))
    half = 0.5 + 0.5 * th
    act = pre * half
    slope = half + act * (1.0 - th) * (0.7978845608028654 + 3 * 0.044715 * 0.7978845608028654 * square)
    return act, slope


def head_masks(shape):
    lane = lax.broadcasted_iota(jnp.int32, shape, 1) // HEAD_DIM
    return [lane == h for h in range(HEADS)]


def spread(value, masks):
    zero = jnp.zeros_like(value)
    return jnp.concatenate([jnp.where(m, value, zero) for m in masks], axis=0)


def gathered(value, masks):
    n = value.shape[0] // HEADS
    out = jnp.where(masks[0], value[:n], 0.0)
    for h in range(1, HEADS):
        out = jnp.where(masks[h], value[h * n : (h + 1) * n], out)
    return out


def head_weights(q4, k, bias):
    s = mm_t(q4, k) * SCALE + jnp.concatenate([bias] * HEADS, axis=0)
    e = jnp.exp(s - jnp.max(s, axis=-1, keepdims=True))
    return e / jnp.sum(e, axis=-1, keepdims=True)


def whole(shape):
    return pl.BlockSpec(shape, lambda g, order: (0,) * len(shape))


def struct(shape, dtype):
    return jax.ShapeDtypeStruct(shape, dtype)


def call(body, order, inputs, in_specs, outs, out_specs, grid, scratch=(), flops=0, moved=0):
    def run(flags, *refs):
        if flags.shape[0] <= ACTIVE:
            return body(flags, *refs)

        @pl.when(flags[ACTIVE] == 1)
        def _():
            body(flags, *refs)

    return pl.pallas_call(
        run,
        out_shape=outs,
        grid_spec=pltpu.PrefetchScalarGridSpec(
            num_scalar_prefetch=1,
            grid=(grid,),
            in_specs=in_specs,
            out_specs=out_specs,
            scratch_shapes=scratch,
        ),
        compiler_params=pltpu.CompilerParams(
            dimension_semantics=("arbitrary",), vmem_limit_bytes=VMEM
        ),
        cost_estimate=pl.CostEstimate(
            flops=flops // COST, bytes_accessed=moved // COST, transcendentals=0
        ),
    )(order, *inputs)


def weight_spec(W, third):
    nz = W.shape[0]

    def at(g, order):
        step, which = third(g)
        return (0, order[step] * order[ACTIVE], which * order[ACTIVE], 0, 0)

    return pl.BlockSpec((nz, 1, 4, BLK, BLK), at)


def clip(g, low, high):
    return jnp.minimum(jnp.maximum(g, low), high)


def deep(ref, index):
    return ref[:, 0, index].reshape(-1, BLK)


def store_out(g, first, held, sems, outs):
    for i, out in enumerate(outs):

        @pl.when(g == first + i)
        def _():
            pltpu.make_async_copy(held.at[i], out, sems.at[i]).start()


def stored(held, sems, outs):
    for i, out in enumerate(outs):
        pltpu.make_async_copy(held.at[i], out, sems.at[i]).wait()


HBM_REF = pl.BlockSpec(memory_space=pl.ANY)


def pick(ref, r, R, F):
    return jnp.concatenate(
        [ref[pl.ds(at, F)] for at in range(r * F, ref.shape[0], R * F)], axis=0
    )


def place(ref, r, R, F, value):
    for i, at in enumerate(range(r * F, ref.shape[0], R * F)):
        ref[pl.ds(at, F)] = value[i * F : (i + 1) * F]


def frames_fwd_body(own, order, s_ref, nin_ref, wa_ref, gain_ref, bias_ref, proj_ref, mixed_ref, hid_ref, nmid_ref, act_ref, slope_ref, held, acts, sems):
    g = pl.program_id(0)
    T = pl.num_programs(0) // 2
    R, N = bias_ref.shape[:2]
    nz = wa_ref.shape[0]

    @pl.when(g == 0)
    def _():
        hid_ref[...] = s_ref[...]

    @pl.when(g < T)
    def _():
        for which in range(3):
            proj_ref[0, which] = mm(nin_ref[...], deep(wa_ref, which)).astype(BF16)
        masks = head_masks((N, BLK))
        for r in range(R):
            q, k, v = (pick(proj_ref.at[0, i], r, R, own) for i in range(3))
            p = head_weights(spread(q, masks), k, bias_ref[r])
            place(held, r, R, own, gathered(mm(p.astype(BF16), v), masks).astype(BF16))
        for z in range(nz):
            hid_ref[:, z * BLK : (z + 1) * BLK] += mm(held[...], wa_ref[z, 0, 3])

    @pl.when(g == 0)
    def _():
        mixed_ref[...] = held[...]

    @pl.when(g == T)
    def _():
        nmid_ref[...] = normed(hid_ref[...], gain_ref[1:2])

    @pl.when(g >= T)
    def _():
        for j in range(4):
            act, slope = gelu_pair(mm(nmid_ref[...], deep(wa_ref, j)))
            slope_ref[0, j] = slope.astype(BF16)
            acts[jnp.minimum(g - T, 1), j] = act.astype(BF16)

    store_out(g, T, acts, sems, [act_ref])

    @pl.when(g == 2 * T - 1)
    def _():
        stored(acts, sems, [act_ref])


def frames_fwd(order, s, nin, W, gain, bias, own):
    rows, D = s.shape
    T = W.shape[1]
    return call(
        functools.partial(frames_fwd_body, own),
        order,
        (s, nin, W, gain, bias),
        [
            whole(s.shape),
            whole(nin.shape),
            weight_spec(W, lambda g: (g % T, g // T)),
            whole(gain.shape),
            whole(bias.shape),
        ],
        (
            struct((T, 3, rows, BLK), BF16),
            struct((rows, BLK), BF16),
            struct((rows, D), F32),
            struct((rows, D), BF16),
            struct((4, rows, BLK), BF16),
            struct((T, 4, rows, BLK), BF16),
        ),
        (
            pl.BlockSpec((1, 3, rows, BLK), lambda g, order: (jnp.minimum(g, T - 1) * order[ACTIVE], 0, 0, 0)),
            whole((rows, BLK)),
            whole((rows, D)),
            whole((rows, D)),
            HBM_REF,
            pl.BlockSpec((1, 4, rows, BLK), lambda g, order: (jnp.maximum(g - T, 0) * order[ACTIVE], 0, 0, 0)),
        ),
        2 * T,
        (
            pltpu.VMEM((rows, BLK), BF16),
            pltpu.VMEM((2, 4, rows, BLK), BF16),
            pltpu.SemaphoreType.DMA((1,)),
        ),
        flops=2 * rows * D * 10 * D,
        moved=24 * D * D + rows * D * 30,
    )


def frames_own_body(own, order, s_ref, nin, wa_ref, wb_ref, gain_ref, bias_ref, out_ref, keys, values, held, hid, nmid):
    g = pl.program_id(0)
    T = pl.num_programs(0) // 2
    R, N = bias_ref.shape[:2]
    nz = wa_ref.shape[0]
    mine = R * own

    @pl.when(g == 0)
    def _():
        hid[...] = s_ref[...]

    @pl.when(g < T)
    def _():
        queries = mm(nin[:mine], deep(wa_ref, 0)).astype(BF16)
        keys[...] = mm(nin[...], deep(wa_ref, 1)).astype(BF16)
        values[...] = mm(nin[...], deep(wa_ref, 2)).astype(BF16)
        masks = head_masks((own, BLK))
        for r in range(R):
            q4 = spread(queries[r * own : (r + 1) * own], masks)
            p = head_weights(q4, pick(keys, r, R, own), bias_ref[r, :own])
            mixed = gathered(mm(p.astype(BF16), pick(values, r, R, own)), masks)
            held[r * own : (r + 1) * own] = mixed.astype(BF16)
        for z in range(nz):
            hid[:, z * BLK : (z + 1) * BLK] += mm(held[...], wa_ref[z, 0, 3])

    @pl.when(g == T)
    def _():
        nmid[...] = normed(hid[...], gain_ref[1:2])

    @pl.when(g >= T)
    def _():
        act = [gelu_pair(mm(nmid[...], deep(wa_ref, j)))[0].astype(BF16) for j in range(4)]
        act = jnp.concatenate(act, axis=1)
        for z in range(nz):
            hid[:, z * BLK : (z + 1) * BLK] += mm(act, wb_ref[z, 0].reshape(-1, BLK))

    @pl.when(g == 2 * T - 1)
    def _():
        out_ref[...] = hid[...].astype(BF16)


def frames_own(order, s, nin, W, gain, bias, own):
    rows, D = nin.shape
    T = W.shape[1]
    mine = bias.shape[0] * own
    return call(
        functools.partial(frames_own_body, own),
        order,
        (s, nin, W, W, gain, bias),
        [
            whole(s.shape),
            whole(nin.shape),
            weight_spec(W, lambda g: (g % T, g // T)),
            weight_spec(W, lambda g: (jnp.maximum(g - T, 0), 2)),
            whole(gain.shape),
            whole(bias.shape),
        ],
        struct((mine, D), BF16),
        whole((mine, D)),
        2 * T,
        (
            pltpu.VMEM((rows, BLK), BF16),
            pltpu.VMEM((rows, BLK), BF16),
            pltpu.VMEM((mine, BLK), BF16),
            pltpu.VMEM((mine, D), F32),
            pltpu.VMEM((mine, D), BF16),
        ),
        flops=2 * mine * D * 12 * D,
        moved=24 * D * D,
    )


def frames_bwd_body(own, order, gy_ref, hid_ref, slope_ref, wa_ref, wb_ref, gain_ref, proj_ref, bias_ref, s_ref, gpre_ref, branch_ref, gproj_ref, frame_ref, gg_ref, held, acc, acc_in, ghid, pres, gmix, sems, hid_at, s_at, bias_at):
    g = pl.program_id(0)
    late = [
        pltpu.make_async_copy(a, b, sems.at[1 + i])
        for i, (a, b) in enumerate([(hid_ref, hid_at), (s_ref, s_at), (bias_ref, bias_at)])
    ]
    T = pl.num_programs(0) // 2
    R, N = bias_ref.shape[:2]
    nz = wa_ref.shape[0]

    @pl.when(g == 0)
    def _():
        for copy in late:
            copy.start()

    @pl.when(g < T)
    def _():
        part = None
        for j in range(4):
            lanes = jnp.concatenate([wb_ref[z, 0, j] for z in range(nz)], axis=1)
            gpre = (mm_t(gy_ref[...], lanes) * slope_ref[0, j].astype(F32)).astype(BF16)

            pres[jnp.minimum(g, 1), j] = gpre
            piece = mm_t(gpre, deep(wa_ref, j))
            part = piece if part is None else part + piece
        acc[...] = part + jnp.where(g == 0, 0.0, acc[...])

    store_out(g, 0, pres, sems, [gpre_ref])

    @pl.when(g == T - 1)
    def _():
        for copy in late:
            copy.wait()
        back, _ = norm_back(hid_at[...], gain_ref[1:2], acc[...])
        branch_ref[...] = (gy_ref[...].astype(F32) + back).astype(BF16)
        back_own, gg = norm_back(hid_at[: R * own], gain_ref[1:2], acc[: R * own])
        gg_ref[1:2] = gg
        ghid[...] = gy_ref[: R * own].astype(F32) + back_own

    @pl.when(g >= T)
    def _():
        lanes = jnp.concatenate([wa_ref[z, 0, 3] for z in range(nz)], axis=1)
        gmix[...] = mm_t(branch_ref[...], lanes).astype(BF16)
        masks = head_masks((N, BLK))
        for r in range(R):
            q, k, v = (pick(proj_ref.at[0, i], r, R, own) for i in range(3))
            q4 = spread(q, masks)
            p = head_weights(q4, k, bias_at[r])
            gm4 = spread(pick(gmix, r, R, own), masks)
            ga = mm_t(gm4, v)
            gs = (SCALE * p * (ga - jnp.sum(p * ga, axis=-1, keepdims=True))).astype(BF16)
            place(held.at[0], r, R, own, gathered(mm(gs, k), masks).astype(BF16))
            place(held.at[1], r, R, own, inner(gs, q4).astype(BF16))
            place(held.at[2], r, R, own, inner(p.astype(BF16), gm4).astype(BF16))

        @pl.when(g == T)
        def _():
            gproj_ref[...] = held[...]

        part = None
        for which in range(3):
            piece = mm_t(held[which, : R * own], deep(wa_ref, which))
            part = piece if part is None else part + piece
        acc_in[...] = part + jnp.where(g == T, 0.0, acc_in[...])

    @pl.when(g == 2 * T - 1)
    def _():
        back, gg = norm_back(s_at[...], gain_ref[0:1], acc_in[...])
        gg_ref[0:1] = gg
        frame_ref[...] = ghid[...] + back
        stored(pres, sems, [gpre_ref])


def frames_bwd(order, gy, hid, slope, W, gain, proj, bias, s, own):
    rows, D = hid.shape
    T = W.shape[1]
    R = bias.shape[0]
    return call(
        functools.partial(frames_bwd_body, own),
        order,
        (gy, hid, slope, W, W, gain, proj, bias, s),
        [
            whole(gy.shape),
            HBM_REF,
            pl.BlockSpec((1, 4, rows, BLK), lambda g, order: (jnp.minimum(g, T - 1) * order[ACTIVE], 0, 0, 0)),
            weight_spec(W, lambda g: (g % T, 1 - g // T)),
            weight_spec(W, lambda g: (jnp.minimum(g, T - 1), 2)),
            whole(gain.shape),
            pl.BlockSpec((1, 3, rows, BLK), lambda g, order: (jnp.maximum(g - T, 0) * order[ACTIVE], 0, 0, 0)),
            HBM_REF,
            HBM_REF,
        ],
        (
            struct((4, rows, BLK), BF16),
            struct((rows, D), BF16),
            struct((3, rows, BLK), BF16),
            struct((R * own, D), F32),
            struct((2, D), F32),
        ),
        (
            HBM_REF,
            whole((rows, D)),
            whole((3, rows, BLK)),
            whole((R * own, D)),
            whole((2, D)),
        ),
        2 * T,
        (
            pltpu.VMEM((3, rows, BLK), BF16),
            pltpu.VMEM((rows, D), F32),
            pltpu.VMEM((R * own, D), F32),
            pltpu.VMEM((R * own, D), F32),
            pltpu.VMEM((2, 4, rows, BLK), BF16),
            pltpu.VMEM((rows, BLK), BF16),
            pltpu.SemaphoreType.DMA((4,)),
            pltpu.VMEM((rows, D), F32),
            pltpu.VMEM((R * own, D), F32),
            pltpu.VMEM(bias.shape, F32),
        ),
        flops=2 * rows * D * 14 * D,
        moved=24 * D * D + rows * D * 30,
    )


def head_sum(prods):
    row = lax.broadcasted_iota(jnp.int32, (BLK, BLK), 0) // HEAD_DIM
    col = lax.broadcasted_iota(jnp.int32, (BLK, BLK), 1) // HEAD_DIM
    ones = jnp.where(row == col, 1.0, 0.0).astype(BF16)
    high = prods.astype(BF16)
    low = (prods - high.astype(F32)).astype(BF16)
    return mm(high, ones) + mm(low, ones)


def token_pairs(count):
    return [(a, b) for a in range(1, count) for b in range(a + 1)]


def pair_sums(left, right, count):
    pairs = token_pairs(count)
    m = left[0].shape[0]
    sums = head_sum(jnp.concatenate([left[a] * right[b] for a, b in pairs], axis=0))
    return {pair: sums[i * m : (i + 1) * m] for i, pair in enumerate(pairs)}


def token_weights(q, k, count):
    s = pair_sums(q, k, count)
    out = {}
    for a in range(1, count):
        top = s[a, 0]
        for b in range(1, a + 1):
            top = jnp.maximum(top, s[a, b])
        e = [jnp.exp((s[a, b] - top) * SCALE) for b in range(a + 1)]
        total = e[0]
        for b in range(1, a + 1):
            total = total + e[b]
        share = 1.0 / total
        for b in range(a + 1):
            out[a, b] = e[b] * share
    return out


def rounded(value):
    return value.astype(BF16).astype(F32)


def split_tokens(value, count):
    m = value.shape[0] // count
    return [value[i * m : (i + 1) * m].astype(F32) for i in range(count)]


def codes_fwd_body(order, codes_ref, sent_ref, cot_ref, gact_ref, w_ref, gain_ref, proj_ref, hid_ref, ghid_ref, gg_ref, own_ref, far_ref, other_ref, bundle_ref, nin, nmid, branch, acc, acts, pres, mixes, sems):
    g = pl.program_id(0)
    T = pl.num_programs(0) // 2
    C, m, _ = codes_ref.shape
    nz = w_ref.shape[0]
    four = lambda ref, at: ref.at[pl.ds(at, 4)]
    to_a = [four(own_ref, 0), far_ref, four(bundle_ref, 0), other_ref]
    to_p = [four(own_ref, 4), four(own_ref, 8), four(bundle_ref, 4), four(bundle_ref, 8)]
    to_m = [own_ref.at[12], own_ref.at[13], bundle_ref.at[24], bundle_ref.at[25]]
    wides = [(nin, 12), (nmid, 16), (branch, 20)]

    def move(i):
        wide, at = wides[i]
        return pltpu.make_async_copy(wide, four(bundle_ref, at), sems.at[3, i])

    @pl.when(g == 0)
    def _():
        for c in range(C):
            s = codes_ref[c].astype(F32) + sent_ref[...].astype(F32)
            rows = pl.ds(c * m, m)
            hid_ref[rows] = s
            s = normed(s, gain_ref[0:1])
            for z in range(nz):
                nin[z, rows] = s[:, z * BLK : (z + 1) * BLK]
        move(0).start()

    @pl.when(g < T)
    def _():
        part = []
        wide = jnp.concatenate([nin[z] for z in range(nz)], axis=1)
        for which in range(3):
            block = mm(wide, deep(w_ref, which)).astype(BF16)
            proj_ref[0, which] = block
            part.append(split_tokens(block, C))
        q, k, v = part
        p = token_weights(q, k, C)
        mixed = [v[0]]
        for a in range(1, C):
            total = rounded(p[a, 0]) * v[0]
            for b in range(1, a + 1):
                total += rounded(p[a, b]) * v[b]
            mixed.append(total)
        mixed = jnp.concatenate(mixed, axis=0).astype(BF16)
        mixes[g] = mixed
        for z in range(nz):
            hid_ref[:, z * BLK : (z + 1) * BLK] += mm(mixed, w_ref[z, 0, 3])

    @pl.when(g == T)
    def _():
        s = normed(hid_ref[...], gain_ref[1:2])
        for z in range(nz):
            nmid[z] = s[:, z * BLK : (z + 1) * BLK]
        move(1).start()

    @pl.when(g >= T)
    def _():
        part = None
        wide = jnp.concatenate([nmid[z] for z in range(nz)], axis=1)
        for j in range(4):
            act, slope = gelu_pair(mm(wide, deep(w_ref, j)))
            gpre = (gact_ref[0, j].astype(F32) * slope).astype(BF16)
            acts[g - T, j] = act.astype(BF16)
            pres[g - T, j] = gpre
            piece = mm_t(gpre, deep(w_ref, j))
            part = piece if part is None else part + piece
        acc[...] = part + jnp.where(g == T, 0.0, acc[...])

    store_out(g, 0, mixes, sems.at[0], to_m)
    store_out(g, T, acts, sems.at[1], to_a)
    store_out(g, T, pres, sems.at[2], to_p)

    @pl.when(g == 2 * T - 1)
    def _():
        back, gg = norm_back(hid_ref[...], gain_ref[1:2], acc[...])
        gg_ref[...] = gg
        ghid = cot_ref[...].astype(F32) + back
        ghid_ref[...] = ghid
        for z in range(nz):
            branch[z] = ghid[:, z * BLK : (z + 1) * BLK].astype(BF16)
        move(2).start()
        stored(mixes, sems.at[0], to_m)
        stored(acts, sems.at[1], to_a)
        stored(pres, sems.at[2], to_p)
        for i in range(3):
            move(i).wait()


OWN_BLOCKS, BUNDLE = 14, 26


def kept(shape, first, half):
    return pl.BlockSpec(
        (1,) + shape, lambda g, order: (clip(g - first, 0, half - 1) * order[ACTIVE],) + (0,) * len(shape)
    )


def codes_fwd(order, codes, sent, cot, gact, W, gain):
    C, m, D = codes.shape
    rows = C * m
    nz, T = W.shape[:2]
    act = struct((4, rows, BLK), BF16)
    wide = pltpu.VMEM((nz, rows, BLK), BF16)
    return call(
        codes_fwd_body,
        order,
        (codes, sent, cot, gact, W, gain),
        [
            whole(codes.shape),
            whole(sent.shape),
            whole(cot.shape),
            kept((4, rows, BLK), T, T),
            weight_spec(W, lambda g: (g % T, g // T)),
            whole(gain.shape),
        ],
        (
            struct((T, 3, rows, BLK), BF16),
            struct((rows, D), F32),
            struct((rows, D), F32),
            struct((1, D), F32),
            struct((OWN_BLOCKS, rows, BLK), BF16),
            act,
            act,
            struct((BUNDLE, rows, BLK), BF16),
        ),
        (
            kept((3, rows, BLK), 0, T),
            whole((rows, D)),
            whole((rows, D)),
            whole((1, D)),
            *[HBM_REF] * 4,
        ),
        2 * T,
        (
            wide,
            wide,
            wide,
            pltpu.VMEM((rows, D), F32),
            pltpu.VMEM((T, 4, rows, BLK), BF16),
            pltpu.VMEM((T, 4, rows, BLK), BF16),
            pltpu.VMEM((T, rows, BLK), BF16),
            pltpu.SemaphoreType.DMA((4, T)),
        ),
        flops=2 * rows * D * 12 * D,
        moved=16 * D * D + rows * D * 40,
    )


def codes_gact_body(order, cot_ref, wd_ref, gact_ref):
    for j in range(4):
        lanes = jnp.concatenate([wd_ref[z, 0, j] for z in range(wd_ref.shape[0])], axis=1)
        gact_ref[0, j] = mm_t(cot_ref[...], lanes).astype(BF16)


def codes_gact(order, cot, W):
    rows, D = cot.shape
    T = W.shape[1]
    return call(
        codes_gact_body,
        order,
        (cot, W),
        [whole(cot.shape), weight_spec(W, lambda g: (g, 2))],
        struct((T, 4, rows, BLK), BF16),
        pl.BlockSpec((1, 4, rows, BLK), lambda g, order: (g * order[ACTIVE], 0, 0, 0)),
        T,
        flops=2 * rows * D * 4 * D,
        moved=8 * D * D + rows * D * 10,
    )


def codes_back_body(order, proj_ref, w_ref, codes_ref, sent_ref, ghid_ref, gain_ref, keep_ref, send_ref, glocal_ref, gsent_ref, gg_ref, acc, held, branch, sems):
    g = pl.program_id(0)
    C, m, _ = codes_ref.shape
    T = pl.num_programs(0)

    @pl.when(g == 0)
    def _():
        branch[...] = ghid_ref[...].astype(BF16)

    nz = w_ref.shape[0]
    lanes = jnp.concatenate([w_ref[z, 0, 3] for z in range(nz)], axis=1)
    gmix = mm_t(branch[...], lanes)
    gm = split_tokens(gmix.astype(BF16), C)
    q, k, v = (split_tokens(proj_ref[0, i], C) for i in range(3))
    p = token_weights(q, k, C)
    ga = pair_sums(gm, v, C)

    def add(left, right):
        return right if left is None else left + right

    gq, gk, gv = [jnp.zeros_like(q[0])], [None] * C, [gm[0]] + [None] * (C - 1)
    for a in range(1, C):
        centre = p[a, 0] * ga[a, 0]
        for b in range(1, a + 1):
            centre += p[a, b] * ga[a, b]
        total = None
        for b in range(a + 1):
            gs = rounded(SCALE * p[a, b] * (ga[a, b] - centre))
            total = add(total, gs * k[b])
            gk[b] = add(gk[b], gs * q[a])
            gv[b] = add(gv[b], rounded(p[a, b]) * gm[a])
        gq.append(total)
    joined = [jnp.concatenate(part, axis=0).astype(BF16) for part in (gq, gk, gv)]

    for which in range(3):
        held[g, which] = joined[which]
    part = None
    for which in range(3):
        part = add(part, mm_t(joined[which], deep(w_ref, which)))
    acc[...] = part + jnp.where(g == 0, 0.0, acc[...])
    outs = [keep_ref.at[0], keep_ref.at[1], send_ref.at[0], send_ref.at[1]]
    store_out(g, 0, held, sems, outs)

    @pl.when(g == T - 1)
    def _():
        total = None
        gains = None
        for c in range(C):
            rows = slice(c * m, (c + 1) * m)
            s = codes_ref[c].astype(F32) + sent_ref[...].astype(F32)
            back, gg = norm_back(s, gain_ref[0:1], acc[rows])
            gains = add(gains, gg)
            local = (ghid_ref[rows] + back).astype(BF16)
            glocal_ref[c] = local
            total = add(total, local.astype(F32))
        gsent_ref[...] = total.astype(BF16)
        gg_ref[...] = gains
        stored(held, sems, outs)


def codes_back(order, proj, W, codes, sent, ghid, gain):
    rows, D = ghid.shape
    C, m, _ = codes.shape
    T = W.shape[1]
    half = T // 2
    blocks = struct((half, 3, rows, BLK), BF16)
    return call(
        codes_back_body,
        order,
        (proj, W, codes, sent, ghid, gain),
        [
            pl.BlockSpec((1, 3, rows, BLK), lambda g, order: (g * order[ACTIVE], 0, 0, 0)),
            weight_spec(W, lambda g: (g, 0)),
            whole(codes.shape),
            whole(sent.shape),
            whole(ghid.shape),
            whole(gain.shape),
        ],
        (blocks, blocks, struct(codes.shape, BF16), struct((m, D), BF16), struct((1, D), F32)),
        (
            HBM_REF,
            HBM_REF,
            whole(codes.shape),
            whole((m, D)),
            whole((1, D)),
        ),
        T,
        (
            pltpu.VMEM((rows, D), F32),
            pltpu.VMEM((T, 3, rows, BLK), BF16),
            pltpu.VMEM((rows, D), BF16),
            pltpu.SemaphoreType.DMA((T,)),
        ),
        flops=2 * rows * D * 4 * D,
        moved=8 * D * D + rows * D * 20,
    )


def codes_out_body(order, hid_ref, a0_ref, a1_ref, a2_ref, a3_ref, wd_ref, out_ref, acc):
    g = pl.program_id(0)
    T = pl.num_programs(0)
    C, m, _ = out_ref.shape

    @pl.when(g == 0)
    def _():
        acc[...] = hid_ref[...]

    for i, act_ref in enumerate((a0_ref, a1_ref, a2_ref, a3_ref)):

        @pl.when(g == i)
        def _():
            act = jnp.concatenate([act_ref[j] for j in range(4)], axis=1)
            for z in range(wd_ref.shape[0]):
                acc[:, z * BLK : (z + 1) * BLK] += mm(act, wd_ref[z, 0].reshape(-1, BLK))

    @pl.when(g == T - 1)
    def _():
        for c in range(C):
            out_ref[c] = acc[c * m : (c + 1) * m].astype(BF16)


def codes_out(order, hid, acts, W, C):
    rows, D = hid.shape
    T = W.shape[1]
    m = rows // C
    return call(
        codes_out_body,
        order,
        (hid, *acts, W),
        [
            whole(hid.shape),
            *[pl.BlockSpec((4, rows, BLK), lambda g, order: (0, 0, 0))] * 4,
            weight_spec(W, lambda g: (g, 2)),
        ],
        struct((C, m, D), BF16),
        whole((C, m, D)),
        T,
        (pltpu.VMEM((rows, D), F32),),
        flops=2 * rows * D * 4 * D,
        moved=8 * D * D + rows * D * 14,
    )


def put(ref, value, by_rows):
    for z in range(ref.shape[0]):
        at = slice(z * BLK, (z + 1) * BLK)
        ref[z, 0] = (value[at] if by_rows else value[:, at]).astype(BF16)


def got(ref, by_rows):
    parts = [ref[z, 0].astype(F32) for z in range(ref.shape[0])]
    return jnp.concatenate(parts, axis=0 if by_rows else 1)


def grads_body(parts, has_got, flag, *refs):
    g = pl.program_id(0)
    slots = sum(part[0] and max(part[3], part[4]) for part in parts)
    out_ref = refs[len(refs) - 1 - slots]
    turned = refs[len(refs) - slots :]
    got_ref = refs[len(refs) - 2 - slots]
    at = 0
    for by_rows, begin, end, ones, zeros in parts:
        for value, count in ((1, ones), (0, zeros)):
            pairs = [(refs[at + 2 * i], refs[at + 2 * i + 1]) for i in range(count)]
            at += 2 * count
            if not count:
                continue

            def full(wide):
                if len(wide.shape) == 3:
                    return jnp.concatenate([wide[z] for z in range(wide.shape[0])], axis=1)
                return wide[...]

            if by_rows:

                @pl.when((flag[0] == value) & (g == begin))
                def _():
                    for (wide, _), turn in zip(pairs, turned):
                        turn[:, : wide.shape[-2]] = full(wide).T

            @pl.when((flag[0] == value) & (g >= begin) & (g < end))
            def _():
                total = None
                for i, (wide, narrow) in enumerate(pairs):
                    if by_rows:
                        piece = mm(turned[i][:, : wide.shape[-2]], narrow[0])
                    else:
                        piece = inner(narrow[0], full(wide))
                    total = piece if total is None else total + piece
                if has_got and value == 0:
                    total = total + got(got_ref, by_rows)
                put(out_ref, total, by_rows)


def grads(flag, nz, parts, received=None):
    inputs, specs, plan = [], [], []
    begin = 0
    for by_rows, count, ones, zeros in parts:
        for wide, narrow, base, *more in ones + zeros:
            if isinstance(wide, tuple):
                wide, at = wide
                rows = wide.shape[1]
                specs.append(
                    pl.BlockSpec((nz, rows, BLK), lambda g, f, a=at // nz: (a, 0, 0))
                )
            else:
                rows = wide.shape[0]
                specs.append(whole(wide.shape))
            specs.append(
                pl.BlockSpec(
                    (1, rows, BLK),
                    lambda g, f, s=begin, b=base, c=count, m=sum(more): (
                        b + clip(g - s, 0, c - 1),
                        m,
                        0,
                    ),
                )
            )
            inputs += [wide, narrow]
        plan.append((by_rows, begin, begin + count, len(ones), len(zeros)))
        begin += count
    turns = []
    for by_rows, _, ones, zeros in parts:
        if by_rows:
            rows = [[p[1].shape[1] for p in side] for side in (ones, zeros)]
            for i in range(max(len(side) for side in rows)):
                longest = max(side[i] for side in rows if len(side) > i)
                turns.append(pltpu.VMEM((nz * BLK, longest), BF16))
    block = pl.BlockSpec((nz, 1, BLK, BLK), lambda g, f: (0, g, 0, 0))
    if received is not None:
        inputs.append(received)
        specs.append(block)
    return call(
        functools.partial(grads_body, plan, received is not None),
        flag,
        inputs,
        specs,
        struct((nz, begin, BLK, BLK), BF16),
        block,
        begin,
        turns,
        flops=COST * (LONG if received is not None else 10**9),
    )


def swap(value, axis, bit):
    count = lax.axis_size(axis)
    return lax.ppermute(value, axis, [(i, i ^ bit) for i in range(count)])


def swap_in(value, section, bit):
    count = lax.axis_size("tensor")
    pairs = [(section * count + i, section * count + (i ^ bit)) for i in range(count)]
    return lax.ppermute(value, ("section", "tensor"), pairs)


def together(*values):
    return lax.optimization_barrier(values)


def mark_body(flag_ref, *refs):
    refs[-1][0] = flag_ref[0]


def mark(flag, *values):
    scalar = pl.BlockSpec(memory_space=pltpu.SMEM)
    return pl.pallas_call(
        mark_body,
        out_shape=struct((1,), jnp.int32),
        in_specs=[scalar] + [HBM_REF] * len(values),
        out_specs=scalar,
        cost_estimate=pl.CostEstimate(flops=10**9, bytes_accessed=0, transcendentals=0),
    )(flag, *values)


def after(value, *others):
    return together(value, *others)[0]


def pack_body(qkv_ref, out_ref, up_ref, down_ref, flat_ref):
    flat_ref[0:3] = qkv_ref[...]
    flat_ref[3] = out_ref[...]
    for j in range(4):
        flat_ref[4 + j] = up_ref[:, j * BLK : (j + 1) * BLK]
    flat_ref[8:12] = down_ref[...]


def widen_body(parts_ref, rows_ref, cols_ref):
    split = rows_ref.shape[0]
    rows_ref[...] = parts_ref[:split].astype(F32)
    cols_ref[...] = parts_ref[split:].astype(F32)


def widen(parts, split):
    rest = (parts.shape[0] - split,) + parts.shape[1:]
    return pl.pallas_call(
        widen_body,
        out_shape=(struct((split,) + parts.shape[1:], F32), struct(rest, F32)),
    )(parts)


def gather_weights(w_qkv, w_out, w_up, w_down):
    depth = w_qkv.shape[1]
    shards = lax.axis_size("dp")
    slices = lax.axis_size("tensor")
    both = ("dp", "tensor")
    if depth == BLK:
        flat = pl.pallas_call(
            pack_body,
            out_shape=struct((12, BLK, BLK), BF16),
        )(w_qkv, w_out, w_up, w_down.reshape(-1, BLK, BLK))
        out = lax.all_gather(flat, both)
        return out.reshape(shards, slices, *flat.shape)
    per = BLK // depth
    nz = shards // per

    def by_rows(value):
        out = lax.all_gather(value, both).reshape(nz, per, slices, value.shape[0], depth, BLK)
        return out.transpose(0, 2, 3, 1, 4, 5).reshape(nz, slices, -1, BLK, BLK)

    def by_cols(value):
        out = lax.all_gather(value, both)
        out = out.reshape(nz, per, slices, value.shape[0] // BLK, BLK, depth)
        return out.transpose(0, 2, 3, 4, 1, 5).reshape(nz, slices, -1, BLK, BLK)

    up_blocks = w_up.reshape(depth, -1, BLK).transpose(1, 0, 2)
    return jnp.concatenate(
        [by_rows(w_qkv), by_cols(w_out), by_rows(up_blocks), by_cols(w_down)], axis=2
    )


def scatter_blocks(parts, split):
    shards = lax.axis_size("dp")
    nz, count = parts.shape[:2]
    per = shards // nz
    if per == 1:
        out = lax.psum_scatter(parts, "dp", scatter_dimension=0, tiled=False)
        return widen(out, split) if 0 < split < count else (out[:split], out[split:])
    depth = BLK // per
    rows = parts[:, :split].reshape(nz, split, per, depth, BLK)
    rows = rows.transpose(0, 2, 1, 3, 4).reshape(shards, -1, BLK)
    columns = parts[:, split:].reshape(nz, count - split, BLK, per, depth)
    columns = columns.transpose(0, 3, 1, 2, 4).reshape(shards, -1, BLK)
    out = lax.psum_scatter(
        jnp.concatenate([rows, columns], axis=1), "dp", scatter_dimension=0, tiled=False
    )
    cut = split * depth
    return out[:cut].reshape(split, depth, BLK), out[cut:].reshape(-1, BLK, depth)


def on_device(codes, cotangent, doc_lengths, w_qkv, w_out, w_up, w_down, gains):
    is_first = lax.axis_index("section") == 0
    flag = is_first.astype(jnp.int32).reshape(1)
    t = lax.axis_index("tensor")
    T = lax.axis_size("tensor")
    R, F, C, D = codes.shape
    M = R * F
    N = T * F
    gain = gains[0]
    W = gather_weights(w_qkv[0], w_out[0], w_up[0], w_down[0])
    nz = W.shape[0]
    slices = t ^ jnp.array([0, 2, 1, 3], jnp.int32)
    order0 = jnp.concatenate([slices, flag])
    order1 = jnp.concatenate([slices, 1 - flag])
    codes_t = codes.transpose(2, 0, 1, 3).reshape(C, M, D)
    cot = cotangent.transpose(2, 0, 1, 3).reshape(C * M, D)

    frame_own = jnp.sum(codes_t.astype(F32), axis=0)
    far = swap(frame_own, "tensor", 2)
    s0 = jnp.concatenate(
        [frame_own, swap(frame_own, "tensor", 1), far, swap(far, "tensor", 1)], axis=0
    )
    spot = t ^ lax.iota(jnp.int32, T)
    pos = (spot[:, None] * F + lax.iota(jnp.int32, F)[None]).reshape(N)
    ends = jnp.cumsum(doc_lengths, axis=1)
    seg = jnp.sum((pos[None, :, None] >= ends[:, None, :]).astype(jnp.int32), axis=2)
    allowed = (pos[:, None] >= pos[None, :])[None] & (seg[:, :, None] == seg[:, None, :])
    bias = jnp.where(allowed, 0.0, NEG).astype(F32)

    n_in0 = normed(s0, gain[0:1])
    out0 = frames_own(order0, frame_own, n_in0, W, gain, bias, F)
    sent = lax.ppermute(out0, "section", [(0, 1)])
    s0 = after(s0, out0)
    proj0, mixed0, hid0, n_mid0, act0, slope0 = frames_fwd(order0, s0, n_in0, W, gain, bias, F)

    def swap1(value, bit):
        return swap_in(value, 1, bit)

    gact1 = codes_gact(order1, cot, W)
    cot_y = swap1(after(cot, out0), 2)
    cot_s = swap1(after(cot, out0), 1)
    sent, gact1, cot_y, cot_s, proj0 = together(sent, gact1, cot_y, cot_s, proj0)
    proj1, hid1, ghid1, gg_mid1, own1, act_far, act_other, bundle = codes_fwd(
        order1, codes_t, sent, cot, gact1, W, gain
    )
    act_y = swap1(act_far, 2)
    bundle_s, cot_d = swap1(bundle, 1), swap1(after(cot_y, bundle), 1)
    gproj1, gproj1_s, glocal, gsent, gg_in1 = codes_back(
        order1, proj1, W, codes_t, sent, ghid1, gain
    )

    gproj1, gproj1_s, glocal, gsent, gg_in1, bundle_s, cot_d = together(
        gproj1, gproj1_s, glocal, gsent, gg_in1, bundle_s, cot_d
    )

    gsent = lax.ppermute(gsent, "section", [(1, 0)])
    act_d = swap1(act_other, 3)

    M1 = C * M
    gproj1 = gproj1.reshape(-1, M1, BLK)
    up_far = grads(
        flag, nz, [(True, 4, [], [((bundle, 16), own1, 8), ((bundle_s, 16), bundle_s, 8)])]
    )
    up_got = swap1(up_far, 2)
    gsent, later = together(gsent, mark(flag, up_far, act_y, act_d))
    gfar = swap_in(gsent, 0, 2)
    gy0 = jnp.concatenate(
        [gsent, swap_in(gsent, 0, 1), gfar, swap_in(gfar, 0, 1)], axis=0
    )

    down_total = grads(
        later,
        nz,
        [
            (
                False,
                4,
                [(gy0, act0, 0)],
                [(cot, own1, 0), (cot_s, bundle_s, 0), (cot_y, act_y, 0), (cot_d, act_d, 0)],
            )
        ],
    )
    down_part = scatter_blocks(down_total, 0)[1]
    hid0 = after(hid0, down_total)
    gpre0, branch0, gproj0, frame, gg0 = frames_bwd(
        order0, gy0, hid0, slope0, W, gain, proj0, bias, frame_own, F
    )
    gproj1, gproj1_s = together(gproj1, gproj1_s, down_total)[:2]
    gproj1_s = swap1(gproj1_s, 1).reshape(-1, M1, BLK)
    att_far = grads(
        flag,
        nz,
        [
            (True, 3, [], [((bundle, 12), gproj1, 3), ((bundle_s, 12), gproj1_s, 3)]),
            (False, 1, [], [((bundle, 20), own1, 13), ((bundle_s, 20), bundle_s, 25)]),
        ],
    )
    att_got = swap1(att_far, 2)
    glocal = after(glocal, att_far)
    glocal = lax.ppermute(glocal, "section", [(1, 0)])
    up_total = grads(
        flag,
        nz,
        [
            (
                True,
                4,
                [(n_mid0, gpre0, 0)],
                [((bundle, 16), own1, 4), ((bundle_s, 16), bundle_s, 4)],
            )
        ],
        up_got,
    )
    up_part = scatter_blocks(up_total, 4)[0]
    hid1 = after(hid1, up_total)
    out1 = codes_out(order1, hid1, [own1, act_far, bundle, act_other], W, C)
    gproj0, out1 = together(gproj0, out1, up_total, glocal)[:2]
    att_total = grads(
        flag,
        nz,
        [
            (
                True,
                3,
                [(n_in0, gproj0, 0)],
                [((bundle, 12), gproj1, 0), ((bundle_s, 12), gproj1_s, 0)],
            ),
            (
                False,
                1,
                [(branch0, mixed0[None], 0)],
                [((bundle, 20), own1, 12), ((bundle_s, 20), bundle_s, 24)],
            ),
        ],
        att_got,
    )
    qkv_part, out_part = scatter_blocks(att_total, 3)
    gain_part = jnp.where(is_first, gg0, jnp.concatenate([gg_in1, gg_mid1], axis=0))
    grad_gains = lax.psum(after(gain_part, att_total), ("dp", "tensor"))

    code_grad = (glocal.astype(F32) + frame[None]).astype(BF16)
    result = jnp.where(is_first, code_grad, out1).reshape(C, R, F, D).transpose(1, 2, 0, 3)
    depth = w_up.shape[1]
    return (
        result[None],
        qkv_part.astype(F32)[None],
        out_part.reshape(-1, depth).astype(F32)[None],
        up_part.transpose(1, 0, 2).reshape(depth, -1).astype(F32)[None],
        down_part.reshape(-1, depth).astype(F32)[None],
        grad_gains[None],
    )


def solution(mesh):
    placed = (
        P("dp", "tensor", None, None),
        P("dp", "tensor", None, None),
        P("dp", None),
        P("section", None, "dp", "tensor"),
        P("section", "tensor", "dp"),
        P("section", "dp", "tensor"),
        P("section", "tensor", "dp"),
        P("section", None, None),
    )
    return jax.shard_map(
        on_device,
        mesh=mesh,
        in_specs=placed,
        out_specs=(
            P("section", "dp", "tensor", None, None),
            P("section", None, "dp", "tensor"),
            P("section", "tensor", "dp"),
            P("section", "dp", "tensor"),
            P("section", "tensor", "dp"),
            P("section", None, None),
        ),
        check_vma=False,
    )
```

```python
import functools

import jax
import jax.numpy as jnp
from jax import lax
from jax.experimental import pallas as pl
from jax.experimental.pallas import tpu as pltpu
from jax.sharding import PartitionSpec as P

HEAD_DIM = 64
BLK = 256
HEADS = BLK // HEAD_DIM
EPS = 1e-05
NEG = -1e30
SCALE = 0.125
F32 = jnp.float32
BF16 = jnp.bfloat16
VMEM = 60 * 1024 * 1024
ACTIVE = 4
COST = 8
LONG = 10**11


def mm(left, right):
    return jnp.dot(left, right, preferred_element_type=F32)


def mm_t(left, right):
    return lax.dot_general(left, right, (((1,), (1,)), ((), ())), preferred_element_type=F32)


def inner(left, right):
    return lax.dot_general(left, right, (((0,), (0,)), ((), ())), preferred_element_type=F32)


def unit_of(values):
    inv_root = lax.rsqrt(jnp.mean(values * values, axis=-1, keepdims=True) + EPS)
    return values * inv_root, inv_root


def normed(values, gain):
    return (unit_of(values)[0] * gain).astype(BF16)


def norm_back(values, gain, grad):
    unit_rows, inv_root = unit_of(values)
    scaled = grad * gain
    back = inv_root * (scaled - unit_rows * jnp.mean(unit_rows * scaled, axis=-1, keepdims=True))
    return back, jnp.sum(grad * unit_rows, axis=0, keepdims=True)


def gelu_pair(pre):
    square = pre * pre
    th = jnp.tanh(0.7978845608028654 * pre * (1.0 + 0.044715 * square))
    half = 0.5 + 0.5 * th
    act = pre * half
    slope = half + act * (1.0 - th) * (0.7978845608028654 + 3 * 0.044715 * 0.7978845608028654 * square)
    return act, slope


def head_masks(shape):
    lane = lax.broadcasted_iota(jnp.int32, shape, 1) // HEAD_DIM
    return [lane == h for h in range(HEADS)]


def spread(value, masks):
    zero = jnp.zeros_like(value)
    return jnp.concatenate([jnp.where(m, value, zero) for m in masks], axis=0)


def gathered(value, masks):
    n = value.shape[0] // HEADS
    out = jnp.where(masks[0], value[:n], 0.0)
    for h in range(1, HEADS):
        out = jnp.where(masks[h], value[h * n : (h + 1) * n], out)
    return out


def head_weights(q4, k, bias):
    s = mm_t(q4, k) * SCALE + jnp.concatenate([bias] * HEADS, axis=0)
    e = jnp.exp(s - jnp.max(s, axis=-1, keepdims=True))
    return e / jnp.sum(e, axis=-1, keepdims=True)


def whole(shape):
    return pl.BlockSpec(shape, lambda g, order: (0,) * len(shape))


def struct(shape, dtype):
    return jax.ShapeDtypeStruct(shape, dtype)


def call(body, order, inputs, in_specs, outs, out_specs, grid, scratch=(), flops=0, moved=0):
    def run(flags, *refs):
        if flags.shape[0] <= ACTIVE:
            return body(flags, *refs)

        @pl.when(flags[ACTIVE] == 1)
        def _():
            body(flags, *refs)

    return pl.pallas_call(
        run,
        out_shape=outs,
        grid_spec=pltpu.PrefetchScalarGridSpec(
            num_scalar_prefetch=1,
            grid=(grid,),
            in_specs=in_specs,
            out_specs=out_specs,
            scratch_shapes=scratch,
        ),
        compiler_params=pltpu.CompilerParams(
            dimension_semantics=("arbitrary",), vmem_limit_bytes=VMEM
        ),
        cost_estimate=pl.CostEstimate(
            flops=flops // COST, bytes_accessed=moved // COST, transcendentals=0
        ),
    )(order, *inputs)


def weight_spec(W, third):
    nz = W.shape[0]

    def at(g, order):
        step, which = third(g)
        return (0, order[step] * order[ACTIVE], which * order[ACTIVE], 0, 0)

    return pl.BlockSpec((nz, 1, 4, BLK, BLK), at)


def clip(g, low, high):
    return jnp.minimum(jnp.maximum(g, low), high)


def deep(ref, index):
    return ref[:, 0, index].reshape(-1, BLK)


def store_out(g, first, held, sems, outs):
    for i, out in enumerate(outs):

        @pl.when(g == first + i)
        def _():
            pltpu.make_async_copy(held.at[i], out, sems.at[i]).start()


def stored(held, sems, outs):
    for i, out in enumerate(outs):
        pltpu.make_async_copy(held.at[i], out, sems.at[i]).wait()


HBM_REF = pl.BlockSpec(memory_space=pl.ANY)


def pick(ref, r, R, F):
    return jnp.concatenate(
        [ref[pl.ds(at, F)] for at in range(r * F, ref.shape[0], R * F)], axis=0
    )


def place(ref, r, R, F, value):
    for i, at in enumerate(range(r * F, ref.shape[0], R * F)):
        ref[pl.ds(at, F)] = value[i * F : (i + 1) * F]


def frames_fwd_body(own, order, s_ref, nin_ref, wa_ref, gain_ref, bias_ref, proj_ref, mixed_ref, hid_ref, nmid_ref, act_ref, slope_ref, held, acts, sems):
    g = pl.program_id(0)
    T = pl.num_programs(0) // 2
    R, N = bias_ref.shape[:2]
    nz = wa_ref.shape[0]

    @pl.when(g == 0)
    def _():
        hid_ref[...] = s_ref[...]

    @pl.when(g < T)
    def _():
        for which in range(3):
            proj_ref[0, which] = mm(nin_ref[...], deep(wa_ref, which)).astype(BF16)
        masks = head_masks((N, BLK))
        for r in range(R):
            q, k, v = (pick(proj_ref.at[0, i], r, R, own) for i in range(3))
            p = head_weights(spread(q, masks), k, bias_ref[r])
            place(held, r, R, own, gathered(mm(p.astype(BF16), v), masks).astype(BF16))
        for z in range(nz):
            hid_ref[:, z * BLK : (z + 1) * BLK] += mm(held[...], wa_ref[z, 0, 3])

    @pl.when(g == 0)
    def _():
        mixed_ref[...] = held[...]

    @pl.when(g == T)
    def _():
        nmid_ref[...] = normed(hid_ref[...], gain_ref[1:2])

    @pl.when(g >= T)
    def _():
        for j in range(4):
            act, slope = gelu_pair(mm(nmid_ref[...], deep(wa_ref, j)))
            slope_ref[0, j] = slope.astype(BF16)
            acts[jnp.minimum(g - T, 1), j] = act.astype(BF16)

    store_out(g, T, acts, sems, [act_ref])

    @pl.when(g == 2 * T - 1)
    def _():
        stored(acts, sems, [act_ref])


def frames_fwd(order, s, nin, W, gain, bias, own):
    rows, D = s.shape
    T = W.shape[1]
    return call(
        functools.partial(frames_fwd_body, own),
        order,
        (s, nin, W, gain, bias),
        [
            whole(s.shape),
            whole(nin.shape),
            weight_spec(W, lambda g: (g % T, g // T)),
            whole(gain.shape),
            whole(bias.shape),
        ],
        (
            struct((T, 3, rows, BLK), BF16),
            struct((rows, BLK), BF16),
            struct((rows, D), F32),
            struct((rows, D), BF16),
            struct((4, rows, BLK), BF16),
            struct((T, 4, rows, BLK), BF16),
        ),
        (
            pl.BlockSpec((1, 3, rows, BLK), lambda g, order: (jnp.minimum(g, T - 1) * order[ACTIVE], 0, 0, 0)),
            whole((rows, BLK)),
            whole((rows, D)),
            whole((rows, D)),
            HBM_REF,
            pl.BlockSpec((1, 4, rows, BLK), lambda g, order: (jnp.maximum(g - T, 0) * order[ACTIVE], 0, 0, 0)),
        ),
        2 * T,
        (
            pltpu.VMEM((rows, BLK), BF16),
            pltpu.VMEM((2, 4, rows, BLK), BF16),
            pltpu.SemaphoreType.DMA((1,)),
        ),
        flops=2 * rows * D * 10 * D,
        moved=24 * D * D + rows * D * 30,
    )


def frames_own_body(own, order, s_ref, nin, wa_ref, wb_ref, gain_ref, bias_ref, out_ref, keys, values, held, hid, nmid):
    g = pl.program_id(0)
    T = pl.num_programs(0) // 2
    R, N = bias_ref.shape[:2]
    nz = wa_ref.shape[0]
    mine = R * own

    @pl.when(g == 0)
    def _():
        hid[...] = s_ref[...]

    @pl.when(g < T)
    def _():
        queries = mm(nin[:mine], deep(wa_ref, 0)).astype(BF16)
        keys[...] = mm(nin[...], deep(wa_ref, 1)).astype(BF16)
        values[...] = mm(nin[...], deep(wa_ref, 2)).astype(BF16)
        masks = head_masks((own, BLK))
        for r in range(R):
            q4 = spread(queries[r * own : (r + 1) * own], masks)
            p = head_weights(q4, pick(keys, r, R, own), bias_ref[r, :own])
            mixed = gathered(mm(p.astype(BF16), pick(values, r, R, own)), masks)
            held[r * own : (r + 1) * own] = mixed.astype(BF16)
        for z in range(nz):
            hid[:, z * BLK : (z + 1) * BLK] += mm(held[...], wa_ref[z, 0, 3])

    @pl.when(g == T)
    def _():
        nmid[...] = normed(hid[...], gain_ref[1:2])

    @pl.when(g >= T)
    def _():
        act = [gelu_pair(mm(nmid[...], deep(wa_ref, j)))[0].astype(BF16) for j in range(4)]
        act = jnp.concatenate(act, axis=1)
        for z in range(nz):
            hid[:, z * BLK : (z + 1) * BLK] += mm(act, wb_ref[z, 0].reshape(-1, BLK))

    @pl.when(g == 2 * T - 1)
    def _():
        out_ref[...] = hid[...].astype(BF16)


def frames_own(order, s, nin, W, gain, bias, own):
    rows, D = nin.shape
    T = W.shape[1]
    mine = bias.shape[0] * own
    return call(
        functools.partial(frames_own_body, own),
        order,
        (s, nin, W, W, gain, bias),
        [
            whole(s.shape),
            whole(nin.shape),
            weight_spec(W, lambda g: (g % T, g // T)),
            weight_spec(W, lambda g: (jnp.maximum(g - T, 0), 2)),
            whole(gain.shape),
            whole(bias.shape),
        ],
        struct((mine, D), BF16),
        whole((mine, D)),
        2 * T,
        (
            pltpu.VMEM((rows, BLK), BF16),
            pltpu.VMEM((rows, BLK), BF16),
            pltpu.VMEM((mine, BLK), BF16),
            pltpu.VMEM((mine, D), F32),
            pltpu.VMEM((mine, D), BF16),
        ),
        flops=2 * mine * D * 12 * D,
        moved=24 * D * D,
    )


def frames_bwd_body(own, order, gy_ref, hid_ref, slope_ref, wa_ref, wb_ref, gain_ref, proj_ref, bias_ref, s_ref, gpre_ref, branch_ref, gproj_ref, frame_ref, gg_ref, held, acc, acc_in, ghid, pres, gmix, sems, hid_at, s_at, bias_at):
    g = pl.program_id(0)
    late = [
        pltpu.make_async_copy(a, b, sems.at[1 + i])
        for i, (a, b) in enumerate([(hid_ref, hid_at), (s_ref, s_at), (bias_ref, bias_at)])
    ]
    T = pl.num_programs(0) // 2
    R, N = bias_ref.shape[:2]
    nz = wa_ref.shape[0]

    @pl.when(g == 0)
    def _():
        for copy in late:
            copy.start()

    @pl.when(g < T)
    def _():
        part = None
        for j in range(4):
            lanes = jnp.concatenate([wb_ref[z, 0, j] for z in range(nz)], axis=1)
            gpre = (mm_t(gy_ref[...], lanes) * slope_ref[0, j].astype(F32)).astype(BF16)

            pres[jnp.minimum(g, 1), j] = gpre
            piece = mm_t(gpre, deep(wa_ref, j))
            part = piece if part is None else part + piece
        acc[...] = part + jnp.where(g == 0, 0.0, acc[...])

    store_out(g, 0, pres, sems, [gpre_ref])

    @pl.when(g == T - 1)
    def _():
        for copy in late:
            copy.wait()
        back, _ = norm_back(hid_at[...], gain_ref[1:2], acc[...])
        branch_ref[...] = (gy_ref[...].astype(F32) + back).astype(BF16)
        back_own, gg = norm_back(hid_at[: R * own], gain_ref[1:2], acc[: R * own])
        gg_ref[1:2] = gg
        ghid[...] = gy_ref[: R * own].astype(F32) + back_own

    @pl.when(g >= T)
    def _():
        lanes = jnp.concatenate([wa_ref[z, 0, 3] for z in range(nz)], axis=1)
        gmix[...] = mm_t(branch_ref[...], lanes).astype(BF16)
        masks = head_masks((N, BLK))
        for r in range(R):
            q, k, v = (pick(proj_ref.at[0, i], r, R, own) for i in range(3))
            q4 = spread(q, masks)
            p = head_weights(q4, k, bias_at[r])
            gm4 = spread(pick(gmix, r, R, own), masks)
            ga = mm_t(gm4, v)
            gs = (SCALE * p * (ga - jnp.sum(p * ga, axis=-1, keepdims=True))).astype(BF16)
            place(held.at[0], r, R, own, gathered(mm(gs, k), masks).astype(BF16))
            place(held.at[1], r, R, own, inner(gs, q4).astype(BF16))
            place(held.at[2], r, R, own, inner(p.astype(BF16), gm4).astype(BF16))

        @pl.when(g == T)
        def _():
            gproj_ref[...] = held[...]

        part = None
        for which in range(3):
            piece = mm_t(held[which, : R * own], deep(wa_ref, which))
            part = piece if part is None else part + piece
        acc_in[...] = part + jnp.where(g == T, 0.0, acc_in[...])

    @pl.when(g == 2 * T - 1)
    def _():
        back, gg = norm_back(s_at[...], gain_ref[0:1], acc_in[...])
        gg_ref[0:1] = gg
        frame_ref[...] = ghid[...] + back
        stored(pres, sems, [gpre_ref])


def frames_bwd(order, gy, hid, slope, W, gain, proj, bias, s, own):
    rows, D = hid.shape
    T = W.shape[1]
    R = bias.shape[0]
    return call(
        functools.partial(frames_bwd_body, own),
        order,
        (gy, hid, slope, W, W, gain, proj, bias, s),
        [
            whole(gy.shape),
            HBM_REF,
            pl.BlockSpec((1, 4, rows, BLK), lambda g, order: (jnp.minimum(g, T - 1) * order[ACTIVE], 0, 0, 0)),
            weight_spec(W, lambda g: (g % T, 1 - g // T)),
            weight_spec(W, lambda g: (jnp.minimum(g, T - 1), 2)),
            whole(gain.shape),
            pl.BlockSpec((1, 3, rows, BLK), lambda g, order: (jnp.maximum(g - T, 0) * order[ACTIVE], 0, 0, 0)),
            HBM_REF,
            HBM_REF,
        ],
        (
            struct((4, rows, BLK), BF16),
            struct((rows, D), BF16),
            struct((3, rows, BLK), BF16),
            struct((R * own, D), F32),
            struct((2, D), F32),
        ),
        (
            HBM_REF,
            whole((rows, D)),
            whole((3, rows, BLK)),
            whole((R * own, D)),
            whole((2, D)),
        ),
        2 * T,
        (
            pltpu.VMEM((3, rows, BLK), BF16),
            pltpu.VMEM((rows, D), F32),
            pltpu.VMEM((R * own, D), F32),
            pltpu.VMEM((R * own, D), F32),
            pltpu.VMEM((2, 4, rows, BLK), BF16),
            pltpu.VMEM((rows, BLK), BF16),
            pltpu.SemaphoreType.DMA((4,)),
            pltpu.VMEM((rows, D), F32),
            pltpu.VMEM((R * own, D), F32),
            pltpu.VMEM(bias.shape, F32),
        ),
        flops=2 * rows * D * 14 * D,
        moved=24 * D * D + rows * D * 30,
    )


def head_sum(prods):
    row = lax.broadcasted_iota(jnp.int32, (BLK, BLK), 0) // HEAD_DIM
    col = lax.broadcasted_iota(jnp.int32, (BLK, BLK), 1) // HEAD_DIM
    ones = jnp.where(row == col, 1.0, 0.0).astype(BF16)
    high = prods.astype(BF16)
    low = (prods - high.astype(F32)).astype(BF16)
    return mm(high, ones) + mm(low, ones)


def token_pairs(count):
    return [(a, b) for a in range(1, count) for b in range(a + 1)]


def pair_sums(left, right, count):
    pairs = token_pairs(count)
    m = left[0].shape[0]
    sums = head_sum(jnp.concatenate([left[a] * right[b] for a, b in pairs], axis=0))
    return {pair: sums[i * m : (i + 1) * m] for i, pair in enumerate(pairs)}


def token_weights(q, k, count):
    s = pair_sums(q, k, count)
    out = {}
    for a in range(1, count):
        top = s[a, 0]
        for b in range(1, a + 1):
            top = jnp.maximum(top, s[a, b])
        e = [jnp.exp((s[a, b] - top) * SCALE) for b in range(a + 1)]
        total = e[0]
        for b in range(1, a + 1):
            total = total + e[b]
        share = 1.0 / total
        for b in range(a + 1):
            out[a, b] = e[b] * share
    return out


def rounded(value):
    return value.astype(BF16).astype(F32)


def split_tokens(value, count):
    m = value.shape[0] // count
    return [value[i * m : (i + 1) * m].astype(F32) for i in range(count)]


def codes_fwd_body(order, codes_ref, sent_ref, cot_ref, gact_ref, w_ref, gain_ref, proj_ref, hid_ref, ghid_ref, gg_ref, own_ref, far_ref, other_ref, bundle_ref, nin, nmid, branch, acc, acts, pres, mixes, sems):
    g = pl.program_id(0)
    T = pl.num_programs(0) // 2
    C, m, _ = codes_ref.shape
    nz = w_ref.shape[0]
    four = lambda ref, at: ref.at[pl.ds(at, 4)]
    to_a = [four(own_ref, 0), far_ref, four(bundle_ref, 0), other_ref]
    to_p = [four(own_ref, 4), four(own_ref, 8), four(bundle_ref, 4), four(bundle_ref, 8)]
    to_m = [own_ref.at[12], own_ref.at[13], bundle_ref.at[24], bundle_ref.at[25]]
    wides = [(nin, 12), (nmid, 16), (branch, 20)]

    def move(i):
        wide, at = wides[i]
        return pltpu.make_async_copy(wide, four(bundle_ref, at), sems.at[3, i])

    @pl.when(g == 0)
    def _():
        for c in range(C):
            s = codes_ref[c].astype(F32) + sent_ref[...].astype(F32)
            rows = pl.ds(c * m, m)
            hid_ref[rows] = s
            s = normed(s, gain_ref[0:1])
            for z in range(nz):
                nin[z, rows] = s[:, z * BLK : (z + 1) * BLK]
        move(0).start()

    @pl.when(g < T)
    def _():
        part = []
        wide = jnp.concatenate([nin[z] for z in range(nz)], axis=1)
        for which in range(3):
            block = mm(wide, deep(w_ref, which)).astype(BF16)
            proj_ref[0, which] = block
            part.append(split_tokens(block, C))
        q, k, v = part
        p = token_weights(q, k, C)
        mixed = [v[0]]
        for a in range(1, C):
            total = rounded(p[a, 0]) * v[0]
            for b in range(1, a + 1):
                total += rounded(p[a, b]) * v[b]
            mixed.append(total)
        mixed = jnp.concatenate(mixed, axis=0).astype(BF16)
        mixes[g] = mixed
        for z in range(nz):
            hid_ref[:, z * BLK : (z + 1) * BLK] += mm(mixed, w_ref[z, 0, 3])

    @pl.when(g == T)
    def _():
        s = normed(hid_ref[...], gain_ref[1:2])
        for z in range(nz):
            nmid[z] = s[:, z * BLK : (z + 1) * BLK]
        move(1).start()

    @pl.when(g >= T)
    def _():
        part = None
        wide = jnp.concatenate([nmid[z] for z in range(nz)], axis=1)
        for j in range(4):
            act, slope = gelu_pair(mm(wide, deep(w_ref, j)))
            gpre = (gact_ref[0, j].astype(F32) * slope).astype(BF16)
            acts[g - T, j] = act.astype(BF16)
            pres[g - T, j] = gpre
            piece = mm_t(gpre, deep(w_ref, j))
            part = piece if part is None else part + piece
        acc[...] = part + jnp.where(g == T, 0.0, acc[...])

    store_out(g, 0, mixes, sems.at[0], to_m)
    store_out(g, T, acts, sems.at[1], to_a)
    store_out(g, T, pres, sems.at[2], to_p)

    @pl.when(g == 2 * T - 1)
    def _():
        back, gg = norm_back(hid_ref[...], gain_ref[1:2], acc[...])
        gg_ref[...] = gg
        ghid = cot_ref[...].astype(F32) + back
        ghid_ref[...] = ghid
        for z in range(nz):
            branch[z] = ghid[:, z * BLK : (z + 1) * BLK].astype(BF16)
        move(2).start()
        stored(mixes, sems.at[0], to_m)
        stored(acts, sems.at[1], to_a)
        stored(pres, sems.at[2], to_p)
        for i in range(3):
            move(i).wait()


OWN_BLOCKS, BUNDLE = 14, 26


def kept(shape, first, half):
    return pl.BlockSpec(
        (1,) + shape, lambda g, order: (clip(g - first, 0, half - 1) * order[ACTIVE],) + (0,) * len(shape)
    )


def codes_fwd(order, codes, sent, cot, gact, W, gain):
    C, m, D = codes.shape
    rows = C * m
    nz, T = W.shape[:2]
    act = struct((4, rows, BLK), BF16)
    wide = pltpu.VMEM((nz, rows, BLK), BF16)
    return call(
        codes_fwd_body,
        order,
        (codes, sent, cot, gact, W, gain),
        [
            whole(codes.shape),
            whole(sent.shape),
            whole(cot.shape),
            kept((4, rows, BLK), T, T),
            weight_spec(W, lambda g: (g % T, g // T)),
            whole(gain.shape),
        ],
        (
            struct((T, 3, rows, BLK), BF16),
            struct((rows, D), F32),
            struct((rows, D), F32),
            struct((1, D), F32),
            struct((OWN_BLOCKS, rows, BLK), BF16),
            act,
            act,
            struct((BUNDLE, rows, BLK), BF16),
        ),
        (
            kept((3, rows, BLK), 0, T),
            whole((rows, D)),
            whole((rows, D)),
            whole((1, D)),
            *[HBM_REF] * 4,
        ),
        2 * T,
        (
            wide,
            wide,
            wide,
            pltpu.VMEM((rows, D), F32),
            pltpu.VMEM((T, 4, rows, BLK), BF16),
            pltpu.VMEM((T, 4, rows, BLK), BF16),
            pltpu.VMEM((T, rows, BLK), BF16),
            pltpu.SemaphoreType.DMA((4, T)),
        ),
        flops=2 * rows * D * 12 * D,
        moved=16 * D * D + rows * D * 40,
    )


def codes_gact_body(order, cot_ref, wd_ref, gact_ref):
    for j in range(4):
        lanes = jnp.concatenate([wd_ref[z, 0, j] for z in range(wd_ref.shape[0])], axis=1)
        gact_ref[0, j] = mm_t(cot_ref[...], lanes).astype(BF16)


def codes_gact(order, cot, W):
    rows, D = cot.shape
    T = W.shape[1]
    return call(
        codes_gact_body,
        order,
        (cot, W),
        [whole(cot.shape), weight_spec(W, lambda g: (g, 2))],
        struct((T, 4, rows, BLK), BF16),
        pl.BlockSpec((1, 4, rows, BLK), lambda g, order: (g * order[ACTIVE], 0, 0, 0)),
        T,
        flops=2 * rows * D * 4 * D,
        moved=8 * D * D + rows * D * 10,
    )


def codes_back_body(order, proj_ref, w_ref, codes_ref, sent_ref, ghid_ref, gain_ref, keep_ref, send_ref, glocal_ref, gsent_ref, gg_ref, acc, held, branch, sems):
    g = pl.program_id(0)
    C, m, _ = codes_ref.shape
    T = pl.num_programs(0)

    @pl.when(g == 0)
    def _():
        branch[...] = ghid_ref[...].astype(BF16)

    nz = w_ref.shape[0]
    lanes = jnp.concatenate([w_ref[z, 0, 3] for z in range(nz)], axis=1)
    gmix = mm_t(branch[...], lanes)
    gm = split_tokens(gmix.astype(BF16), C)
    q, k, v = (split_tokens(proj_ref[0, i], C) for i in range(3))
    p = token_weights(q, k, C)
    ga = pair_sums(gm, v, C)

    def add(left, right):
        return right if left is None else left + right

    gq, gk, gv = [jnp.zeros_like(q[0])], [None] * C, [gm[0]] + [None] * (C - 1)
    for a in range(1, C):
        centre = p[a, 0] * ga[a, 0]
        for b in range(1, a + 1):
            centre += p[a, b] * ga[a, b]
        total = None
        for b in range(a + 1):
            gs = rounded(SCALE * p[a, b] * (ga[a, b] - centre))
            total = add(total, gs * k[b])
            gk[b] = add(gk[b], gs * q[a])
            gv[b] = add(gv[b], rounded(p[a, b]) * gm[a])
        gq.append(total)
    joined = [jnp.concatenate(part, axis=0).astype(BF16) for part in (gq, gk, gv)]

    for which in range(3):
        held[g, which] = joined[which]
    part = None
    for which in range(3):
        part = add(part, mm_t(joined[which], deep(w_ref, which)))
    acc[...] = part + jnp.where(g == 0, 0.0, acc[...])
    outs = [keep_ref.at[0], keep_ref.at[1], send_ref.at[0], send_ref.at[1]]
    store_out(g, 0, held, sems, outs)

    @pl.when(g == T - 1)
    def _():
        total = None
        gains = None
        for c in range(C):
            rows = slice(c * m, (c + 1) * m)
            s = codes_ref[c].astype(F32) + sent_ref[...].astype(F32)
            back, gg = norm_back(s, gain_ref[0:1], acc[rows])
            gains = add(gains, gg)
            local = (ghid_ref[rows] + back).astype(BF16)
            glocal_ref[c] = local
            total = add(total, local.astype(F32))
        gsent_ref[...] = total.astype(BF16)
        gg_ref[...] = gains
        stored(held, sems, outs)


def codes_back(order, proj, W, codes, sent, ghid, gain):
    rows, D = ghid.shape
    C, m, _ = codes.shape
    T = W.shape[1]
    half = T // 2
    blocks = struct((half, 3, rows, BLK), BF16)
    return call(
        codes_back_body,
        order,
        (proj, W, codes, sent, ghid, gain),
        [
            pl.BlockSpec((1, 3, rows, BLK), lambda g, order: (g * order[ACTIVE], 0, 0, 0)),
            weight_spec(W, lambda g: (g, 0)),
            whole(codes.shape),
            whole(sent.shape),
            whole(ghid.shape),
            whole(gain.shape),
        ],
        (blocks, blocks, struct(codes.shape, BF16), struct((m, D), BF16), struct((1, D), F32)),
        (
            HBM_REF,
            HBM_REF,
            whole(codes.shape),
            whole((m, D)),
            whole((1, D)),
        ),
        T,
        (
            pltpu.VMEM((rows, D), F32),
            pltpu.VMEM((T, 3, rows, BLK), BF16),
            pltpu.VMEM((rows, D), BF16),
            pltpu.SemaphoreType.DMA((T,)),
        ),
        flops=2 * rows * D * 4 * D,
        moved=8 * D * D + rows * D * 20,
    )


def codes_out_body(order, hid_ref, a0_ref, a1_ref, a2_ref, a3_ref, wd_ref, out_ref, acc):
    g = pl.program_id(0)
    T = pl.num_programs(0)
    C, m, _ = out_ref.shape

    @pl.when(g == 0)
    def _():
        acc[...] = hid_ref[...]

    for i, act_ref in enumerate((a0_ref, a1_ref, a2_ref, a3_ref)):

        @pl.when(g == i)
        def _():
            act = jnp.concatenate([act_ref[j] for j in range(4)], axis=1)
            for z in range(wd_ref.shape[0]):
                acc[:, z * BLK : (z + 1) * BLK] += mm(act, wd_ref[z, 0].reshape(-1, BLK))

    @pl.when(g == T - 1)
    def _():
        for c in range(C):
            out_ref[c] = acc[c * m : (c + 1) * m].astype(BF16)


def codes_out(order, hid, acts, W, C):
    rows, D = hid.shape
    T = W.shape[1]
    m = rows // C
    return call(
        codes_out_body,
        order,
        (hid, *acts, W),
        [
            whole(hid.shape),
            *[pl.BlockSpec((4, rows, BLK), lambda g, order: (0, 0, 0))] * 4,
            weight_spec(W, lambda g: (g, 2)),
        ],
        struct((C, m, D), BF16),
        whole((C, m, D)),
        T,
        (pltpu.VMEM((rows, D), F32),),
        flops=2 * rows * D * 4 * D,
        moved=8 * D * D + rows * D * 14,
    )


def put(ref, value, by_rows):
    for z in range(ref.shape[0]):
        at = slice(z * BLK, (z + 1) * BLK)
        ref[z, 0] = (value[at] if by_rows else value[:, at]).astype(BF16)


def got(ref, by_rows):
    parts = [ref[z, 0].astype(F32) for z in range(ref.shape[0])]
    return jnp.concatenate(parts, axis=0 if by_rows else 1)


def grads_body(parts, has_got, flag, *refs):
    g = pl.program_id(0)
    slots = sum(part[0] and max(part[3], part[4]) for part in parts)
    out_ref = refs[len(refs) - 1 - slots]
    turned = refs[len(refs) - slots :]
    got_ref = refs[len(refs) - 2 - slots]
    at = 0
    for by_rows, begin, end, ones, zeros in parts:
        for value, count in ((1, ones), (0, zeros)):
            pairs = [(refs[at + 2 * i], refs[at + 2 * i + 1]) for i in range(count)]
            at += 2 * count
            if not count:
                continue

            def full(wide):
                if len(wide.shape) == 3:
                    return jnp.concatenate([wide[z] for z in range(wide.shape[0])], axis=1)
                return wide[...]

            if by_rows:

                @pl.when((flag[0] == value) & (g == begin))
                def _():
                    for (wide, _), turn in zip(pairs, turned):
                        turn[:, : wide.shape[-2]] = full(wide).T

            @pl.when((flag[0] == value) & (g >= begin) & (g < end))
            def _():
                total = None
                for i, (wide, narrow) in enumerate(pairs):
                    if by_rows:
                        piece = mm(turned[i][:, : wide.shape[-2]], narrow[0])
                    else:
                        piece = inner(narrow[0], full(wide))
                    total = piece if total is None else total + piece
                if has_got and value == 0:
                    total = total + got(got_ref, by_rows)
                put(out_ref, total, by_rows)


def grads(flag, nz, parts, received=None):
    inputs, specs, plan = [], [], []
    begin = 0
    for by_rows, count, ones, zeros in parts:
        for wide, narrow, base, *more in ones + zeros:
            if isinstance(wide, tuple):
                wide, at = wide
                rows = wide.shape[1]
                specs.append(
                    pl.BlockSpec((nz, rows, BLK), lambda g, f, a=at // nz: (a, 0, 0))
                )
            else:
                rows = wide.shape[0]
                specs.append(whole(wide.shape))
            specs.append(
                pl.BlockSpec(
                    (1, rows, BLK),
                    lambda g, f, s=begin, b=base, c=count, m=sum(more): (
                        b + clip(g - s, 0, c - 1),
                        m,
                        0,
                    ),
                )
            )
            inputs += [wide, narrow]
        plan.append((by_rows, begin, begin + count, len(ones), len(zeros)))
        begin += count
    turns = []
    for by_rows, _, ones, zeros in parts:
        if by_rows:
            rows = [[p[1].shape[1] for p in side] for side in (ones, zeros)]
            for i in range(max(len(side) for side in rows)):
                longest = max(side[i] for side in rows if len(side) > i)
                turns.append(pltpu.VMEM((nz * BLK, longest), BF16))
    block = pl.BlockSpec((nz, 1, BLK, BLK), lambda g, f: (0, g, 0, 0))
    if received is not None:
        inputs.append(received)
        specs.append(block)
    return call(
        functools.partial(grads_body, plan, received is not None),
        flag,
        inputs,
        specs,
        struct((nz, begin, BLK, BLK), BF16),
        block,
        begin,
        turns,
        flops=COST * (LONG if received is not None else 10**9),
    )


def swap(value, axis, bit):
    count = lax.axis_size(axis)
    return lax.ppermute(value, axis, [(i, i ^ bit) for i in range(count)])


def swap_in(value, section, bit):
    count = lax.axis_size("tensor")
    pairs = [(section * count + i, section * count + (i ^ bit)) for i in range(count)]
    return lax.ppermute(value, ("section", "tensor"), pairs)


def together(*values):
    return lax.optimization_barrier(values)


def mark_body(flag_ref, *refs):
    refs[-1][0] = flag_ref[0]


def mark(flag, *values):
    scalar = pl.BlockSpec(memory_space=pltpu.SMEM)
    return pl.pallas_call(
        mark_body,
        out_shape=struct((1,), jnp.int32),
        in_specs=[scalar] + [HBM_REF] * len(values),
        out_specs=scalar,
        cost_estimate=pl.CostEstimate(flops=10**9, bytes_accessed=0, transcendentals=0),
    )(flag, *values)


def after(value, *others):
    return together(value, *others)[0]


def pack_body(qkv_ref, out_ref, up_ref, down_ref, flat_ref):
    flat_ref[0:3] = qkv_ref[...]
    flat_ref[3] = out_ref[...]
    for j in range(4):
        flat_ref[4 + j] = up_ref[:, j * BLK : (j + 1) * BLK]
    flat_ref[8:12] = down_ref[...]


def widen_body(parts_ref, rows_ref, cols_ref):
    split = rows_ref.shape[0]
    rows_ref[...] = parts_ref[:split].astype(F32)
    cols_ref[...] = parts_ref[split:].astype(F32)


def widen(parts, split):
    rest = (parts.shape[0] - split,) + parts.shape[1:]
    return pl.pallas_call(
        widen_body,
        out_shape=(struct((split,) + parts.shape[1:], F32), struct(rest, F32)),
    )(parts)


def gather_weights(w_qkv, w_out, w_up, w_down):
    depth = w_qkv.shape[1]
    shards = lax.axis_size("dp")
    slices = lax.axis_size("tensor")
    both = ("dp", "tensor")
    if depth == BLK:
        flat = pl.pallas_call(
            pack_body,
            out_shape=struct((12, BLK, BLK), BF16),
        )(w_qkv, w_out, w_up, w_down.reshape(-1, BLK, BLK))
        out = lax.all_gather(flat, both)
        return out.reshape(shards, slices, *flat.shape)
    per = BLK // depth
    nz = shards // per

    def by_rows(value):
        out = lax.all_gather(value, both).reshape(nz, per, slices, value.shape[0], depth, BLK)
        return out.transpose(0, 2, 3, 1, 4, 5).reshape(nz, slices, -1, BLK, BLK)

    def by_cols(value):
        out = lax.all_gather(value, both)
        out = out.reshape(nz, per, slices, value.shape[0] // BLK, BLK, depth)
        return out.transpose(0, 2, 3, 4, 1, 5).reshape(nz, slices, -1, BLK, BLK)

    up_blocks = w_up.reshape(depth, -1, BLK).transpose(1, 0, 2)
    return jnp.concatenate(
        [by_rows(w_qkv), by_cols(w_out), by_rows(up_blocks), by_cols(w_down)], axis=2
    )


def scatter_blocks(parts, split):
    shards = lax.axis_size("dp")
    nz, count = parts.shape[:2]
    per = shards // nz
    if per == 1:
        out = lax.psum_scatter(parts, "dp", scatter_dimension=0, tiled=False)
        return widen(out, split) if 0 < split < count else (out[:split], out[split:])
    depth = BLK // per
    rows = parts[:, :split].reshape(nz, split, per, depth, BLK)
    rows = rows.transpose(0, 2, 1, 3, 4).reshape(shards, -1, BLK)
    columns = parts[:, split:].reshape(nz, count - split, BLK, per, depth)
    columns = columns.transpose(0, 3, 1, 2, 4).reshape(shards, -1, BLK)
    out = lax.psum_scatter(
        jnp.concatenate([rows, columns], axis=1), "dp", scatter_dimension=0, tiled=False
    )
    cut = split * depth
    return out[:cut].reshape(split, depth, BLK), out[cut:].reshape(-1, BLK, depth)


def on_device(codes, cotangent, doc_lengths, w_qkv, w_out, w_up, w_down, gains):
    is_first = lax.axis_index("section") == 0
    flag = is_first.astype(jnp.int32).reshape(1)
    t = lax.axis_index("tensor")
    T = lax.axis_size("tensor")
    R, F, C, D = codes.shape
    M = R * F
    N = T * F
    gain = gains[0]
    W = gather_weights(w_qkv[0], w_out[0], w_up[0], w_down[0])
    nz = W.shape[0]
    slices = t ^ jnp.array([0, 2, 1, 3], jnp.int32)
    order0 = jnp.concatenate([slices, flag])
    order1 = jnp.concatenate([slices, 1 - flag])
    codes_t = codes.transpose(2, 0, 1, 3).reshape(C, M, D)
    cot = cotangent.transpose(2, 0, 1, 3).reshape(C * M, D)

    frame_own = jnp.sum(codes_t.astype(F32), axis=0)
    near = frame_own.astype(BF16)
    far = swap(near, "tensor", 2)
    others = [swap(near, "tensor", 1), far, swap(far, "tensor", 1)]
    s0 = jnp.concatenate([frame_own, *[part.astype(F32) for part in others]], axis=0)
    spot = t ^ lax.iota(jnp.int32, T)
    pos = (spot[:, None] * F + lax.iota(jnp.int32, F)[None]).reshape(N)
    ends = jnp.cumsum(doc_lengths, axis=1)
    seg = jnp.sum((pos[None, :, None] >= ends[:, None, :]).astype(jnp.int32), axis=2)
    allowed = (pos[:, None] >= pos[None, :])[None] & (seg[:, :, None] == seg[:, None, :])
    bias = jnp.where(allowed, 0.0, NEG).astype(F32)

    n_in0 = normed(s0, gain[0:1])
    out0 = frames_own(order0, frame_own, n_in0, W, gain, bias, F)
    sent = lax.ppermute(out0, "section", [(0, 1)])
    s0 = after(s0, out0)
    proj0, mixed0, hid0, n_mid0, act0, slope0 = frames_fwd(order0, s0, n_in0, W, gain, bias, F)

    def swap1(value, bit):
        return swap_in(value, 1, bit)

    gact1 = codes_gact(order1, cot, W)
    cot_y = swap1(after(cot, out0), 2)
    cot_s = swap1(after(cot, out0), 1)
    sent, gact1, cot_y, cot_s, proj0 = together(sent, gact1, cot_y, cot_s, proj0)
    proj1, hid1, ghid1, gg_mid1, own1, act_far, act_other, bundle = codes_fwd(
        order1, codes_t, sent, cot, gact1, W, gain
    )
    act_y = swap1(act_far, 2)
    bundle_s, cot_d = swap1(bundle, 1), swap1(after(cot_y, bundle), 1)
    gproj1, gproj1_s, glocal, gsent, gg_in1 = codes_back(
        order1, proj1, W, codes_t, sent, ghid1, gain
    )

    gproj1, gproj1_s, glocal, gsent, gg_in1, bundle_s = together(
        gproj1, gproj1_s, glocal, gsent, gg_in1, bundle_s
    )

    gsent = lax.ppermute(gsent, "section", [(1, 0)])
    act_d = swap1(act_other, 3)

    M1 = C * M
    gproj1 = gproj1.reshape(-1, M1, BLK)
    up_far = grads(
        flag, nz, [(True, 4, [], [((bundle, 16), own1, 8), ((bundle_s, 16), bundle_s, 8)])]
    )
    up_got = swap1(up_far, 2)
    gsent, later = together(gsent, mark(flag, up_far, act_y, act_d))
    gfar = swap_in(gsent, 0, 2)
    gy0 = jnp.concatenate(
        [gsent, swap_in(gsent, 0, 1), gfar, swap_in(gfar, 0, 1)], axis=0
    )

    down_total = grads(
        later,
        nz,
        [
            (
                False,
                4,
                [(gy0, act0, 0)],
                [(cot, own1, 0), (cot_s, bundle_s, 0), (cot_y, act_y, 0), (cot_d, act_d, 0)],
            )
        ],
    )
    down_part = scatter_blocks(down_total, 0)[1]
    hid0 = after(hid0, down_total)
    gpre0, branch0, gproj0, frame, gg0 = frames_bwd(
        order0, gy0, hid0, slope0, W, gain, proj0, bias, frame_own, F
    )
    gproj1, gproj1_s = together(gproj1, gproj1_s, down_total)[:2]
    gproj1_s = swap1(gproj1_s, 1).reshape(-1, M1, BLK)
    att_far = grads(
        flag,
        nz,
        [
            (True, 3, [], [((bundle, 12), gproj1, 3), ((bundle_s, 12), gproj1_s, 3)]),
            (False, 1, [], [((bundle, 20), own1, 13), ((bundle_s, 20), bundle_s, 25)]),
        ],
    )
    att_got = swap1(att_far, 2)
    glocal = after(glocal, att_far)
    glocal = lax.ppermute(glocal, "section", [(1, 0)])
    up_total = grads(
        flag,
        nz,
        [
            (
                True,
                4,
                [(n_mid0, gpre0, 0)],
                [((bundle, 16), own1, 4), ((bundle_s, 16), bundle_s, 4)],
            )
        ],
        up_got,
    )
    up_part = scatter_blocks(up_total, 4)[0]
    hid1 = after(hid1, up_total)
    out1 = codes_out(order1, hid1, [own1, act_far, bundle, act_other], W, C)
    gproj0, out1 = together(gproj0, out1, up_total, glocal)[:2]
    att_total = grads(
        flag,
        nz,
        [
            (
                True,
                3,
                [(n_in0, gproj0, 0)],
                [((bundle, 12), gproj1, 0), ((bundle_s, 12), gproj1_s, 0)],
            ),
            (
                False,
                1,
                [(branch0, mixed0[None], 0)],
                [((bundle, 20), own1, 12), ((bundle_s, 20), bundle_s, 24)],
            ),
        ],
        att_got,
    )
    qkv_part, out_part = scatter_blocks(att_total, 3)
    gain_part = jnp.where(is_first, gg0, jnp.concatenate([gg_in1, gg_mid1], axis=0))
    grad_gains = lax.psum(after(gain_part, att_total), ("dp", "tensor"))

    code_grad = (glocal.astype(F32) + frame[None]).astype(BF16)
    result = jnp.where(is_first, code_grad, out1).reshape(C, R, F, D).transpose(1, 2, 0, 3)
    depth = w_up.shape[1]
    return (
        result[None],
        qkv_part.astype(F32)[None],
        out_part.reshape(-1, depth).astype(F32)[None],
        up_part.transpose(1, 0, 2).reshape(depth, -1).astype(F32)[None],
        down_part.reshape(-1, depth).astype(F32)[None],
        grad_gains[None],
    )


def solution(mesh):
    placed = (
        P("dp", "tensor", None, None),
        P("dp", "tensor", None, None),
        P("dp", None),
        P("section", None, "dp", "tensor"),
        P("section", "tensor", "dp"),
        P("section", "dp", "tensor"),
        P("section", "tensor", "dp"),
        P("section", None, None),
    )
    return jax.shard_map(
        on_device,
        mesh=mesh,
        in_specs=placed,
        out_specs=(
            P("section", "dp", "tensor", None, None),
            P("section", None, "dp", "tensor"),
            P("section", "tensor", "dp"),
            P("section", "dp", "tensor"),
            P("section", "tensor", "dp"),
            P("section", None, None),
        ),
        check_vma=False,
    )
```
